512 devices in a mesh: band: 8 (over x, core), dom: 64 (over y, z).
Axes of the slice: x: 4, y: 4, z: 16, core: 2. Of those that a mesh axis runs over, the one named last changes fastest.
Arguments:
- orbitals: float32 [64, 512, 16, 64], P('band', 'dom'), may hold values from -6 to 6
- spin_group: int32 [64], P('band'), may hold values from 0 to 1
- occupation: int32 [64], P('band'), may hold values from 1 to 16
- potential_guess: float32 [1024, 32, 128], P('dom'), may hold values from -6 to 6
Outputs:
- potential: float32 [1024, 32, 128], P('dom')
- magnetization: float32 [1024, 32, 128], P('dom')
The draws below stay inside these ranges and needn't reach their ends.
All inputs are finite; a program needn't handle non-finite values.
Results may differ from the reference program's by a relative error of at most 0.00016.
Values sent between devices are 32-bit elements; how exact they have to be, the bound alone decides.
No kernel may reach another device: no remote copies, remote signals or barrier semaphores. Data moves between devices by JAX's collectives and lax.ppermute only.
A program may use at most 64 MiB of HBM per device.

```python
import jax
import jax.numpy as jnp
from jax import lax

CY = 16
CZ = 64
SPINS = 2
DEN = 16
LEVELS = 5
NU = 2
COARSE_SWEEPS = 4
ORBITALS = 64
COARSE_X = 512
NX = 1024
NY = 32
NZ = 128


def place_ends(result, key, least, high):
    longest = result.shape.index(max(result.shape))
    spots = []
    for shift in (0, 1):
        where = [jax.random.randint(jax.random.fold_in(key, axis), (), 0, length) for axis, length in enumerate(result.shape)]
        where[longest] = (where[longest] + shift) % result.shape[longest]
        spots.append(tuple(where))
    return result.at[spots[0]].set(least).at[spots[1]].set(high)


def steps_of(rng, extent, cuts, smallest, high):
    gain = 1.0
    for axis_at, parts in cuts:
        draws = jax.random.uniform(jax.random.fold_in(jax.random.fold_in(rng, 6), axis_at), (parts,), jnp.float32, smallest / len(cuts), high / len(cuts))
        gain = gain * jnp.repeat(jnp.exp(draws), extent[axis_at] // parts).reshape((-1,) + (1,) * (len(extent) - 1 - axis_at))
    return gain


def scatter_about(own_key, dims, scale, reach, cuts=(), kind=jnp.bfloat16):
    gain = steps_of(own_key, dims, cuts, -0.22, 0.18) if cuts else 1.0
    drawn = jax.random.normal(own_key, dims, jnp.float32) * scale * gain
    return jnp.minimum(jnp.maximum(drawn, -reach), reach).astype(kind)


def setup_inputs(seed: int = 0) -> dict:
    keys = jax.random.split(jax.random.key(seed), 5)
    orbitals = scatter_about(keys[0], (ORBITALS, COARSE_X, CY, CZ), 1.0, 6.0, ((0, 8), (1, 64)), jnp.float32)
    spin_group = place_ends(jax.random.randint(keys[1], (ORBITALS,), 0, SPINS), jax.random.fold_in(keys[1], 1), 0, SPINS - 1).astype(jnp.int32)
    occupation = place_ends(jax.random.randint(keys[2], (ORBITALS,), 1, DEN + 1), jax.random.fold_in(keys[2], 1), 1, DEN).astype(jnp.int32)
    potential_guess = scatter_about(keys[3], (NX, NY, NZ), 1.0, 6.0, ((0, 64),), jnp.float32)
    return {"orbitals": orbitals, "spin_group": spin_group, "occupation": occupation, "potential_guess": potential_guess}


OMEGA = 2.0 / 3.0
SOURCE_SCALE = 0.6


def refine_from(coarse, padded, axis):
    count = coarse.shape[axis]
    lower = lax.slice_in_dim(padded, 0, count, axis=axis)
    upper = lax.slice_in_dim(padded, 2, count + 2, axis=axis)
    first = 0.75 * coarse + 0.25 * lower
    second = 0.75 * coarse + 0.25 * upper
    both = jnp.stack([first, second], axis=axis + 1)
    shape = list(coarse.shape)
    shape[axis] = 2 * count
    return both.reshape(shape)


def refine_local(coarse, axis):
    widths = [(0, 0)] * coarse.ndim
    widths[axis] = (1, 1)
    return refine_from(coarse, jnp.pad(coarse, widths), axis)


def neighbour_sum(field, xpad):
    total = xpad[2:] + xpad[:-2]
    ypad = jnp.pad(field, ((0, 0), (1, 1), (0, 0)))
    total = total + ypad[:, 2:] + ypad[:, :-2]
    zpad = jnp.pad(field, ((0, 0), (0, 0), (1, 1)))
    return total + zpad[:, :, 2:] + zpad[:, :, :-2]


def local_pad(field):
    return jnp.pad(field, ((1, 1), (0, 0), (0, 0)))


def operate(field):
    return 6.0 * field - neighbour_sum(field, local_pad(field))


def sweep(field, right):
    return field + OMEGA * (right - operate(field)) / 6.0


def restrict(field):
    a, b, c = field.shape
    return 0.5 * field.reshape(a // 2, 2, b // 2, 2, c // 2, 2).sum(axis=(1, 3, 5))


def prolong(field):
    field = jnp.repeat(field, 2, axis=0)
    field = jnp.repeat(field, 2, axis=1)
    return jnp.repeat(field, 2, axis=2)


def vcycle(right, level):
    correction = OMEGA * right / 6.0
    if level == LEVELS - 1:
        for turn in range(COARSE_SWEEPS - 1):
            correction = sweep(correction, right)
        return correction
    for turn in range(NU - 1):
        correction = sweep(correction, right)
    leftover = right - operate(correction)
    correction = correction + prolong(vcycle(restrict(leftover), level + 1))
    for turn in range(NU):
        correction = sweep(correction, right)
    return correction


def reference(orbitals, spin_group, occupation, potential_guess):
    channels = jnp.arange(SPINS, dtype=jnp.int32)[:, None]
    weights = (spin_group[None, :] == channels).astype(jnp.float32) * (occupation[None, :].astype(jnp.float32) * (0.125 / DEN))
    squares = (orbitals * orbitals).reshape(orbitals.shape[0], -1)
    coarse = jnp.dot(weights, squares, precision=lax.Precision.HIGHEST, preferred_element_type=jnp.float32)
    coarse = coarse.reshape((SPINS,) + orbitals.shape[1:])
    fine = refine_local(coarse, 1)
    fine = refine_local(fine, 2)
    fine = refine_local(fine, 3)
    magnetization = fine[0] - fine[1]
    source = SOURCE_SCALE * (fine[0] + fine[1])
    defect = source - operate(potential_guess)
    potential = potential_guess + vcycle(defect, 0)
    return potential, magnetization
```

```python
import functools

import jax
import jax.numpy as jnp
from jax import lax
from jax.experimental import pallas as pl
from jax.experimental.pallas import tpu as pltpu
from jax.sharding import PartitionSpec as P

DEN = 16
BANDS = 8
DOMS = 64
REACH = 7
ALPHA = 1.0 / 9.0
SOURCE_SCALE = 0.6
F32 = jnp.float32


def lanes_of(shape):
    return lax.broadcasted_iota(jnp.int32, shape, len(shape) - 1)


def rows_of(shape):
    return lax.broadcasted_iota(jnp.int32, shape, len(shape) - 2)


def sides_z(v, step):
    lane = lanes_of(v.shape)
    ax = v.ndim - 1
    left = jnp.where(lane >= step, pltpu.roll(v, step, ax), 0.0)
    right = jnp.where(lane < 128 - step, pltpu.roll(v, 128 - step, ax), 0.0)
    return left + right


def from_below(v, step=1):
    return jnp.where(rows_of(v.shape) >= step, pltpu.roll(v, step, v.ndim - 2), 0.0)


def from_above(v, step=1):
    return jnp.where(rows_of(v.shape) < 8 - step, pltpu.roll(v, 8 - step, v.ndim - 2), 0.0)


def sides_y(v, step):
    if v.ndim == 2:
        return from_below(v, step) + from_above(v, step)
    parts = [v[q] for q in range(v.shape[0])]
    n = len(parts)
    out = []
    for q in range(n):
        lower = parts[q - 1] if q > 0 else from_below(parts[n - 1])
        upper = parts[q + 1] if q < n - 1 else from_above(parts[0])
        out.append(lower + upper)
    return jnp.stack(out, axis=0)


def smooth(low, v, high, zstep, ystep=1):
    around = sides_y(v, ystep) + sides_z(v, zstep)
    if low is not None:
        around = around + low
    if high is not None:
        around = around + high
    return v * (1.0 / 3.0) + around * ALPHA


def pair_z(v, step):
    lane = lanes_of(v.shape)
    ax = v.ndim - 1
    other = jnp.where((lane & step) == 0, pltpu.roll(v, 128 - step, ax), pltpu.roll(v, step, ax))
    return v + other


def pair_y(v, step):
    row = rows_of(v.shape)
    ax = v.ndim - 2
    other = jnp.where((row & step) == 0, pltpu.roll(v, 8 - step, ax), pltpu.roll(v, step, ax))
    return v + other


def run_T(src, planes, zstep, ystep=1, mask=None):
    out = {}
    for k in planes:
        v = src.get(k)
        low, high = src.get(k - 1), src.get(k + 1)
        if v is None:
            edge = low if low is not None else high
            got = edge * ALPHA
        else:
            got = smooth(low, v, high, zstep, ystep)
        out[k] = got if mask is None else mask(k, got)
    return out


class Held:
    def __init__(self, ref, first):
        self.ref, self.first, self.have = ref, first, set()

    def put(self, k, value):
        self.ref[k - self.first] = value
        self.have.add(k)

    def get(self, k):
        return self.ref[k - self.first] if k in self.have else None

    def __getitem__(self, k):
        return self.ref[k - self.first]


def hold_T(src, held, planes, zstep, mask):
    for k in planes:
        v = src.get(k)
        low, high = src.get(k - 1), src.get(k + 1)
        if v is None:
            got = (low if low is not None else high) * ALPHA
        else:
            got = smooth(low, v, high, zstep)
        held.put(k, mask(k, got))


def density_kernel(spin_ref, occ_ref, orb_ref, out_ref):
    weights = []
    for k in range(8):
        weight = occ_ref[k].astype(F32) * (0.125 / DEN)
        up = spin_ref[k] == 0
        weights.append((jnp.where(up, weight, 0.0), jnp.where(up, 0.0, weight)))
    for x in range(8):
        up, down = 0.0, 0.0
        for k in range(8):
            square = orb_ref[k, x] * orb_ref[k, x]
            up = up + weights[k][0] * square
            down = down + weights[k][1] * square
        both = jnp.concatenate([up, down], axis=-1)
        for copy in range(BANDS):
            out_ref[copy, pl.ds(16 * x, 16), :] = both


def density(spin_group, occupation, orbitals):
    smem = pl.BlockSpec(memory_space=pltpu.SMEM)
    vmem = pl.BlockSpec(memory_space=pltpu.VMEM)
    return pl.pallas_call(
        density_kernel,
        out_shape=jax.ShapeDtypeStruct((BANDS, 128, 128), F32),
        in_specs=[smem, smem, vmem],
        out_specs=vmem,
        compiler_params=pltpu.CompilerParams(vmem_limit_bytes=32 * 2**20),
        name="density",
    )(spin_group, occupation, orbitals)


def refine_matrix():
    row = lax.broadcasted_iota(jnp.int32, (128, 256), 0)
    col = lax.broadcasted_iota(jnp.int32, (128, 256), 1)
    cell, spin = row & 63, row >> 6
    fine, half = col & 127, col >> 7
    own = fine >> 1
    other = jnp.where((fine & 1) == 0, own - 1, own + 1)
    value = jnp.where(cell == own, 0.75, jnp.where(cell == other, 0.25, 0.0))
    return jnp.where((spin == 1) & (half == 1), -value, value)


def refine_y(pair):
    first, second = pair
    return jnp.stack(
        [
            0.75 * first + 0.25 * from_below(second),
            0.75 * first + 0.25 * second,
            0.75 * second + 0.25 * first,
            0.75 * second + 0.25 * from_above(first),
        ],
        axis=0,
    )


def refine_x(coarse, k):
    i = k // 2
    other = i - 1 if k % 2 == 0 else i + 1
    total = None
    for j, factor in ((i, 0.75), (other, 0.25)):
        if 0 <= j < 8:
            term = factor * coarse[j]
            total = term if total is None else total + term
    return total


def local_kernel(
    flag_ref, part_ref, guess_ref,
    far_ref, low_ref, high_ref, own0_ref, own1_ref, mag_ref,
    sum_ref, wide_ref, d_ref, t_ref, r_ref, t1_ref,
):
    low_flag, high_flag = flag_ref[0], flag_ref[1]

    def masked(last):
        def mask(k, v):
            if k < 0:
                return v * low_flag
            if k > last:
                return v * high_flag
            return v
        return mask

    inside0, inside1 = masked(15), masked(7)

    for x in range(8):
        rows = pl.ds(16 * x, 16)
        total = part_ref[0, rows, :]
        for band in range(1, BANDS):
            total = total + part_ref[band, rows, :]
        sum_ref[rows, :] = total
    wide = jnp.dot(
        sum_ref[...], refine_matrix(),
        precision=lax.Precision.HIGHEST, preferred_element_type=F32,
    )
    wide_ref[0], wide_ref[1] = wide[:, :128], wide[:, 128:]
    plus, minus = [], []
    for x in range(8):
        pairs = [[wide_ref[half, pl.ds(16 * x + p, 8, stride=2), :] for p in range(2)] for half in range(2)]
        plus.append(SOURCE_SCALE * refine_y(pairs[0]))
        minus.append(refine_y(pairs[1]))

    def guess(k):
        if not 0 <= k < 16:
            return None
        return jnp.stack([guess_ref[k, pl.ds(q, 8, stride=4), :] for q in range(4)], axis=0)

    d = Held(d_ref, -1)
    for k in range(-1, 17):
        v, low, high = guess(k), guess(k - 1), guess(k + 1)
        around = None
        if v is not None:
            around = sides_y(v, 1) + sides_z(v, 1)
        for side in (low, high):
            if side is not None:
                around = side if around is None else around + side
        applied = 6.0 * v - around if v is not None else -around
        d.put(k, inside0(k, refine_x(plus, k) - applied))
        mag = refine_x(minus, k)
        if 0 <= k < 16:
            for q in range(4):
                mag_ref[k, pl.ds(q, 8, stride=4), :] = mag[q]
        else:
            (low_ref if k < 0 else high_ref)[pl.ds(22, 4)] = mag

    t, r = Held(t_ref, -2), Held(r_ref, -3)
    hold_T(d, t, range(-2, 18), 1, inside0)
    hold_T(t, r, range(-3, 19), 1, inside0)

    def geometric(b, t, r, k, zstep):
        low, v, high = r.get(k - 1), r.get(k), r.get(k + 1)
        if v is None:
            last = (low if low is not None else high) * ALPHA
        else:
            last = smooth(low, v, high, zstep)
        for term in (r.get(k), t.get(k), b.get(k)):
            if term is not None:
                last = last + term
        return last * ALPHA

    for k in range(16):
        own0_ref[k] = geometric(d, t, r, k, 1)
    for k in range(4):
        low_ref[pl.ds(4 * k, 4)] = geometric(d, t, r, k - 4, 1)
        high_ref[pl.ds(4 * k, 4)] = geometric(d, t, r, k + 16, 1)

    b1 = {}
    for k in range(-2, 10):
        total = None
        for fine in (2 * k, 2 * k + 1):
            v = r.get(fine)
            if v is not None:
                total = v if total is None else total + v
        total = jnp.stack([total[0] + total[1], total[2] + total[3]], axis=0)
        b1[k] = 0.5 * pair_z(total, 1)
    t1 = run_T(b1, range(-3, 11), 2, mask=inside1)
    r1 = Held(t1_ref, -4)
    hold_T(t1, r1, range(-4, 12), 2, inside1)
    f1 = {k: geometric(b1, t1, r1, k, 2) for k in range(-5, 13)}
    for k in range(-1, 9):
        own1_ref[k + 1] = f1[k]
    even = (lanes_of((8, 128)) & 1) == 0
    for pair in range(3):
        for q in range(2):
            low_ref[16 + 2 * pair + q] = jnp.where(even, f1[2 * pair - 5][q], f1[2 * pair - 4][q])
            high_ref[16 + 2 * pair + q] = jnp.where(even, f1[2 * pair + 7][q], f1[2 * pair + 8][q])

    lane = lanes_of((8, 128)) & 3
    for group in range(2):
        packed = None
        for p in range(4):
            k = 4 * group + p - 2
            v = r1[2 * k] + r1[2 * k + 1]
            v = 0.5 * pair_z(v[0] + v[1], 2)
            packed = v if packed is None else jnp.where(lane == p, v, packed)
        far_ref[pl.ds(8 * group, 8), :] = packed


def local_part(flags, parts, guess):
    smem = pl.BlockSpec(memory_space=pltpu.SMEM)
    vmem = pl.BlockSpec(memory_space=pltpu.VMEM)
    shape = lambda *s: jax.ShapeDtypeStruct(s, F32)
    return pl.pallas_call(
        local_kernel,
        out_shape=(
            shape(16, 128), shape(26, 8, 128), shape(26, 8, 128),
            shape(16, 4, 8, 128), shape(10, 2, 8, 128), shape(16, 32, 128),
        ),
        in_specs=[smem, vmem, vmem],
        out_specs=(vmem,) * 6,
        scratch_shapes=[
            pltpu.VMEM((128, 128), F32), pltpu.VMEM((2, 128, 128), F32),
            pltpu.VMEM((18, 4, 8, 128), F32), pltpu.VMEM((20, 4, 8, 128), F32),
            pltpu.VMEM((22, 4, 8, 128), F32), pltpu.VMEM((16, 2, 8, 128), F32),
        ],
        compiler_params=pltpu.CompilerParams(vmem_limit_bytes=32 * 2**20),
        name="local",
    )(flags, parts, guess)


def final_kernel(
    place_ref, far_ref, mine_ref, low_ref, high_ref, own0_ref, own1_ref, mag_ref, guess_ref,
    pot_out, mag_out,
    b2_ref, t2_ref, r2_ref, p1_ref,
):
    dom = place_ref[0]

    def masked(count):
        first, last = -dom * count, (DOMS - dom) * count
        def mask(k, v):
            if 0 <= k < count:
                return v
            ok = (k >= first) & (k < last)
            return jnp.where(ok, v, 0.0)
        return mask

    lane = lanes_of((8, 128)) & 3
    def message(i):
        shift = i - REACH
        if shift == 0:
            return mine_ref, 0, None
        return far_ref, (0 if shift < 0 else 16), abs(shift)

    def vector(i, half):
        ref, row, member = message(i)
        rows = pl.ds(row + 8 * half, 8)
        return ref[rows, :] if member is None else ref[member, rows, :]

    b2, t2, r2 = Held(b2_ref, -30), Held(t2_ref, -25), Held(r2_ref, -24)
    for i in range(16):
        packed = None
        for part in ((i, 0), (i - 1, 1)):
            if 0 <= part[0] < 15:
                v = vector(*part)
                packed = v if packed is None else packed + v
        for p in range(4):
            only = jnp.where(lane == p, packed, 0.0)
            only = only + pltpu.roll(only, 1 if p % 2 == 0 else 127, 1)
            only = only + pltpu.roll(only, 2 if p < 2 else 126, 1)
            b2.put(4 * (i - REACH) - 2 + p, only)
    inside2, inside3, inside4 = masked(4), masked(2), masked(1)
    hold_T(b2, t2, range(-25, 29), 4, inside2)
    hold_T(t2, r2, range(-24, 28), 4, lambda k, v: v)

    b3 = {}
    for k in range(-12, 14):
        v = pair_y(pair_z(r2[2 * k] + r2[2 * k + 1], 4), 1)
        b3[k] = inside3(k, 0.5 * v)
    t3 = run_T(b3, range(-11, 13), 8, 2, inside3)
    r3 = run_T(t3, range(-10, 12), 8, 2)

    b4 = {}
    for k in range(-5, 6):
        v = pair_y(pair_z(r3[2 * k] + r3[2 * k + 1], 8), 2)
        b4[k] = inside4(k, 0.5 * v)
    t4 = run_T(b4, range(-4, 5), 16, 4, inside4)
    r4 = run_T(t4, range(-3, 4), 16, 4, inside4)
    u4 = run_T(r4, range(-2, 3), 16, 4)
    e4 = {k: ALPHA * (b4[k] + t4[k] + r4[k] + u4[k]) for k in range(-2, 3)}
    e4 = {k: inside4(k, v) for k, v in e4.items()}

    v3 = {k: ALPHA * t3[k] + e4[k // 2] for k in range(-4, 6)}
    v3 = run_T(v3, range(-3, 5), 8, 2, inside3)
    w3 = run_T(v3, range(-2, 4), 8, 2)
    e3 = {k: inside3(k, w3[k] + ALPHA * (b3[k] + t3[k] + r3[k])) for k in range(-2, 4)}

    v2 = {k: ALPHA * t2[k] + e3[k // 2] for k in range(-4, 8)}
    v2 = run_T(v2, range(-3, 7), 4, 1, inside2)
    w2 = run_T(v2, range(-2, 6), 4, 1)
    e2 = {k: inside2(k, w2[k] + ALPHA * (b2[k] + t2[k] + r2[k])) for k in range(-2, 6)}

    inside1, inside0 = masked(8), masked(16)
    spread = {k: jnp.stack([e2[k // 2]] * 2, axis=0) for k in range(-4, 12)}
    v1 = run_T(spread, range(-2, 10), 2, 1, inside1)
    w1 = run_T(v1, range(-1, 9), 2, 1)
    even = (lanes_of((8, 128)) & 1) == 0
    extra = {}
    for ref, first in ((low_ref, -1), (high_ref, 3)):
        for pair in range(3):
            both = [ref[16 + 2 * pair + q] for q in range(2)]
            one = jnp.stack([jnp.where(even, v, pltpu.roll(v, 1, 1)) for v in both], axis=0)
            two = jnp.stack([jnp.where(even, pltpu.roll(v, 127, 1), v) for v in both], axis=0)
            for k, v in ((first + 2 * pair, one), (first + 2 * pair + 1, two)):
                extra[k] = extra[k] + v if k in extra else v
    e1 = {}
    for k in range(-1, 9):
        e1[k] = inside1(k, w1[k] + own1_ref[k + 1] + extra[k])

    def prolonged(k):
        v = e1[k // 2]
        return jnp.stack([v[0], v[0], v[1], v[1]], axis=0)

    p1 = Held(p1_ref, -1)
    wide = {k: prolonged(k) for k in range(-2, 18)}
    hold_T(wide, p1, range(-1, 17), 1, inside0)
    for k in range(16):
        v = smooth(p1[k - 1], p1[k], p1[k + 1], 1) + own0_ref[k]
        if k < 4:
            v = v + low_ref[pl.ds(4 * k, 4)]
        if k >= 12:
            v = v + high_ref[pl.ds(4 * (k - 12), 4)]
        for q in range(4):
            rows = pl.ds(q, 8, stride=4)
            pot_out[k, rows, :] = guess_ref[k, rows, :] + v[q]
    mag_out[...] = mag_ref[...]
    for q in range(4):
        rows = pl.ds(q, 8, stride=4)
        mag_out[0, rows, :] = mag_ref[0, rows, :] + low_ref[22 + q]
        mag_out[15, rows, :] = mag_ref[15, rows, :] + high_ref[22 + q]


def final_part(place, far, mine, low, high, own0, own1, mag, guess):
    smem = pl.BlockSpec(memory_space=pltpu.SMEM)
    vmem = pl.BlockSpec(memory_space=pltpu.VMEM)
    shape = lambda *s: jax.ShapeDtypeStruct(s, F32)
    return pl.pallas_call(
        final_kernel,
        out_shape=(shape(16, 32, 128), shape(16, 32, 128)),
        in_specs=[smem] + [vmem] * 8,
        out_specs=(vmem, vmem),
        scratch_shapes=[
            pltpu.VMEM((64, 8, 128), F32), pltpu.VMEM((54, 8, 128), F32),
            pltpu.VMEM((52, 8, 128), F32), pltpu.VMEM((18, 4, 8, 128), F32),
        ],
        compiler_params=pltpu.CompilerParams(vmem_limit_bytes=32 * 2**20),
        name="final",
    )(place, far, mine, low, high, own0, own1, mag, guess)


def on_device(orbitals, spin_group, occupation, potential_guess):
    dom = lax.axis_index("dom")
    flags = jnp.stack([dom > 0, dom < DOMS - 1]).astype(F32)
    place = dom.astype(jnp.int32)[None]
    parts = lax.all_to_all(density(spin_group, occupation, orbitals), "band", 0, 0)
    far, to_low, to_high, own0, own1, mag = local_part(flags, parts, potential_guess)

    ups = [(k * DOMS + d, k * DOMS + d + k) for k in range(1, BANDS) for d in range(DOMS - k)]
    downs = [(target, source) for source, target in ups]
    from_low = lax.ppermute(far, ("band", "dom"), ups)
    from_high = lax.ppermute(far, ("band", "dom"), downs)
    near_low = lax.ppermute(to_high, "dom", [(d, d + 1) for d in range(DOMS - 1)])
    near_high = lax.ppermute(to_low, "dom", [(d + 1, d) for d in range(DOMS - 1)])
    both = jnp.concatenate([from_low, from_high], axis=0)
    everyone = lax.all_to_all(jnp.broadcast_to(both[None], (BANDS, 32, 128)), "band", 0, 0)
    return final_part(
        place, everyone, far, near_low, near_high, own0, own1, mag, potential_guess
    )


def solution(mesh):
    placed = (P("band", "dom", None, None), P("band"), P("band"), P("dom", None, None))
    return jax.shard_map(
        on_device,
        mesh=mesh,
        in_specs=placed,
        out_specs=(P("dom", None, None), P("dom", None, None)),
        check_vma=False,
    )
```

```python
import functools

import jax
import jax.numpy as jnp
from jax import lax
from jax.experimental import pallas as pl
from jax.experimental.pallas import tpu as pltpu
from jax.sharding import PartitionSpec as P

DEN = 16
BANDS = 8
DOMS = 64
REACH = 7
RING = 16
ALPHA = 1.0 / 9.0
SOURCE_SCALE = 0.6
F32 = jnp.float32


def lanes_of(shape):
    return lax.broadcasted_iota(jnp.int32, shape, len(shape) - 1)


def rows_of(shape):
    return lax.broadcasted_iota(jnp.int32, shape, len(shape) - 2)


def sides_z(v, step):
    lane = lanes_of(v.shape)
    ax = v.ndim - 1
    left = jnp.where(lane >= step, pltpu.roll(v, step, ax), 0.0)
    right = jnp.where(lane < 128 - step, pltpu.roll(v, 128 - step, ax), 0.0)
    return left + right


def from_below(v, step=1):
    return jnp.where(rows_of(v.shape) >= step, pltpu.roll(v, step, v.ndim - 2), 0.0)


def from_above(v, step=1):
    return jnp.where(rows_of(v.shape) < 8 - step, pltpu.roll(v, 8 - step, v.ndim - 2), 0.0)


def sides_y(v, step):
    if v.ndim == 2:
        return from_below(v, step) + from_above(v, step)
    parts = [v[q] for q in range(v.shape[0])]
    n = len(parts)
    out = []
    for q in range(n):
        lower = parts[q - 1] if q > 0 else from_below(parts[n - 1])
        upper = parts[q + 1] if q < n - 1 else from_above(parts[0])
        out.append(lower + upper)
    return jnp.stack(out, axis=0)


def smooth(low, v, high, zstep, ystep=1):
    around = sides_y(v, ystep) + sides_z(v, zstep)
    if low is not None:
        around = around + low
    if high is not None:
        around = around + high
    return v * (1.0 / 3.0) + around * ALPHA


def pair_z(v, step):
    lane = lanes_of(v.shape)
    ax = v.ndim - 1
    other = jnp.where((lane & step) == 0, pltpu.roll(v, 128 - step, ax), pltpu.roll(v, step, ax))
    return v + other


def pair_y(v, step):
    row = rows_of(v.shape)
    ax = v.ndim - 2
    other = jnp.where((row & step) == 0, pltpu.roll(v, 8 - step, ax), pltpu.roll(v, step, ax))
    return v + other


def run_T(src, planes, zstep, ystep=1, mask=None):
    out = {}
    for k in planes:
        v = src.get(k)
        low, high = src.get(k - 1), src.get(k + 1)
        if v is None:
            edge = low if low is not None else high
            got = edge * ALPHA
        else:
            got = smooth(low, v, high, zstep, ystep)
        out[k] = got if mask is None else mask(k, got)
    return out


class Held:
    def __init__(self, ref, first):
        self.ref, self.first, self.have = ref, first, set()

    def put(self, k, value):
        self.ref[k - self.first] = value
        self.have.add(k)

    def get(self, k):
        return self.ref[k - self.first] if k in self.have else None

    def __getitem__(self, k):
        return self.ref[k - self.first]


def hold_T(src, held, planes, zstep, mask):
    for k in planes:
        v = src.get(k)
        low, high = src.get(k - 1), src.get(k + 1)
        if v is None:
            got = (low if low is not None else high) * ALPHA
        else:
            got = smooth(low, v, high, zstep)
        held.put(k, mask(k, got))


def density_kernel(spin_hbm, occ_hbm, orb_hbm, out_ref, spin_ref, occ_ref, orb_ref, sems):
    copies = [
        pltpu.make_async_copy(spin_hbm, spin_ref, sems.at[8]),
        pltpu.make_async_copy(occ_hbm, occ_ref, sems.at[9]),
    ]
    copies += [pltpu.make_async_copy(orb_hbm.at[k], orb_ref.at[k], sems.at[k]) for k in range(8)]
    for copy in copies:
        copy.start()
    copies[0].wait()
    copies[1].wait()
    ups, downs = [0.0] * 8, [0.0] * 8
    for k in range(8):
        weight = occ_ref[k].astype(F32) * (0.125 / DEN)
        up = spin_ref[k] == 0
        up, down = jnp.where(up, weight, 0.0), jnp.where(up, 0.0, weight)
        copies[2 + k].wait()
        for x in range(8):
            square = orb_ref[k, x] * orb_ref[k, x]
            ups[x] = ups[x] + up * square
            downs[x] = downs[x] + down * square
    for x in range(8):
        both = jnp.concatenate([ups[x], downs[x]], axis=-1)
        for copy in range(BANDS):
            out_ref[copy, pl.ds(16 * x, 16), :] = both


def density(spin_group, occupation, orbitals):
    anywhere = pl.BlockSpec(memory_space=pl.ANY)
    vmem = pl.BlockSpec(memory_space=pltpu.VMEM)
    return pl.pallas_call(
        density_kernel,
        out_shape=jax.ShapeDtypeStruct((BANDS, 128, 128), F32),
        in_specs=[anywhere] * 3,
        out_specs=vmem,
        scratch_shapes=[
            pltpu.SMEM((8,), jnp.int32), pltpu.SMEM((8,), jnp.int32),
            pltpu.VMEM((8, 8, 16, 64), F32), pltpu.SemaphoreType.DMA((10,)),
        ],
        compiler_params=pltpu.CompilerParams(vmem_limit_bytes=32 * 2**20),
        name="density",
    )(spin_group, occupation, orbitals)


def refine_matrix():
    row = lax.broadcasted_iota(jnp.int32, (128, 256), 0)
    col = lax.broadcasted_iota(jnp.int32, (128, 256), 1)
    cell, spin = row & 63, row >> 6
    fine, half = col & 127, col >> 7
    own = fine >> 1
    other = jnp.where((fine & 1) == 0, own - 1, own + 1)
    value = jnp.where(cell == own, 0.75, jnp.where(cell == other, 0.25, 0.0))
    return jnp.where((spin == 1) & (half == 1), -value, value)


def refine_y(pair):
    first, second = pair
    return jnp.stack(
        [
            0.75 * first + 0.25 * from_below(second),
            0.75 * first + 0.25 * second,
            0.75 * second + 0.25 * first,
            0.75 * second + 0.25 * from_above(first),
        ],
        axis=0,
    )


def refine_x(coarse, k):
    i = k // 2
    other = i - 1 if k % 2 == 0 else i + 1
    total = None
    for j, factor in ((i, 0.75), (other, 0.25)):
        if 0 <= j < 8:
            term = factor * coarse[j]
            total = term if total is None else total + term
    return total


def local_kernel(
    flag_ref, part_ref, guess_ref,
    far_ref, low_ref, high_ref, own0_ref, own1_ref, mag_ref,
    sum_ref, wide_ref, d_ref, t_ref, r_ref, t1_ref,
):
    low_flag, high_flag = flag_ref[0], flag_ref[1]

    def masked(last):
        def mask(k, v):
            if k < 0:
                return v * low_flag
            if k > last:
                return v * high_flag
            return v
        return mask

    inside0, inside1 = masked(15), masked(7)

    for x in range(8):
        rows = pl.ds(16 * x, 16)
        total = part_ref[0, rows, :]
        for band in range(1, BANDS):
            total = total + part_ref[band, rows, :]
        sum_ref[rows, :] = total
    wide = jnp.dot(
        sum_ref[...], refine_matrix(),
        precision=lax.Precision.HIGHEST, preferred_element_type=F32,
    )
    wide_ref[0], wide_ref[1] = wide[:, :128], wide[:, 128:]
    plus, minus = [], []
    for x in range(8):
        pairs = [[wide_ref[half, pl.ds(16 * x + p, 8, stride=2), :] for p in range(2)] for half in range(2)]
        plus.append(SOURCE_SCALE * refine_y(pairs[0]))
        minus.append(refine_y(pairs[1]))

    def guess(k):
        if not 0 <= k < 16:
            return None
        return jnp.stack([guess_ref[k, pl.ds(q, 8, stride=4), :] for q in range(4)], axis=0)

    d = Held(d_ref, -1)
    for k in range(-1, 17):
        v, low, high = guess(k), guess(k - 1), guess(k + 1)
        around = None
        if v is not None:
            around = sides_y(v, 1) + sides_z(v, 1)
        for side in (low, high):
            if side is not None:
                around = side if around is None else around + side
        applied = 6.0 * v - around if v is not None else -around
        d.put(k, inside0(k, refine_x(plus, k) - applied))
        mag = refine_x(minus, k)
        if 0 <= k < 16:
            for q in range(4):
                mag_ref[k, pl.ds(q, 8, stride=4), :] = mag[q]
        else:
            (low_ref if k < 0 else high_ref)[pl.ds(22, 4)] = mag

    t, r = Held(t_ref, -2), Held(r_ref, -3)
    hold_T(d, t, range(-2, 18), 1, inside0)
    hold_T(t, r, range(-3, 19), 1, inside0)

    def geometric(b, t, r, k, zstep):
        low, v, high = r.get(k - 1), r.get(k), r.get(k + 1)
        if v is None:
            last = (low if low is not None else high) * ALPHA
        else:
            last = smooth(low, v, high, zstep)
        for term in (r.get(k), t.get(k), b.get(k)):
            if term is not None:
                last = last + term
        return last * ALPHA

    for k in range(16):
        own0_ref[k] = geometric(d, t, r, k, 1)
    for k in range(4):
        low_ref[pl.ds(4 * k, 4)] = geometric(d, t, r, k - 4, 1)
        high_ref[pl.ds(4 * k, 4)] = geometric(d, t, r, k + 16, 1)

    b1 = {}
    for k in range(-2, 10):
        total = None
        for fine in (2 * k, 2 * k + 1):
            v = r.get(fine)
            if v is not None:
                total = v if total is None else total + v
        total = jnp.stack([total[0] + total[1], total[2] + total[3]], axis=0)
        b1[k] = 0.5 * pair_z(total, 1)
    t1 = run_T(b1, range(-3, 11), 2, mask=inside1)
    r1 = Held(t1_ref, -4)
    hold_T(t1, r1, range(-4, 12), 2, inside1)
    f1 = {k: geometric(b1, t1, r1, k, 2) for k in range(-5, 13)}
    for k in range(-1, 9):
        own1_ref[k + 1] = f1[k]
    even = (lanes_of((8, 128)) & 1) == 0
    for pair in range(3):
        for q in range(2):
            low_ref[16 + 2 * pair + q] = jnp.where(even, f1[2 * pair - 5][q], f1[2 * pair - 4][q])
            high_ref[16 + 2 * pair + q] = jnp.where(even, f1[2 * pair + 7][q], f1[2 * pair + 8][q])

    lane = lanes_of((8, 128)) & 3
    for group in range(2):
        packed = None
        for p in range(4):
            k = 4 * group + p - 2
            v = r1[2 * k] + r1[2 * k + 1]
            v = 0.5 * pair_z(v[0] + v[1], 2)
            packed = v if packed is None else jnp.where(lane == p, v, packed)
        for copy in range(RING):
            far_ref[copy, pl.ds(8 * group, 8), :] = packed


def local_part(flags, parts, guess):
    smem = pl.BlockSpec(memory_space=pltpu.SMEM)
    vmem = pl.BlockSpec(memory_space=pltpu.VMEM)
    shape = lambda *s: jax.ShapeDtypeStruct(s, F32)
    return pl.pallas_call(
        local_kernel,
        out_shape=(
            shape(RING, 16, 128), shape(26, 8, 128), shape(26, 8, 128),
            shape(16, 4, 8, 128), shape(10, 2, 8, 128), shape(16, 32, 128),
        ),
        in_specs=[smem, vmem, vmem],
        out_specs=(vmem,) * 6,
        scratch_shapes=[
            pltpu.VMEM((128, 128), F32), pltpu.VMEM((2, 128, 128), F32),
            pltpu.VMEM((18, 4, 8, 128), F32), pltpu.VMEM((20, 4, 8, 128), F32),
            pltpu.VMEM((22, 4, 8, 128), F32), pltpu.VMEM((16, 2, 8, 128), F32),
        ],
        compiler_params=pltpu.CompilerParams(vmem_limit_bytes=32 * 2**20),
        name="local",
    )(flags, parts, guess)


def final_kernel(
    place_ref, far_ref, mine_ref, low_ref, high_ref, own0_ref, own1_ref, mag_ref, guess_ref,
    pot_out, mag_out,
    b2_ref, t2_ref, r2_ref, p1_ref,
):
    dom = place_ref[0]

    def masked(count):
        first, last = -dom * count, (DOMS - dom) * count
        def mask(k, v):
            if 0 <= k < count:
                return v
            ok = (k >= first) & (k < last)
            return jnp.where(ok, v, 0.0)
        return mask

    lane = lanes_of((8, 128)) & 3
    core = place_ref[1]
    ring, spot = dom // RING, dom % RING
    even_first = RING * ring
    odd_first = even_first + jnp.where(spot >= RING // 2, RING // 2, -(RING // 2))

    def vector(i, half):
        wanted = dom - REACH + i
        at = wanted - even_first
        in_even = (at >= 0) & (at < RING)
        at = jnp.clip(jnp.where(in_even, at, wanted - odd_first), 0, RING - 1)
        rows = pl.ds(8 * half, 8)
        held = in_even == (core == 0)
        v = jnp.where(held, mine_ref[at, rows, :], far_ref[at, rows, :])
        return jnp.where((wanted >= 0) & (wanted < DOMS), v, 0.0)

    b2, t2, r2 = Held(b2_ref, -30), Held(t2_ref, -25), Held(r2_ref, -24)
    for i in range(16):
        packed = None
        for part in ((i, 0), (i - 1, 1)):
            if 0 <= part[0] < 15:
                v = vector(*part)
                packed = v if packed is None else packed + v
        for p in range(4):
            only = jnp.where(lane == p, packed, 0.0)
            only = only + pltpu.roll(only, 1 if p % 2 == 0 else 127, 1)
            only = only + pltpu.roll(only, 2 if p < 2 else 126, 1)
            b2.put(4 * (i - REACH) - 2 + p, only)
    inside2, inside3, inside4 = masked(4), masked(2), masked(1)
    hold_T(b2, t2, range(-25, 29), 4, inside2)
    hold_T(t2, r2, range(-24, 28), 4, lambda k, v: v)

    b3 = {}
    for k in range(-12, 14):
        v = pair_y(pair_z(r2[2 * k] + r2[2 * k + 1], 4), 1)
        b3[k] = inside3(k, 0.5 * v)
    t3 = run_T(b3, range(-11, 13), 8, 2, inside3)
    r3 = run_T(t3, range(-10, 12), 8, 2)

    b4 = {}
    for k in range(-5, 6):
        v = pair_y(pair_z(r3[2 * k] + r3[2 * k + 1], 8), 2)
        b4[k] = inside4(k, 0.5 * v)
    t4 = run_T(b4, range(-4, 5), 16, 4, inside4)
    r4 = run_T(t4, range(-3, 4), 16, 4, inside4)
    u4 = run_T(r4, range(-2, 3), 16, 4)
    e4 = {k: ALPHA * (b4[k] + t4[k] + r4[k] + u4[k]) for k in range(-2, 3)}
    e4 = {k: inside4(k, v) for k, v in e4.items()}

    v3 = {k: ALPHA * t3[k] + e4[k // 2] for k in range(-4, 6)}
    v3 = run_T(v3, range(-3, 5), 8, 2, inside3)
    w3 = run_T(v3, range(-2, 4), 8, 2)
    e3 = {k: inside3(k, w3[k] + ALPHA * (b3[k] + t3[k] + r3[k])) for k in range(-2, 4)}

    v2 = {k: ALPHA * t2[k] + e3[k // 2] for k in range(-4, 8)}
    v2 = run_T(v2, range(-3, 7), 4, 1, inside2)
    w2 = run_T(v2, range(-2, 6), 4, 1)
    e2 = {k: inside2(k, w2[k] + ALPHA * (b2[k] + t2[k] + r2[k])) for k in range(-2, 6)}

    inside1, inside0 = masked(8), masked(16)
    spread = {k: jnp.stack([e2[k // 2]] * 2, axis=0) for k in range(-4, 12)}
    v1 = run_T(spread, range(-2, 10), 2, 1, inside1)
    w1 = run_T(v1, range(-1, 9), 2, 1)
    even = (lanes_of((8, 128)) & 1) == 0
    extra = {}
    for ref, first in ((low_ref, -1), (high_ref, 3)):
        for pair in range(3):
            both = [ref[16 + 2 * pair + q] for q in range(2)]
            one = jnp.stack([jnp.where(even, v, pltpu.roll(v, 1, 1)) for v in both], axis=0)
            two = jnp.stack([jnp.where(even, pltpu.roll(v, 127, 1), v) for v in both], axis=0)
            for k, v in ((first + 2 * pair, one), (first + 2 * pair + 1, two)):
                extra[k] = extra[k] + v if k in extra else v
    e1 = {}
    for k in range(-1, 9):
        e1[k] = inside1(k, w1[k] + own1_ref[k + 1] + extra[k])

    def prolonged(k):
        v = e1[k // 2]
        return jnp.stack([v[0], v[0], v[1], v[1]], axis=0)

    p1 = Held(p1_ref, -1)
    wide = {k: prolonged(k) for k in range(-2, 18)}
    hold_T(wide, p1, range(-1, 17), 1, inside0)
    for k in range(16):
        v = smooth(p1[k - 1], p1[k], p1[k + 1], 1) + own0_ref[k]
        if k < 4:
            v = v + low_ref[pl.ds(4 * k, 4)]
        if k >= 12:
            v = v + high_ref[pl.ds(4 * (k - 12), 4)]
        for q in range(4):
            rows = pl.ds(q, 8, stride=4)
            pot_out[k, rows, :] = guess_ref[k, rows, :] + v[q]
    mag_out[...] = mag_ref[...]
    for q in range(4):
        rows = pl.ds(q, 8, stride=4)
        mag_out[0, rows, :] = mag_ref[0, rows, :] + low_ref[22 + q]
        mag_out[15, rows, :] = mag_ref[15, rows, :] + high_ref[22 + q]


def final_part(place, far, mine, low, high, own0, own1, mag, guess):
    smem = pl.BlockSpec(memory_space=pltpu.SMEM)
    vmem = pl.BlockSpec(memory_space=pltpu.VMEM)
    shape = lambda *s: jax.ShapeDtypeStruct(s, F32)
    return pl.pallas_call(
        final_kernel,
        out_shape=(shape(16, 32, 128), shape(16, 32, 128)),
        in_specs=[smem] + [vmem] * 8,
        out_specs=(vmem, vmem),
        scratch_shapes=[
            pltpu.VMEM((64, 8, 128), F32), pltpu.VMEM((54, 8, 128), F32),
            pltpu.VMEM((52, 8, 128), F32), pltpu.VMEM((18, 4, 8, 128), F32),
        ],
        compiler_params=pltpu.CompilerParams(vmem_limit_bytes=32 * 2**20),
        name="final",
    )(place, far, mine, low, high, own0, own1, mag, guess)


def on_device(orbitals, spin_group, occupation, potential_guess):
    dom = lax.axis_index("dom")
    flags = jnp.stack([dom > 0, dom < DOMS - 1]).astype(F32)
    core = lax.axis_index("band") % 2
    place = jnp.stack([dom, core]).astype(jnp.int32)
    parts = lax.all_to_all(density(spin_group, occupation, orbitals), "band", 0, 0)
    far, to_low, to_high, own0, own1, mag = local_part(flags, parts, potential_guess)

    rings = [
        [b * DOMS + (first + 8 * (b % 2) + i) % DOMS for i in range(RING)]
        for b in range(BANDS) for first in range(0, DOMS, RING)
    ]
    mine = lax.all_to_all(far, ("band", "dom"), 0, 0, axis_index_groups=rings)
    near_low = lax.ppermute(to_high, "dom", [(d, d + 1) for d in range(DOMS - 1)])
    near_high = lax.ppermute(to_low, "dom", [(d + 1, d) for d in range(DOMS - 1)])
    other = lax.ppermute(mine, "band", [(b, b ^ 1) for b in range(BANDS)])
    return final_part(
        place, other, mine, near_low, near_high, own0, own1, mag, potential_guess
    )


def solution(mesh):
    placed = (P("band", "dom", None, None), P("band"), P("band"), P("dom", None, None))
    return jax.shard_map(
        on_device,
        mesh=mesh,
        in_specs=placed,
        out_specs=(P("dom", None, None), P("dom", None, None)),
        check_vma=False,
    )
```

```python
import functools

import jax
import jax.numpy as jnp
from jax import lax
from jax.experimental import pallas as pl
from jax.experimental.pallas import tpu as pltpu
from jax.sharding import PartitionSpec as P

DEN = 16
BANDS = 8
DOMS = 64
REACH = 7
RING = 16
ALPHA = 1.0 / 9.0
SOURCE_SCALE = 0.6
F32 = jnp.float32


def lanes_of(shape):
    return lax.broadcasted_iota(jnp.int32, shape, len(shape) - 1)


def rows_of(shape):
    return lax.broadcasted_iota(jnp.int32, shape, len(shape) - 2)


def sides_z(v, step):
    lane = lanes_of(v.shape)
    ax = v.ndim - 1
    left = jnp.where(lane >= step, pltpu.roll(v, step, ax), 0.0)
    right = jnp.where(lane < 128 - step, pltpu.roll(v, 128 - step, ax), 0.0)
    return left + right


def from_below(v, step=1):
    return jnp.where(rows_of(v.shape) >= step, pltpu.roll(v, step, v.ndim - 2), 0.0)


def from_above(v, step=1):
    return jnp.where(rows_of(v.shape) < 8 - step, pltpu.roll(v, 8 - step, v.ndim - 2), 0.0)


def sides_y(v, step):
    if v.ndim == 2:
        return from_below(v, step) + from_above(v, step)
    parts = [v[q] for q in range(v.shape[0])]
    n = len(parts)
    out = []
    for q in range(n):
        lower = parts[q - 1] if q > 0 else from_below(parts[n - 1])
        upper = parts[q + 1] if q < n - 1 else from_above(parts[0])
        out.append(lower + upper)
    return jnp.stack(out, axis=0)


def smooth(low, v, high, zstep, ystep=1):
    around = sides_y(v, ystep) + sides_z(v, zstep)
    if low is not None:
        around = around + low
    if high is not None:
        around = around + high
    return v * (1.0 / 3.0) + around * ALPHA


def pair_z(v, step):
    lane = lanes_of(v.shape)
    ax = v.ndim - 1
    other = jnp.where((lane & step) == 0, pltpu.roll(v, 128 - step, ax), pltpu.roll(v, step, ax))
    return v + other


def pair_y(v, step):
    row = rows_of(v.shape)
    ax = v.ndim - 2
    other = jnp.where((row & step) == 0, pltpu.roll(v, 8 - step, ax), pltpu.roll(v, step, ax))
    return v + other


def run_T(src, planes, zstep, ystep=1, mask=None):
    out = {}
    for k in planes:
        v = src.get(k)
        low, high = src.get(k - 1), src.get(k + 1)
        if v is None:
            edge = low if low is not None else high
            got = edge * ALPHA
        else:
            got = smooth(low, v, high, zstep, ystep)
        out[k] = got if mask is None else mask(k, got)
    return out


class Held:
    def __init__(self, ref, first):
        self.ref, self.first, self.have = ref, first, set()

    def put(self, k, value):
        self.ref[k - self.first] = value
        self.have.add(k)

    def get(self, k):
        return self.ref[k - self.first] if k in self.have else None

    def __getitem__(self, k):
        return self.ref[k - self.first]


def hold_T(src, held, planes, zstep, mask):
    for k in planes:
        v = src.get(k)
        low, high = src.get(k - 1), src.get(k + 1)
        if v is None:
            got = (low if low is not None else high) * ALPHA
        else:
            got = smooth(low, v, high, zstep)
        held.put(k, mask(k, got))


def density_kernel(spin_hbm, occ_hbm, orb_hbm, out_hbm, spin_ref, occ_ref, orb_ref, own_ref, sems):
    copies = [
        pltpu.make_async_copy(spin_hbm, spin_ref, sems.at[8]),
        pltpu.make_async_copy(occ_hbm, occ_ref, sems.at[9]),
    ]
    copies += [pltpu.make_async_copy(orb_hbm.at[k], orb_ref.at[k], sems.at[k]) for k in range(8)]
    for copy in copies:
        copy.start()
    copies[0].wait()
    copies[1].wait()
    ups, downs = [0.0] * 8, [0.0] * 8
    for k in range(8):
        weight = occ_ref[k].astype(F32) * (0.125 / DEN)
        up = spin_ref[k] == 0
        up, down = jnp.where(up, weight, 0.0), jnp.where(up, 0.0, weight)
        copies[2 + k].wait()
        for x in range(8):
            square = orb_ref[k, x] * orb_ref[k, x]
            ups[x] = ups[x] + up * square
            downs[x] = downs[x] + down * square
    for x in range(8):
        own_ref[pl.ds(16 * x, 16), :] = jnp.concatenate([ups[x], downs[x]], axis=-1)
    copies = [pltpu.make_async_copy(own_ref, out_hbm.at[b], sems.at[b]) for b in range(BANDS)]
    for copy in copies:
        copy.start()
    for copy in copies:
        copy.wait()


def density(spin_group, occupation, orbitals):
    hbm = pl.BlockSpec(memory_space=pltpu.HBM)
    return pl.pallas_call(
        density_kernel,
        out_shape=jax.ShapeDtypeStruct((BANDS, 128, 128), F32),
        in_specs=[hbm] * 3,
        out_specs=hbm,
        scratch_shapes=[
            pltpu.SMEM((8,), jnp.int32), pltpu.SMEM((8,), jnp.int32),
            pltpu.VMEM((8, 8, 16, 64), F32), pltpu.VMEM((128, 128), F32),
            pltpu.SemaphoreType.DMA((10,)),
        ],
        compiler_params=pltpu.CompilerParams(vmem_limit_bytes=60 * 2**20),
        name="density",
    )(spin_group, occupation, orbitals)


def refine_matrix():
    row = lax.broadcasted_iota(jnp.int32, (128, 256), 0)
    col = lax.broadcasted_iota(jnp.int32, (128, 256), 1)
    cell, spin = row & 63, row >> 6
    fine, half = col & 127, col >> 7
    own = fine >> 1
    other = jnp.where((fine & 1) == 0, own - 1, own + 1)
    value = jnp.where(cell == own, 0.75, jnp.where(cell == other, 0.25, 0.0))
    return jnp.where((spin == 1) & (half == 1), -value, value)


def refine_y(pair):
    first, second = pair
    return jnp.stack(
        [
            0.75 * first + 0.25 * from_below(second),
            0.75 * first + 0.25 * second,
            0.75 * second + 0.25 * first,
            0.75 * second + 0.25 * from_above(first),
        ],
        axis=0,
    )


def refine_x(coarse, k):
    i = k // 2
    other = i - 1 if k % 2 == 0 else i + 1
    total = None
    for j, factor in ((i, 0.75), (other, 0.25)):
        if 0 <= j < 8:
            term = factor * coarse[j]
            total = term if total is None else total + term
    return total


def local_kernel(
    flag_ref, part_ref, guess_ref,
    far_hbm, low_ref, high_ref, own0_ref, own1_ref, mag_ref,
    sum_ref, wide_ref, d_ref, t_ref, r_ref, t1_ref, far_ref, sems,
):
    low_flag, high_flag = flag_ref[0], flag_ref[1]

    def masked(last):
        def mask(k, v):
            if k < 0:
                return v * low_flag
            if k > last:
                return v * high_flag
            return v
        return mask

    inside0, inside1 = masked(15), masked(7)

    for x in range(8):
        rows = pl.ds(16 * x, 16)
        total = part_ref[0, rows, :]
        for band in range(1, BANDS):
            total = total + part_ref[band, rows, :]
        sum_ref[rows, :] = total
    wide = jnp.dot(
        sum_ref[...], refine_matrix(),
        precision=lax.Precision.HIGHEST, preferred_element_type=F32,
    )
    wide_ref[0], wide_ref[1] = wide[:, :128], wide[:, 128:]
    plus, minus = [], []
    for x in range(8):
        pairs = [[wide_ref[half, pl.ds(16 * x + p, 8, stride=2), :] for p in range(2)] for half in range(2)]
        plus.append(SOURCE_SCALE * refine_y(pairs[0]))
        minus.append(refine_y(pairs[1]))

    def guess(k):
        if not 0 <= k < 16:
            return None
        return jnp.stack([guess_ref[k, pl.ds(q, 8, stride=4), :] for q in range(4)], axis=0)

    d = Held(d_ref, -1)
    for k in range(-1, 17):
        v, low, high = guess(k), guess(k - 1), guess(k + 1)
        around = None
        if v is not None:
            around = sides_y(v, 1) + sides_z(v, 1)
        for side in (low, high):
            if side is not None:
                around = side if around is None else around + side
        applied = 6.0 * v - around if v is not None else -around
        d.put(k, inside0(k, refine_x(plus, k) - applied))
        mag = refine_x(minus, k)
        if 0 <= k < 16:
            for q in range(4):
                mag_ref[k, pl.ds(q, 8, stride=4), :] = mag[q]
        else:
            (low_ref if k < 0 else high_ref)[pl.ds(22, 4)] = mag

    t, r = Held(t_ref, -2), Held(r_ref, -3)
    hold_T(d, t, range(-2, 18), 1, inside0)
    hold_T(t, r, range(-3, 19), 1, inside0)

    def geometric(b, t, r, k, zstep):
        low, v, high = r.get(k - 1), r.get(k), r.get(k + 1)
        if v is None:
            last = (low if low is not None else high) * ALPHA
        else:
            last = smooth(low, v, high, zstep)
        for term in (r.get(k), t.get(k), b.get(k)):
            if term is not None:
                last = last + term
        return last * ALPHA

    for k in range(16):
        own0_ref[k] = geometric(d, t, r, k, 1)
    for k in range(4):
        low_ref[pl.ds(4 * k, 4)] = geometric(d, t, r, k - 4, 1)
        high_ref[pl.ds(4 * k, 4)] = geometric(d, t, r, k + 16, 1)

    b1 = {}
    for k in range(-2, 10):
        total = None
        for fine in (2 * k, 2 * k + 1):
            v = r.get(fine)
            if v is not None:
                total = v if total is None else total + v
        total = jnp.stack([total[0] + total[1], total[2] + total[3]], axis=0)
        b1[k] = 0.5 * pair_z(total, 1)
    t1 = run_T(b1, range(-3, 11), 2, mask=inside1)
    r1 = Held(t1_ref, -4)
    hold_T(t1, r1, range(-4, 12), 2, inside1)
    f1 = {k: geometric(b1, t1, r1, k, 2) for k in range(-5, 13)}
    for k in range(-1, 9):
        own1_ref[k + 1] = f1[k]
    even = (lanes_of((8, 128)) & 1) == 0
    for pair in range(3):
        for q in range(2):
            low_ref[16 + 2 * pair + q] = jnp.where(even, f1[2 * pair - 5][q], f1[2 * pair - 4][q])
            high_ref[16 + 2 * pair + q] = jnp.where(even, f1[2 * pair + 7][q], f1[2 * pair + 8][q])

    lane = lanes_of((8, 128)) & 3
    for group in range(2):
        packed = None
        for p in range(4):
            k = 4 * group + p - 2
            v = r1[2 * k] + r1[2 * k + 1]
            v = 0.5 * pair_z(v[0] + v[1], 2)
            packed = v if packed is None else jnp.where(lane == p, v, packed)
        far_ref[pl.ds(8 * group, 8), :] = packed
    copies = [pltpu.make_async_copy(far_ref, far_hbm.at[i], sems.at[i]) for i in range(RING)]
    for copy in copies:
        copy.start()
    for copy in copies:
        copy.wait()


def local_part(flags, parts, guess):
    smem = pl.BlockSpec(memory_space=pltpu.SMEM)
    vmem = pl.BlockSpec(memory_space=pltpu.VMEM)
    shape = lambda *s: jax.ShapeDtypeStruct(s, F32)
    return pl.pallas_call(
        local_kernel,
        out_shape=(
            shape(RING, 16, 128), shape(26, 8, 128), shape(26, 8, 128),
            shape(16, 4, 8, 128), shape(10, 2, 8, 128), shape(16, 32, 128),
        ),
        in_specs=[smem, vmem, vmem],
        out_specs=(pl.BlockSpec(memory_space=pltpu.HBM),) + (vmem,) * 5,
        scratch_shapes=[
            pltpu.VMEM((128, 128), F32), pltpu.VMEM((2, 128, 128), F32),
            pltpu.VMEM((18, 4, 8, 128), F32), pltpu.VMEM((20, 4, 8, 128), F32),
            pltpu.VMEM((22, 4, 8, 128), F32), pltpu.VMEM((16, 2, 8, 128), F32),
            pltpu.VMEM((16, 128), F32), pltpu.SemaphoreType.DMA((RING,)),
        ],
        compiler_params=pltpu.CompilerParams(vmem_limit_bytes=32 * 2**20),
        name="local",
    )(flags, parts, guess)


def final_kernel(
    place_ref, far_ref, mine_ref, low_ref, high_ref, own0_ref, own1_ref, mag_ref, guess_ref,
    pot_out, mag_out,
    b2_ref, t2_ref, r2_ref, p1_ref,
):
    dom = place_ref[0]

    def masked(count):
        first, last = -dom * count, (DOMS - dom) * count
        def mask(k, v):
            if 0 <= k < count:
                return v
            ok = (k >= first) & (k < last)
            return jnp.where(ok, v, 0.0)
        return mask

    lane = lanes_of((8, 128)) & 3
    core = place_ref[1]
    ring, spot = dom // RING, dom % RING
    even_first = RING * ring
    odd_first = even_first + jnp.where(spot >= RING // 2, RING // 2, -(RING // 2))

    def vector(i, half):
        wanted = dom - REACH + i
        at = wanted - even_first
        in_even = (at >= 0) & (at < RING)
        at = jnp.clip(jnp.where(in_even, at, wanted - odd_first), 0, RING - 1)
        rows = pl.ds(8 * half, 8)
        held = in_even == (core == 0)
        v = jnp.where(held, mine_ref[at, rows, :], far_ref[at, rows, :])
        return jnp.where((wanted >= 0) & (wanted < DOMS), v, 0.0)

    b2, t2, r2 = Held(b2_ref, -30), Held(t2_ref, -25), Held(r2_ref, -24)
    for i in range(16):
        packed = None
        for part in ((i, 0), (i - 1, 1)):
            if 0 <= part[0] < 15:
                v = vector(*part)
                packed = v if packed is None else packed + v
        for p in range(4):
            only = jnp.where(lane == p, packed, 0.0)
            only = only + pltpu.roll(only, 1 if p % 2 == 0 else 127, 1)
            only = only + pltpu.roll(only, 2 if p < 2 else 126, 1)
            b2.put(4 * (i - REACH) - 2 + p, only)
    inside2, inside3, inside4 = masked(4), masked(2), masked(1)
    hold_T(b2, t2, range(-25, 29), 4, inside2)
    hold_T(t2, r2, range(-24, 28), 4, lambda k, v: v)

    b3 = {}
    for k in range(-12, 14):
        v = pair_y(pair_z(r2[2 * k] + r2[2 * k + 1], 4), 1)
        b3[k] = inside3(k, 0.5 * v)
    t3 = run_T(b3, range(-11, 13), 8, 2, inside3)
    r3 = run_T(t3, range(-10, 12), 8, 2)

    b4 = {}
    for k in range(-5, 6):
        v = pair_y(pair_z(r3[2 * k] + r3[2 * k + 1], 8), 2)
        b4[k] = inside4(k, 0.5 * v)
    t4 = run_T(b4, range(-4, 5), 16, 4, inside4)
    r4 = run_T(t4, range(-3, 4), 16, 4, inside4)
    u4 = run_T(r4, range(-2, 3), 16, 4)
    e4 = {k: ALPHA * (b4[k] + t4[k] + r4[k] + u4[k]) for k in range(-2, 3)}
    e4 = {k: inside4(k, v) for k, v in e4.items()}

    v3 = {k: ALPHA * t3[k] + e4[k // 2] for k in range(-4, 6)}
    v3 = run_T(v3, range(-3, 5), 8, 2, inside3)
    w3 = run_T(v3, range(-2, 4), 8, 2)
    e3 = {k: inside3(k, w3[k] + ALPHA * (b3[k] + t3[k] + r3[k])) for k in range(-2, 4)}

    v2 = {k: ALPHA * t2[k] + e3[k // 2] for k in range(-4, 8)}
    v2 = run_T(v2, range(-3, 7), 4, 1, inside2)
    w2 = run_T(v2, range(-2, 6), 4, 1)
    e2 = {k: inside2(k, w2[k] + ALPHA * (b2[k] + t2[k] + r2[k])) for k in range(-2, 6)}

    inside1, inside0 = masked(8), masked(16)
    spread = {k: jnp.stack([e2[k // 2]] * 2, axis=0) for k in range(-4, 12)}
    v1 = run_T(spread, range(-2, 10), 2, 1, inside1)
    w1 = run_T(v1, range(-1, 9), 2, 1)
    even = (lanes_of((8, 128)) & 1) == 0
    extra = {}
    for ref, first in ((low_ref, -1), (high_ref, 3)):
        for pair in range(3):
            both = [ref[16 + 2 * pair + q] for q in range(2)]
            one = jnp.stack([jnp.where(even, v, pltpu.roll(v, 1, 1)) for v in both], axis=0)
            two = jnp.stack([jnp.where(even, pltpu.roll(v, 127, 1), v) for v in both], axis=0)
            for k, v in ((first + 2 * pair, one), (first + 2 * pair + 1, two)):
                extra[k] = extra[k] + v if k in extra else v
    e1 = {}
    for k in range(-1, 9):
        e1[k] = inside1(k, w1[k] + own1_ref[k + 1] + extra[k])

    def prolonged(k):
        v = e1[k // 2]
        return jnp.stack([v[0], v[0], v[1], v[1]], axis=0)

    p1 = Held(p1_ref, -1)
    wide = {k: prolonged(k) for k in range(-2, 18)}
    hold_T(wide, p1, range(-1, 17), 1, inside0)
    for k in range(16):
        v = smooth(p1[k - 1], p1[k], p1[k + 1], 1) + own0_ref[k]
        if k < 4:
            v = v + low_ref[pl.ds(4 * k, 4)]
        if k >= 12:
            v = v + high_ref[pl.ds(4 * (k - 12), 4)]
        for q in range(4):
            rows = pl.ds(q, 8, stride=4)
            pot_out[k, rows, :] = guess_ref[k, rows, :] + v[q]
    mag_out[...] = mag_ref[...]
    for q in range(4):
        rows = pl.ds(q, 8, stride=4)
        mag_out[0, rows, :] = mag_ref[0, rows, :] + low_ref[22 + q]
        mag_out[15, rows, :] = mag_ref[15, rows, :] + high_ref[22 + q]


def final_part(place, far, mine, low, high, own0, own1, mag, guess):
    smem = pl.BlockSpec(memory_space=pltpu.SMEM)
    vmem = pl.BlockSpec(memory_space=pltpu.VMEM)
    shape = lambda *s: jax.ShapeDtypeStruct(s, F32)
    return pl.pallas_call(
        final_kernel,
        out_shape=(shape(16, 32, 128), shape(16, 32, 128)),
        in_specs=[smem] + [vmem] * 8,
        out_specs=(vmem, vmem),
        scratch_shapes=[
            pltpu.VMEM((64, 8, 128), F32), pltpu.VMEM((54, 8, 128), F32),
            pltpu.VMEM((52, 8, 128), F32), pltpu.VMEM((18, 4, 8, 128), F32),
        ],
        compiler_params=pltpu.CompilerParams(vmem_limit_bytes=32 * 2**20),
        name="final",
    )(place, far, mine, low, high, own0, own1, mag, guess)


def on_device(orbitals, spin_group, occupation, potential_guess):
    dom = lax.axis_index("dom")
    flags = jnp.stack([dom > 0, dom < DOMS - 1]).astype(F32)
    core = lax.axis_index("band") % 2
    place = jnp.stack([dom, core]).astype(jnp.int32)
    parts = lax.all_to_all(density(spin_group, occupation, orbitals), "band", 0, 0)
    far, to_low, to_high, own0, own1, mag = local_part(flags, parts, potential_guess)

    rings = [
        [b * DOMS + (first + 8 * (b % 2) + i) % DOMS for i in range(RING)]
        for b in range(BANDS) for first in range(0, DOMS, RING)
    ]
    mine = lax.all_to_all(far, ("band", "dom"), 0, 0, axis_index_groups=rings)
    near_low = lax.ppermute(to_high, "dom", [(d, d + 1) for d in range(DOMS - 1)])
    near_high = lax.ppermute(to_low, "dom", [(d + 1, d) for d in range(DOMS - 1)])
    mine, near_low, near_high = lax.optimization_barrier((mine, near_low, near_high))
    other = lax.ppermute(mine, "band", [(b, b ^ 1) for b in range(BANDS)])
    return final_part(
        place, other, mine, near_low, near_high, own0, own1, mag, potential_guess
    )


def solution(mesh):
    placed = (P("band", "dom", None, None), P("band"), P("band"), P("dom", None, None))
    return jax.shard_map(
        on_device,
        mesh=mesh,
        in_specs=placed,
        out_specs=(P("dom", None, None), P("dom", None, None)),
        check_vma=False,
    )
```

```python
import functools

import jax
import jax.numpy as jnp
from jax import lax
from jax.experimental import pallas as pl
from jax.experimental.pallas import tpu as pltpu
from jax.sharding import PartitionSpec as P

DEN = 16
BANDS = 8
DOMS = 64
REACH = 7
RING = 16
ALPHA = 1.0 / 9.0
SOURCE_SCALE = 0.6
F32 = jnp.float32


def lanes_of(shape):
    return lax.broadcasted_iota(jnp.int32, shape, len(shape) - 1)


def rows_of(shape):
    return lax.broadcasted_iota(jnp.int32, shape, len(shape) - 2)


def sides_z(v, step):
    lane = lanes_of(v.shape)
    ax = v.ndim - 1
    left = jnp.where(lane >= step, pltpu.roll(v, step, ax), 0.0)
    right = jnp.where(lane < 128 - step, pltpu.roll(v, 128 - step, ax), 0.0)
    return left + right


def from_below(v, step=1):
    return jnp.where(rows_of(v.shape) >= step, pltpu.roll(v, step, v.ndim - 2), 0.0)


def from_above(v, step=1):
    return jnp.where(rows_of(v.shape) < 8 - step, pltpu.roll(v, 8 - step, v.ndim - 2), 0.0)


def sides_y(v, step):
    if v.ndim == 2:
        return from_below(v, step) + from_above(v, step)
    parts = [v[q] for q in range(v.shape[0])]
    n = len(parts)
    out = []
    for q in range(n):
        lower = parts[q - 1] if q > 0 else from_below(parts[n - 1])
        upper = parts[q + 1] if q < n - 1 else from_above(parts[0])
        out.append(lower + upper)
    return jnp.stack(out, axis=0)


def smooth(low, v, high, zstep, ystep=1):
    around = sides_y(v, ystep) + sides_z(v, zstep)
    if low is not None:
        around = around + low
    if high is not None:
        around = around + high
    return v * (1.0 / 3.0) + around * ALPHA


def pair_z(v, step):
    lane = lanes_of(v.shape)
    ax = v.ndim - 1
    other = jnp.where((lane & step) == 0, pltpu.roll(v, 128 - step, ax), pltpu.roll(v, step, ax))
    return v + other


def pair_y(v, step):
    row = rows_of(v.shape)
    ax = v.ndim - 2
    other = jnp.where((row & step) == 0, pltpu.roll(v, 8 - step, ax), pltpu.roll(v, step, ax))
    return v + other


def run_T(src, planes, zstep, ystep=1, mask=None):
    out = {}
    for k in planes:
        v = src.get(k)
        low, high = src.get(k - 1), src.get(k + 1)
        if v is None:
            edge = low if low is not None else high
            got = edge * ALPHA
        else:
            got = smooth(low, v, high, zstep, ystep)
        out[k] = got if mask is None else mask(k, got)
    return out


class Held:
    def __init__(self, ref, first):
        self.ref, self.first, self.have = ref, first, set()

    def put(self, k, value):
        self.ref[k - self.first] = value
        self.have.add(k)

    def get(self, k):
        return self.ref[k - self.first] if k in self.have else None

    def __getitem__(self, k):
        return self.ref[k - self.first]


def hold_T(src, held, planes, zstep, mask):
    for k in planes:
        v = src.get(k)
        low, high = src.get(k - 1), src.get(k + 1)
        if v is None:
            got = (low if low is not None else high) * ALPHA
        else:
            got = smooth(low, v, high, zstep)
        held.put(k, mask(k, got))


def refine_matrix(rows, columns):
    row = lax.broadcasted_iota(jnp.int32, (rows, columns), 0)
    col = lax.broadcasted_iota(jnp.int32, (rows, columns), 1)
    cell, spin = row & 63, row >> 6
    fine, half = col & 127, col >> 7
    own = fine >> 1
    other = jnp.where((fine & 1) == 0, own - 1, own + 1)
    value = jnp.where(cell == own, 0.75, jnp.where(cell == other, 0.25, 0.0))
    return jnp.where((spin == 1) & (half == 1), -value, value)


def refine_y(pair):
    first, second = pair
    return jnp.stack(
        [
            0.75 * first + 0.25 * from_below(second),
            0.75 * first + 0.25 * second,
            0.75 * second + 0.25 * first,
            0.75 * second + 0.25 * from_above(first),
        ],
        axis=0,
    )


def refine_x(coarse, k):
    i = k // 2
    other = i - 1 if k % 2 == 0 else i + 1
    total = None
    for j, factor in ((i, 0.75), (other, 0.25)):
        if 0 <= j < 8:
            term = factor * coarse[j]
            total = term if total is None else total + term
    return total


def refine_z(coarse, columns):
    return jnp.dot(
        coarse, refine_matrix(coarse.shape[1], columns),
        precision=lax.Precision.HIGHEST, preferred_element_type=F32,
    )


def masks(dom):
    low_flag = jnp.where(dom > 0, 1.0, 0.0).astype(F32)
    high_flag = jnp.where(dom < DOMS - 1, 1.0, 0.0).astype(F32)

    def masked(last):
        def mask(k, v):
            if k < 0:
                return v * low_flag
            if k > last:
                return v * high_flag
            return v
        return mask

    return masked(15), masked(7)


def guess_planes(guess_ref):
    def guess(k):
        if not 0 <= k < 16:
            return None
        return jnp.stack([guess_ref[k, pl.ds(q, 8, stride=4), :] for q in range(4)], axis=0)
    return guess


def restricted(r, k):
    total = None
    for fine in (2 * k, 2 * k + 1):
        v = r.get(fine)
        if v is not None:
            total = v if total is None else total + v
    total = jnp.stack([total[0] + total[1], total[2] + total[3]], axis=0)
    return 0.5 * pair_z(total, 1)


def geometric(b, t, r, k, zstep):
    low, v, high = r.get(k - 1), r.get(k), r.get(k + 1)
    if v is None:
        last = (low if low is not None else high) * ALPHA
    else:
        last = smooth(low, v, high, zstep)
    for term in (r.get(k), t.get(k), b.get(k)):
        if term is not None:
            last = last + term
    return last * ALPHA


def copy_all(source, target, count, sems):
    copies = [pltpu.make_async_copy(source, target.at[i], sems.at[i]) for i in range(count)]
    for copy in copies:
        copy.start()
    return copies


def density_kernel(
    spin_hbm, occ_hbm, orb_hbm, part_hbm, spin_ref, occ_ref, orb_ref, own_ref, sems,
):
    loads = [
        pltpu.make_async_copy(spin_hbm, spin_ref, sems.at[8]),
        pltpu.make_async_copy(occ_hbm, occ_ref, sems.at[9]),
    ]
    loads += [pltpu.make_async_copy(orb_hbm.at[k], orb_ref.at[k], sems.at[k]) for k in range(8)]
    for load in loads:
        load.start()
    loads[0].wait()
    loads[1].wait()
    ups, downs = [0.0] * 8, [0.0] * 8
    for k in range(8):
        weight = occ_ref[k].astype(F32) * (0.125 / DEN)
        up = spin_ref[k] == 0
        up, down = jnp.where(up, weight, 0.0), jnp.where(up, 0.0, weight)
        loads[2 + k].wait()
        for x in range(8):
            square = orb_ref[k, x] * orb_ref[k, x]
            ups[x] = ups[x] + up * square
            downs[x] = downs[x] + down * square
    for x in range(8):
        own_ref[pl.ds(16 * x, 16), :] = jnp.concatenate([ups[x], downs[x]], axis=-1)
    for copy in copy_all(own_ref, part_hbm, BANDS, sems):
        copy.wait()


def density(spin_group, occupation, orbitals):
    hbm = pl.BlockSpec(memory_space=pltpu.HBM)
    return pl.pallas_call(
        density_kernel,
        out_shape=jax.ShapeDtypeStruct((BANDS, 128, 128), F32),
        in_specs=[hbm] * 3,
        out_specs=hbm,
        scratch_shapes=[
            pltpu.SMEM((8,), jnp.int32), pltpu.SMEM((8,), jnp.int32),
            pltpu.VMEM((8, 8, 16, 64), F32), pltpu.VMEM((128, 128), F32),
            pltpu.SemaphoreType.DMA((10,)),
        ],
        compiler_params=pltpu.CompilerParams(vmem_limit_bytes=60 * 2**20),
        name="density",
    )(spin_group, occupation, orbitals)


def guess_kernel(guess_ref, out_ref):
    inside0, _ = masks(lax.axis_index("dom"))
    guess = guess_planes(guess_ref)
    for k in range(-1, 17):
        v, low, high = guess(k), guess(k - 1), guess(k + 1)
        around = None
        if v is not None:
            around = sides_y(v, 1) + sides_z(v, 1)
        for side in (low, high):
            if side is not None:
                around = side if around is None else around + side
        out_ref[k + 1] = inside0(k, around - 6.0 * v if v is not None else around)


def guess_part(guess):
    vmem = pl.BlockSpec(memory_space=pltpu.VMEM)
    return pl.pallas_call(
        guess_kernel,
        out_shape=jax.ShapeDtypeStruct((18, 4, 8, 128), F32),
        in_specs=[vmem],
        out_specs=vmem,
        compiler_params=pltpu.CompilerParams(vmem_limit_bytes=32 * 2**20),
        cost_estimate=pl.CostEstimate(flops=10**6, bytes_accessed=2**19, transcendentals=0),
        name="guess",
    )(guess)


def far_kernel(
    part_ref, applied_ref, far_hbm, minus_ref, d_ref, t_ref, r_ref, b1_ref, t1_ref, r1_ref,
    sum_ref, wide_ref, far_ref, sems,
):
    inside0, inside1 = masks(lax.axis_index("dom"))
    for x in range(8):
        rows = pl.ds(16 * x, 16)
        total = part_ref[0, rows, :]
        for band in range(1, BANDS):
            total = total + part_ref[band, rows, :]
        sum_ref[rows, :] = total
    wide = refine_z(sum_ref[...], 256)
    wide_ref[...] = wide[:, :128]
    minus_ref[...] = wide[:, 128:]
    plus = []
    for x in range(8):
        pair = [wide_ref[pl.ds(16 * x + p, 8, stride=2), :] for p in range(2)]
        plus.append(SOURCE_SCALE * refine_y(pair))
    d, t, r = Held(d_ref, -1), Held(t_ref, -2), Held(r_ref, -3)
    for k in range(-1, 17):
        d.put(k, inside0(k, refine_x(plus, k)) + applied_ref[k + 1])
    hold_T(d, t, range(-2, 18), 1, inside0)
    hold_T(t, r, range(-3, 19), 1, inside0)
    b1, t1, r1 = Held(b1_ref, -2), Held(t1_ref, -3), Held(r1_ref, -4)
    for k in range(-2, 10):
        b1.put(k, restricted(r, k))
    hold_T(b1, t1, range(-3, 11), 2, inside1)
    hold_T(t1, r1, range(-4, 12), 2, inside1)
    lane = lanes_of((8, 128)) & 3
    for group in range(2):
        packed = None
        for p in range(4):
            k = 4 * group + p - 2
            v = r1[2 * k] + r1[2 * k + 1]
            v = 0.5 * pair_z(v[0] + v[1], 2)
            packed = v if packed is None else jnp.where(lane == p, v, packed)
        far_ref[pl.ds(8 * group, 8), :] = packed
    for copy in copy_all(far_ref, far_hbm, RING, sems):
        copy.wait()


def far_part(parts, applied):
    vmem = pl.BlockSpec(memory_space=pltpu.VMEM)
    shape = lambda *s: jax.ShapeDtypeStruct(s, F32)
    return pl.pallas_call(
        far_kernel,
        out_shape=(
            shape(RING, 16, 128), shape(128, 128),
            shape(18, 4, 8, 128), shape(20, 4, 8, 128), shape(22, 4, 8, 128),
            shape(12, 2, 8, 128), shape(14, 2, 8, 128), shape(16, 2, 8, 128),
        ),
        in_specs=[vmem, vmem],
        out_specs=(pl.BlockSpec(memory_space=pltpu.HBM),) + (vmem,) * 7,
        scratch_shapes=[
            pltpu.VMEM((128, 128), F32), pltpu.VMEM((128, 128), F32),
            pltpu.VMEM((16, 128), F32), pltpu.SemaphoreType.DMA((RING,)),
        ],
        compiler_params=pltpu.CompilerParams(vmem_limit_bytes=32 * 2**20),
        name="far",
    )(parts, applied)


class Given(Held):
    def __init__(self, ref, first):
        super().__init__(ref, first)
        self.have = set(range(first, first + ref.shape[0]))


def near_kernel(
    guess_ref, minus_ref, d_ref, t_ref, r_ref, b1_ref, t1_ref, r1_ref,
    low_ref, high_ref, own0_ref, own1_ref, mag_ref,
):
    d, t, r = Given(d_ref, -1), Given(t_ref, -2), Given(r_ref, -3)
    b1, t1, r1 = Given(b1_ref, -2), Given(t1_ref, -3), Given(r1_ref, -4)
    minus = []
    for x in range(8):
        minus.append(refine_y([minus_ref[pl.ds(16 * x + p, 8, stride=2), :] for p in range(2)]))
    guess = guess_planes(guess_ref)
    for k in range(4):
        low_ref[pl.ds(4 * k, 4)] = geometric(d, t, r, k - 4, 1)
        high_ref[pl.ds(4 * k, 4)] = geometric(d, t, r, k + 16, 1)
    low_ref[pl.ds(22, 4)] = refine_x(minus, -1)
    high_ref[pl.ds(22, 4)] = refine_x(minus, 16)
    f1 = {k: geometric(b1, t1, r1, k, 2) for k in range(-5, 13)}
    for k in range(-1, 9):
        own1_ref[k + 1] = f1[k]
    even = (lanes_of((8, 128)) & 1) == 0
    for pair in range(3):
        for q in range(2):
            low_ref[16 + 2 * pair + q] = jnp.where(even, f1[2 * pair - 5][q], f1[2 * pair - 4][q])
            high_ref[16 + 2 * pair + q] = jnp.where(even, f1[2 * pair + 7][q], f1[2 * pair + 8][q])
    for k in range(16):
        own0_ref[k] = geometric(d, t, r, k, 1) + guess(k)
        mag_ref[k] = refine_x(minus, k)


def near_part(guess, *held):
    vmem = pl.BlockSpec(memory_space=pltpu.VMEM)
    shape = lambda *s: jax.ShapeDtypeStruct(s, F32)
    return pl.pallas_call(
        near_kernel,
        out_shape=(
            shape(26, 8, 128), shape(26, 8, 128),
            shape(16, 4, 8, 128), shape(10, 2, 8, 128), shape(16, 4, 8, 128),
        ),
        in_specs=[vmem] * 8,
        out_specs=(vmem,) * 5,
        compiler_params=pltpu.CompilerParams(vmem_limit_bytes=32 * 2**20),
        cost_estimate=pl.CostEstimate(flops=10**6, bytes_accessed=2**20, transcendentals=0),
        name="near",
    )(guess, *held)


def edge_kernel(low_ref, high_ref, own0_ref, own1_ref, mag_ref, base0_ref, base1_ref, mag_out):
    even = (lanes_of((8, 128)) & 1) == 0
    extra = {}
    for ref, first in ((low_ref, -1), (high_ref, 3)):
        for pair in range(3):
            both = [ref[16 + 2 * pair + q] for q in range(2)]
            one = jnp.stack([jnp.where(even, v, pltpu.roll(v, 1, 1)) for v in both], axis=0)
            two = jnp.stack([jnp.where(even, pltpu.roll(v, 127, 1), v) for v in both], axis=0)
            for k, v in ((first + 2 * pair, one), (first + 2 * pair + 1, two)):
                extra[k] = extra[k] + v if k in extra else v
    for k in range(-1, 9):
        base1_ref[k + 1] = own1_ref[k + 1] + extra[k]
    for k in range(16):
        v, mag = own0_ref[k], mag_ref[k]
        if k < 4:
            v = v + low_ref[pl.ds(4 * k, 4)]
        if k >= 12:
            v = v + high_ref[pl.ds(4 * (k - 12), 4)]
        base0_ref[k] = v
        if k == 0:
            mag = mag + low_ref[pl.ds(22, 4)]
        if k == 15:
            mag = mag + high_ref[pl.ds(22, 4)]
        for q in range(4):
            mag_out[k, pl.ds(q, 8, stride=4), :] = mag[q]


def edge_part(low, high, own0, own1, mag):
    vmem = pl.BlockSpec(memory_space=pltpu.VMEM)
    shape = lambda *s: jax.ShapeDtypeStruct(s, F32)
    return pl.pallas_call(
        edge_kernel,
        out_shape=(shape(16, 4, 8, 128), shape(10, 2, 8, 128), shape(16, 32, 128)),
        in_specs=[vmem] * 5,
        out_specs=(vmem,) * 3,
        compiler_params=pltpu.CompilerParams(vmem_limit_bytes=32 * 2**20),
        name="edge",
    )(low, high, own0, own1, mag)


def final_kernel(
    far_ref, mine_ref, base0_ref, base1_ref, pot_out,
    b2_ref, t2_ref, r2_ref, p1_ref,
):
    dom = lax.axis_index("dom")

    def masked(count):
        first, last = -dom * count, (DOMS - dom) * count
        def mask(k, v):
            if 0 <= k < count:
                return v
            ok = (k >= first) & (k < last)
            return jnp.where(ok, v, 0.0)
        return mask

    lane = lanes_of((8, 128)) & 3
    core = lax.axis_index("band") % 2
    ring, spot = dom // RING, dom % RING
    even_first = RING * ring
    odd_first = even_first + jnp.where(spot >= RING // 2, RING // 2, -(RING // 2))

    def vector(i, half):
        wanted = dom - REACH + i
        at = wanted - even_first
        in_even = (at >= 0) & (at < RING)
        at = jnp.clip(jnp.where(in_even, at, wanted - odd_first), 0, RING - 1)
        rows = pl.ds(8 * half, 8)
        held = in_even == (core == 0)
        v = jnp.where(held, mine_ref[at, rows, :], far_ref[at, rows, :])
        return jnp.where((wanted >= 0) & (wanted < DOMS), v, 0.0)

    b2, t2, r2 = Held(b2_ref, -30), Held(t2_ref, -25), Held(r2_ref, -24)
    for i in range(16):
        packed = None
        for part in ((i, 0), (i - 1, 1)):
            if 0 <= part[0] < 15:
                v = vector(*part)
                packed = v if packed is None else packed + v
        for p in range(4):
            only = jnp.where(lane == p, packed, 0.0)
            only = only + pltpu.roll(only, 1 if p % 2 == 0 else 127, 1)
            only = only + pltpu.roll(only, 2 if p < 2 else 126, 1)
            b2.put(4 * (i - REACH) - 2 + p, only)
    inside2, inside3, inside4 = masked(4), masked(2), masked(1)
    hold_T(b2, t2, range(-25, 29), 4, inside2)
    hold_T(t2, r2, range(-24, 28), 4, lambda k, v: v)

    b3 = {}
    for k in range(-12, 14):
        v = pair_y(pair_z(r2[2 * k] + r2[2 * k + 1], 4), 1)
        b3[k] = inside3(k, 0.5 * v)
    t3 = run_T(b3, range(-11, 13), 8, 2, inside3)
    r3 = run_T(t3, range(-10, 12), 8, 2)

    b4 = {}
    for k in range(-5, 6):
        v = pair_y(pair_z(r3[2 * k] + r3[2 * k + 1], 8), 2)
        b4[k] = inside4(k, 0.5 * v)
    t4 = run_T(b4, range(-4, 5), 16, 4, inside4)
    r4 = run_T(t4, range(-3, 4), 16, 4, inside4)
    u4 = run_T(r4, range(-2, 3), 16, 4)
    e4 = {k: ALPHA * (b4[k] + t4[k] + r4[k] + u4[k]) for k in range(-2, 3)}
    e4 = {k: inside4(k, v) for k, v in e4.items()}

    v3 = {k: ALPHA * t3[k] + e4[k // 2] for k in range(-4, 6)}
    v3 = run_T(v3, range(-3, 5), 8, 2, inside3)
    w3 = run_T(v3, range(-2, 4), 8, 2)
    e3 = {k: inside3(k, w3[k] + ALPHA * (b3[k] + t3[k] + r3[k])) for k in range(-2, 4)}

    v2 = {k: ALPHA * t2[k] + e3[k // 2] for k in range(-4, 8)}
    v2 = run_T(v2, range(-3, 7), 4, 1, inside2)
    w2 = run_T(v2, range(-2, 6), 4, 1)
    e2 = {k: inside2(k, w2[k] + ALPHA * (b2[k] + t2[k] + r2[k])) for k in range(-2, 6)}

    inside1, inside0 = masked(8), masked(16)
    spread = {k: jnp.stack([e2[k // 2]] * 2, axis=0) for k in range(-4, 12)}
    v1 = run_T(spread, range(-2, 10), 2, 1, inside1)
    w1 = run_T(v1, range(-1, 9), 2, 1)
    e1 = {k: inside1(k, w1[k] + base1_ref[k + 1]) for k in range(-1, 9)}

    def prolonged(k):
        v = e1[k // 2]
        return jnp.stack([v[0], v[0], v[1], v[1]], axis=0)

    p1 = Held(p1_ref, -1)
    wide = {k: prolonged(k) for k in range(-2, 18)}
    hold_T(wide, p1, range(-1, 17), 1, inside0)
    for k in range(16):
        v = smooth(p1[k - 1], p1[k], p1[k + 1], 1) + base0_ref[k]
        for q in range(4):
            pot_out[k, pl.ds(q, 8, stride=4), :] = v[q]


def final_part(far, mine, base0, base1):
    vmem = pl.BlockSpec(memory_space=pltpu.VMEM)
    return pl.pallas_call(
        final_kernel,
        out_shape=jax.ShapeDtypeStruct((16, 32, 128), F32),
        in_specs=[vmem] * 4,
        out_specs=vmem,
        scratch_shapes=[
            pltpu.VMEM((64, 8, 128), F32), pltpu.VMEM((54, 8, 128), F32),
            pltpu.VMEM((52, 8, 128), F32), pltpu.VMEM((18, 4, 8, 128), F32),
        ],
        compiler_params=pltpu.CompilerParams(vmem_limit_bytes=32 * 2**20),
        name="final",
    )(far, mine, base0, base1)


def on_device(orbitals, spin_group, occupation, potential_guess):
    applied = guess_part(potential_guess)
    parts = lax.all_to_all(density(spin_group, occupation, orbitals), "band", 0, 0)
    far, *held = far_part(parts, applied)
    rings = [
        [b * DOMS + (first + 8 * (b % 2) + i) % DOMS for i in range(RING)]
        for b in range(BANDS) for first in range(0, DOMS, RING)
    ]
    mine = lax.all_to_all(far, ("band", "dom"), 0, 0, axis_index_groups=rings)

    to_low, to_high, own0, own1, mag = near_part(potential_guess, *held)
    near_low = lax.ppermute(to_high, "dom", [(d, d + 1) for d in range(DOMS - 1)])
    near_high = lax.ppermute(to_low, "dom", [(d + 1, d) for d in range(DOMS - 1)])

    mine, near_low, near_high = lax.optimization_barrier((mine, near_low, near_high))
    other = lax.ppermute(mine, "band", [(b, b ^ 1) for b in range(BANDS)])
    base0, base1, magnetization = edge_part(near_low, near_high, own0, own1, mag)
    return final_part(other, mine, base0, base1), magnetization


def solution(mesh):
    placed = (P("band", "dom", None, None), P("band"), P("band"), P("dom", None, None))
    return jax.shard_map(
        on_device,
        mesh=mesh,
        in_specs=placed,
        out_specs=(P("dom", None, None), P("dom", None, None)),
        check_vma=False,
    )
```

```python
import functools

import jax
import jax.numpy as jnp
from jax import lax
from jax.experimental import pallas as pl
from jax.experimental.pallas import tpu as pltpu
from jax.sharding import PartitionSpec as P

DEN = 16
BANDS = 8
DOMS = 64
REACH = 7
RING = 16
ROWS = 96
ROOT = 11
ALPHA = 1.0 / 9.0
SOURCE_SCALE = 0.6
F32 = jnp.float32


def lanes_of(shape):
    return lax.broadcasted_iota(jnp.int32, shape, len(shape) - 1)


def rows_of(shape):
    return lax.broadcasted_iota(jnp.int32, shape, len(shape) - 2)


def sides_z(v, step):
    lane = lanes_of(v.shape)
    ax = v.ndim - 1
    left = jnp.where(lane >= step, pltpu.roll(v, step, ax), 0.0)
    right = jnp.where(lane < 128 - step, pltpu.roll(v, 128 - step, ax), 0.0)
    return left + right


def from_below(v, step=1):
    return jnp.where(rows_of(v.shape) >= step, pltpu.roll(v, step, v.ndim - 2), 0.0)


def from_above(v, step=1):
    return jnp.where(rows_of(v.shape) < 8 - step, pltpu.roll(v, 8 - step, v.ndim - 2), 0.0)


def sides_y(v, step):
    if v.ndim == 2:
        return from_below(v, step) + from_above(v, step)
    parts = [v[q] for q in range(v.shape[0])]
    n = len(parts)
    out = []
    for q in range(n):
        lower = parts[q - 1] if q > 0 else from_below(parts[n - 1])
        upper = parts[q + 1] if q < n - 1 else from_above(parts[0])
        out.append(lower + upper)
    return jnp.stack(out, axis=0)


def smooth(low, v, high, zstep, ystep=1):
    around = sides_y(v, ystep) + sides_z(v, zstep)
    if low is not None:
        around = around + low
    if high is not None:
        around = around + high
    return v * (1.0 / 3.0) + around * ALPHA


def pair_z(v, step):
    lane = lanes_of(v.shape)
    ax = v.ndim - 1
    other = jnp.where((lane & step) == 0, pltpu.roll(v, 128 - step, ax), pltpu.roll(v, step, ax))
    return v + other


def pair_y(v, step):
    row = rows_of(v.shape)
    ax = v.ndim - 2
    other = jnp.where((row & step) == 0, pltpu.roll(v, 8 - step, ax), pltpu.roll(v, step, ax))
    return v + other


def run_T(src, planes, zstep, ystep=1, mask=None):
    out = {}
    for k in planes:
        v = src.get(k)
        low, high = src.get(k - 1), src.get(k + 1)
        if v is None:
            edge = low if low is not None else high
            got = edge * ALPHA
        else:
            got = smooth(low, v, high, zstep, ystep)
        out[k] = got if mask is None else mask(k, got)
    return out


class Held:
    def __init__(self, ref, first):
        self.ref, self.first, self.have = ref, first, set()

    def put(self, k, value):
        self.ref[k - self.first] = value
        self.have.add(k)

    def get(self, k):
        return self.ref[k - self.first] if k in self.have else None

    def __getitem__(self, k):
        return self.ref[k - self.first]


def hold_T(src, held, planes, zstep, mask):
    for k in planes:
        v = src.get(k)
        low, high = src.get(k - 1), src.get(k + 1)
        if v is None:
            got = (low if low is not None else high) * ALPHA
        else:
            got = smooth(low, v, high, zstep)
        held.put(k, mask(k, got))


def refine_z(coarse):
    row = lax.broadcasted_iota(jnp.int32, (128, 256), 0)
    col = lax.broadcasted_iota(jnp.int32, (128, 256), 1)
    own = col >> 1
    other = jnp.where((col & 1) == 0, own - 1, own + 1)
    inside = (other >> 6) == (col >> 7)
    matrix = jnp.where(row == own, 0.75, jnp.where((row == other) & inside, 0.25, 0.0))
    return jnp.dot(
        coarse, matrix, precision=lax.Precision.HIGHEST, preferred_element_type=F32
    )


def refine_y(pair):
    first, second = pair
    return jnp.stack(
        [
            0.75 * first + 0.25 * from_below(second),
            0.75 * first + 0.25 * second,
            0.75 * second + 0.25 * first,
            0.75 * second + 0.25 * from_above(first),
        ],
        axis=0,
    )


def refine_x(coarse, k):
    i = k // 2
    other = i - 1 if k % 2 == 0 else i + 1
    total = None
    for j, factor in ((i, 0.75), (other, 0.25)):
        if 0 <= j < 8:
            term = factor * coarse[j]
            total = term if total is None else total + term
    return total


def masks(dom):
    low_flag = jnp.where(dom > 0, 1.0, 0.0).astype(F32)
    high_flag = jnp.where(dom < DOMS - 1, 1.0, 0.0).astype(F32)

    def masked(last):
        def mask(k, v):
            if k < 0:
                return v * low_flag
            if k > last:
                return v * high_flag
            return v
        return mask

    return masked(15), masked(7)


def guess_planes(guess_ref):
    def guess(k):
        if not 0 <= k < 16:
            return None
        return jnp.stack([guess_ref[k, pl.ds(q, 8, stride=4), :] for q in range(4)], axis=0)
    return guess


def restricted(r, k):
    total = None
    for fine in (2 * k, 2 * k + 1):
        v = r.get(fine)
        if v is not None:
            total = v if total is None else total + v
    total = jnp.stack([total[0] + total[1], total[2] + total[3]], axis=0)
    return 0.5 * pair_z(total, 1)


def geometric(b, t, r, k, zstep):
    low, v, high = r.get(k - 1), r.get(k), r.get(k + 1)
    if v is None:
        last = (low if low is not None else high) * ALPHA
    else:
        last = smooth(low, v, high, zstep)
    for term in (r.get(k), t.get(k), b.get(k)):
        if term is not None:
            last = last + term
    return last * ALPHA


def copy_all(source, target, count, sems):
    copies = [pltpu.make_async_copy(source, target.at[i], sems.at[i]) for i in range(count)]
    for copy in copies:
        copy.start()
    return copies


def density_kernel(
    spin_hbm, occ_hbm, orb_hbm, part_hbm, spin_ref, occ_ref, orb_ref, own_ref, sems,
):
    loads = [
        pltpu.make_async_copy(spin_hbm, spin_ref, sems.at[8]),
        pltpu.make_async_copy(occ_hbm, occ_ref, sems.at[9]),
    ]
    loads += [pltpu.make_async_copy(orb_hbm.at[k], orb_ref.at[k], sems.at[k]) for k in range(8)]
    for load in loads:
        load.start()
    loads[0].wait()
    loads[1].wait()
    ups, downs = [0.0] * 8, [0.0] * 8
    for k in range(8):
        weight = occ_ref[k].astype(F32) * (0.125 / DEN)
        up = spin_ref[k] == 0
        up, down = jnp.where(up, weight, 0.0), jnp.where(up, 0.0, weight)
        loads[2 + k].wait()
        for x in range(8):
            square = orb_ref[k, x] * orb_ref[k, x]
            ups[x] = ups[x] + up * square
            downs[x] = downs[x] + down * square
    for core in range(2):
        for i in range(4):
            own_ref[core, pl.ds(16 * i, 16), :] = jnp.concatenate(
                [ups[i] + downs[i], ups[i + 4] + downs[i + 4]], axis=-1
            )
        for i in range(2):
            one, two = 4 * core + i, 4 * core + i + 2
            own_ref[core, pl.ds(64 + 16 * i, 16), :] = jnp.concatenate(
                [ups[one] - downs[one], ups[two] - downs[two]], axis=-1
            )
    copies = [
        pltpu.make_async_copy(own_ref.at[b % 2], part_hbm.at[b], sems.at[b]) for b in range(BANDS)
    ]
    for copy in copies:
        copy.start()
    for copy in copies:
        copy.wait()


def density(spin_group, occupation, orbitals):
    hbm = pl.BlockSpec(memory_space=pltpu.HBM)
    return pl.pallas_call(
        density_kernel,
        out_shape=jax.ShapeDtypeStruct((BANDS, ROWS, 128), F32),
        in_specs=[hbm] * 3,
        out_specs=hbm,
        scratch_shapes=[
            pltpu.SMEM((8,), jnp.int32), pltpu.SMEM((8,), jnp.int32),
            pltpu.VMEM((8, 8, 16, 64), F32), pltpu.VMEM((2, ROWS, 128), F32),
            pltpu.SemaphoreType.DMA((10,)),
        ],
        compiler_params=pltpu.CompilerParams(vmem_limit_bytes=60 * 2**20),
        name="density",
    )(spin_group, occupation, orbitals)


def guess_kernel(guess_ref, out_ref):
    inside0, _ = masks(lax.axis_index("dom"))
    guess = guess_planes(guess_ref)
    for k in range(-1, 17):
        v, low, high = guess(k), guess(k - 1), guess(k + 1)
        around = None
        if v is not None:
            around = sides_y(v, 1) + sides_z(v, 1)
        for side in (low, high):
            if side is not None:
                around = side if around is None else around + side
        out_ref[k + 1] = inside0(k, around - 6.0 * v if v is not None else around)


def guess_part(guess):
    vmem = pl.BlockSpec(memory_space=pltpu.VMEM)
    return pl.pallas_call(
        guess_kernel,
        out_shape=jax.ShapeDtypeStruct((18, 4, 8, 128), F32),
        in_specs=[vmem],
        out_specs=vmem,
        compiler_params=pltpu.CompilerParams(vmem_limit_bytes=32 * 2**20),
        cost_estimate=pl.CostEstimate(flops=10**6, bytes_accessed=2**19, transcendentals=0),
        name="guess",
    )(guess)


def far_kernel(
    part_ref, applied_ref, far_hbm, halo_ref, minus_ref,
    d_ref, t_ref, r_ref, b1_ref, t1_ref, r1_ref, sum_ref, wide_ref, far_ref, sems,
):
    inside0, inside1 = masks(lax.axis_index("dom"))
    for i in range(ROWS // 16):
        rows = pl.ds(16 * i, 16)
        total = part_ref[0, rows, :]
        for band in range(1, BANDS):
            total = total + part_ref[band, rows, :]
        sum_ref[rows, :] = total
    wide = refine_z(sum_ref[...])
    for half in range(2):
        wide_ref[half] = wide[:64, 128 * half:128 * half + 128]
        minus_ref[pl.ds(32 * half, 32), :] = wide[64:, 128 * half:128 * half + 128]
    plus = []
    for x in range(8):
        start = 16 * (x % 4)
        pair = [wide_ref[x // 4, pl.ds(start + p, 8, stride=2), :] for p in range(2)]
        plus.append(SOURCE_SCALE * refine_y(pair))
    d, t, r = Held(d_ref, -1), Held(t_ref, -2), Held(r_ref, -3)
    for k in range(-1, 17):
        d.put(k, inside0(k, refine_x(plus, k)) + applied_ref[k + 1])
    hold_T(d, t, range(-2, 18), 1, inside0)
    hold_T(t, r, range(-3, 19), 1, inside0)
    b1, t1, r1 = Held(b1_ref, -2), Held(t1_ref, -3), Held(r1_ref, -4)
    for k in range(-2, 10):
        b1.put(k, restricted(r, k))
    hold_T(b1, t1, range(-3, 11), 2, inside1)
    hold_T(t1, r1, range(-4, 12), 2, inside1)
    lane = lanes_of((8, 128)) & 3
    for group in range(2):
        packed = None
        for p in range(4):
            k = 4 * group + p - 2
            v = r1[2 * k] + r1[2 * k + 1]
            v = 0.5 * pair_z(v[0] + v[1], 2)
            packed = v if packed is None else jnp.where(lane == p, v, packed)
        far_ref[pl.ds(8 * group, 8), :] = packed
    copies = copy_all(far_ref, far_hbm, RING, sems)

    core = lax.axis_index("band") % 2
    even = (lanes_of((8, 128)) & 1) == 0

    def edges(first0, first1, plane):
        for k in range(4):
            halo_ref[pl.ds(4 * k, 4)] = geometric(d, t, r, first0 + k, 1)
        for pair in range(3):
            one = geometric(b1, t1, r1, first1 + 2 * pair, 2)
            two = geometric(b1, t1, r1, first1 + 2 * pair + 1, 2)
            for q in range(2):
                halo_ref[16 + 2 * pair + q] = jnp.where(even, one[q], two[q])
        start = 32 * (plane // 2) + 16 * (plane % 2)
        pair = [minus_ref[pl.ds(start + p, 8, stride=2), :] for p in range(2)]
        halo_ref[pl.ds(22, 4)] = 0.25 * refine_y(pair)

    @pl.when(core == 0)
    def _():
        edges(-4, -5, 0)

    @pl.when(core == 1)
    def _():
        edges(16, 7, 3)

    for copy in copies:
        copy.wait()


def far_part(parts, applied):
    vmem = pl.BlockSpec(memory_space=pltpu.VMEM)
    shape = lambda *s: jax.ShapeDtypeStruct(s, F32)
    return pl.pallas_call(
        far_kernel,
        out_shape=(
            shape(RING, 16, 128), shape(26, 8, 128), shape(64, 128),
            shape(18, 4, 8, 128), shape(20, 4, 8, 128), shape(22, 4, 8, 128),
            shape(12, 2, 8, 128), shape(14, 2, 8, 128), shape(16, 2, 8, 128),
        ),
        in_specs=[vmem, vmem],
        out_specs=(pl.BlockSpec(memory_space=pltpu.HBM),) + (vmem,) * 8,
        scratch_shapes=[
            pltpu.VMEM((ROWS, 128), F32), pltpu.VMEM((2, 64, 128), F32),
            pltpu.VMEM((16, 128), F32), pltpu.SemaphoreType.DMA((RING,)),
        ],
        compiler_params=pltpu.CompilerParams(vmem_limit_bytes=32 * 2**20),
        name="far",
    )(parts, applied)


class Given(Held):
    def __init__(self, ref, first):
        super().__init__(ref, first)
        self.have = set(range(first, first + ref.shape[0]))


def near_kernel(
    guess_ref, d_ref, t_ref, r_ref, b1_ref, t1_ref, r1_ref, own0_ref, own1_ref,
):
    d, t, r = Given(d_ref, -1), Given(t_ref, -2), Given(r_ref, -3)
    b1, t1, r1 = Given(b1_ref, -2), Given(t1_ref, -3), Given(r1_ref, -4)
    guess = guess_planes(guess_ref)
    for k in range(-1, 9):
        own1_ref[k + 1] = geometric(b1, t1, r1, k, 2)
    for k in range(16):
        own0_ref[k] = geometric(d, t, r, k, 1) + guess(k)


def near_part(guess, *held):
    vmem = pl.BlockSpec(memory_space=pltpu.VMEM)
    shape = lambda *s: jax.ShapeDtypeStruct(s, F32)
    return pl.pallas_call(
        near_kernel,
        out_shape=(shape(16, 4, 8, 128), shape(10, 2, 8, 128)),
        in_specs=[vmem] * 7,
        out_specs=(vmem,) * 2,
        compiler_params=pltpu.CompilerParams(vmem_limit_bytes=32 * 2**20),
        cost_estimate=pl.CostEstimate(flops=10**6, bytes_accessed=2**20, transcendentals=0),
        name="near",
    )(guess, *held)


def ring_place():
    dom, core = lax.axis_index("dom"), lax.axis_index("band") % 2
    ring, spot = dom // RING, dom % RING
    aligned = RING * ring
    shifted = aligned + jnp.where(spot >= RING // 2, RING // 2, -(RING // 2))
    return dom, core, spot, jnp.where(core == 0, aligned, shifted)


def ring_slot(at, core):
    first = jnp.where(core == 0, ROOT, ROOT - RING // 2)
    return (at - first + RING) % RING


def pack_kernel(mine_ref, halo_ref, minus_ref, out_ref):
    _, core, spot, _ = ring_place()
    start = jnp.where((spot < RING // 2) == (core == 0), RING // 2, 0)
    for i in range(RING // 2):
        slot = ring_slot(start + i, core)
        for half in range(2):
            out_ref[34 + 2 * i + half] = mine_ref[slot, pl.ds(8 * half, 8), :]
    out_ref[pl.ds(0, 26)] = halo_ref[...]
    for j in range(4):
        for p in range(2):
            out_ref[26 + 2 * j + p] = minus_ref[pl.ds(16 * j + p, 8, stride=2), :]


def pack(mine, halo, minus):
    vmem = pl.BlockSpec(memory_space=pltpu.VMEM)
    return pl.pallas_call(
        pack_kernel,
        out_shape=jax.ShapeDtypeStruct((50, 8, 128), F32),
        in_specs=[vmem] * 3,
        out_specs=vmem,
        compiler_params=pltpu.CompilerParams(vmem_limit_bytes=32 * 2**20),
        name="pack",
    )(mine, halo, minus)


def final_kernel(
    mine_ref, swapped_ref, halo_ref, minus_ref, own0_ref, own1_ref, pot_hbm, mag_hbm,
    b2_ref, t2_ref, r2_ref, p1_ref, pot_ref, mag_ref, sems,
):
    dom, core, spot, own_first = ring_place()
    lower = core == 0

    def high(i):
        return jnp.where(lower, halo_ref[i], swapped_ref[i])

    def low(i):
        return jnp.where(lower, swapped_ref[i], halo_ref[i])

    minus = []
    for x in range(8):
        j = x % 4
        pair = []
        for p in range(2):
            own = minus_ref[pl.ds(16 * j + p, 8, stride=2), :]
            pair.append(jnp.where(lower == (x < 4), own, swapped_ref[26 + 2 * j + p]))
        minus.append(refine_y(pair))
    for k in range(16):
        mag = refine_x(minus, k)
        if k == 0:
            mag = mag + low(pl.ds(22, 4))
        if k == 15:
            mag = mag + high(pl.ds(22, 4))
        for q in range(4):
            mag_ref[k, pl.ds(q, 8, stride=4), :] = mag[q]
    copies = [pltpu.make_async_copy(mag_ref, mag_hbm, sems.at[4])]
    copies[0].start()

    def masked(count):
        first, last = -dom * count, (DOMS - dom) * count
        def mask(k, v):
            if 0 <= k < count:
                return v
            ok = (k >= first) & (k < last)
            return jnp.where(ok, v, 0.0)
        return mask

    lane = lanes_of((8, 128)) & 3
    aligned = dom - spot
    swapped_first = aligned + jnp.where(
        spot < RING // 2, jnp.where(lower, -(RING // 2), RING // 2), jnp.where(lower, RING, 0)
    )

    def vector(i, half):
        wanted = dom - REACH + i
        at = wanted - own_first
        held = (at >= 0) & (at < RING)
        slot = ring_slot(jnp.clip(at, 0, RING - 1), core)
        extra = jnp.clip(wanted - swapped_first, 0, RING // 2 - 1)
        v = jnp.where(
            held, mine_ref[slot, pl.ds(8 * half, 8), :], swapped_ref[34 + 2 * extra + half]
        )
        return jnp.where((wanted >= 0) & (wanted < DOMS), v, 0.0)

    b2, t2, r2 = Held(b2_ref, -30), Held(t2_ref, -25), Held(r2_ref, -24)
    for i in range(16):
        packed = None
        for part in ((i, 0), (i - 1, 1)):
            if 0 <= part[0] < 15:
                v = vector(*part)
                packed = v if packed is None else packed + v
        for p in range(4):
            only = jnp.where(lane == p, packed, 0.0)
            only = only + pltpu.roll(only, 1 if p % 2 == 0 else 127, 1)
            only = only + pltpu.roll(only, 2 if p < 2 else 126, 1)
            b2.put(4 * (i - REACH) - 2 + p, only)
    inside2, inside3, inside4 = masked(4), masked(2), masked(1)
    hold_T(b2, t2, range(-25, 29), 4, inside2)
    hold_T(t2, r2, range(-24, 28), 4, lambda k, v: v)

    b3 = {}
    for k in range(-12, 14):
        v = pair_y(pair_z(r2[2 * k] + r2[2 * k + 1], 4), 1)
        b3[k] = inside3(k, 0.5 * v)
    t3 = run_T(b3, range(-11, 13), 8, 2, inside3)
    r3 = run_T(t3, range(-10, 12), 8, 2)

    b4 = {}
    for k in range(-5, 6):
        v = pair_y(pair_z(r3[2 * k] + r3[2 * k + 1], 8), 2)
        b4[k] = inside4(k, 0.5 * v)
    t4 = run_T(b4, range(-4, 5), 16, 4, inside4)
    r4 = run_T(t4, range(-3, 4), 16, 4, inside4)
    u4 = run_T(r4, range(-2, 3), 16, 4)
    e4 = {k: ALPHA * (b4[k] + t4[k] + r4[k] + u4[k]) for k in range(-2, 3)}
    e4 = {k: inside4(k, v) for k, v in e4.items()}

    v3 = {k: ALPHA * t3[k] + e4[k // 2] for k in range(-4, 6)}
    v3 = run_T(v3, range(-3, 5), 8, 2, inside3)
    w3 = run_T(v3, range(-2, 4), 8, 2)
    e3 = {k: inside3(k, w3[k] + ALPHA * (b3[k] + t3[k] + r3[k])) for k in range(-2, 4)}

    v2 = {k: ALPHA * t2[k] + e3[k // 2] for k in range(-4, 8)}
    v2 = run_T(v2, range(-3, 7), 4, 1, inside2)
    w2 = run_T(v2, range(-2, 6), 4, 1)
    e2 = {k: inside2(k, w2[k] + ALPHA * (b2[k] + t2[k] + r2[k])) for k in range(-2, 6)}

    inside1, inside0 = masked(8), masked(16)
    spread = {k: jnp.stack([e2[k // 2]] * 2, axis=0) for k in range(-4, 12)}
    v1 = run_T(spread, range(-2, 10), 2, 1, inside1)
    w1 = run_T(v1, range(-1, 9), 2, 1)
    even = (lanes_of((8, 128)) & 1) == 0
    for side, first in ((low, -1), (high, 3)):
        for pair in range(3):
            both = [side(16 + 2 * pair + q) for q in range(2)]
            one = jnp.stack([jnp.where(even, v, pltpu.roll(v, 1, 1)) for v in both], axis=0)
            two = jnp.stack([jnp.where(even, pltpu.roll(v, 127, 1), v) for v in both], axis=0)
            for k, v in ((first + 2 * pair, one), (first + 2 * pair + 1, two)):
                w1[k] = w1[k] + v
    e1 = {k: inside1(k, w1[k] + own1_ref[k + 1]) for k in range(-1, 9)}

    def prolonged(k):
        v = e1[k // 2]
        return jnp.stack([v[0], v[0], v[1], v[1]], axis=0)

    p1 = Held(p1_ref, -1)
    wide = {k: prolonged(k) for k in range(-2, 18)}
    hold_T(wide, p1, range(-1, 17), 1, inside0)
    for k in range(16):
        v = smooth(p1[k - 1], p1[k], p1[k + 1], 1) + own0_ref[k]
        if k < 4:
            v = v + low(pl.ds(4 * k, 4))
        if k >= 12:
            v = v + high(pl.ds(4 * (k - 12), 4))
        for q in range(4):
            pot_ref[k, pl.ds(q, 8, stride=4), :] = v[q]
        if k % 4 == 3:
            part = pl.ds(k - 3, 4)
            copies.append(pltpu.make_async_copy(pot_ref.at[part], pot_hbm.at[part], sems.at[k // 4]))
            copies[-1].start()
    for copy in copies:
        copy.wait()


def final_part(*operands):
    vmem = pl.BlockSpec(memory_space=pltpu.VMEM)
    hbm = pl.BlockSpec(memory_space=pltpu.HBM)
    shape = lambda *s: jax.ShapeDtypeStruct(s, F32)
    return pl.pallas_call(
        final_kernel,
        out_shape=(shape(16, 32, 128), shape(16, 32, 128)),
        in_specs=[vmem] * 6,
        out_specs=(hbm, hbm),
        scratch_shapes=[
            pltpu.VMEM((64, 8, 128), F32), pltpu.VMEM((54, 8, 128), F32),
            pltpu.VMEM((52, 8, 128), F32), pltpu.VMEM((18, 4, 8, 128), F32),
            pltpu.VMEM((16, 32, 128), F32), pltpu.VMEM((16, 32, 128), F32),
            pltpu.SemaphoreType.DMA((5,)),
        ],
        compiler_params=pltpu.CompilerParams(vmem_limit_bytes=32 * 2**20),
        name="final",
    )(*operands)


def on_device(orbitals, spin_group, occupation, potential_guess):
    applied = guess_part(potential_guess)
    parts = lax.all_to_all(density(spin_group, occupation, orbitals), "band", 0, 0)
    far, to_send, minus, *held = far_part(parts, applied)
    rings = [
        [
            b * DOMS + (first + 8 * (b % 2) + (ROOT - 8 * (b % 2) + i) % RING) % DOMS
            for i in range(RING)
        ]
        for b in range(BANDS) for first in range(0, DOMS, RING)
    ]
    mine = lax.all_to_all(far, ("band", "dom"), 0, 0, axis_index_groups=rings)

    edges = [
        (b * DOMS + d + 1 - b % 2, b * DOMS + d + b % 2) for b in range(BANDS) for d in range(DOMS - 1)
    ]
    halo = lax.ppermute(to_send, ("band", "dom"), edges)
    own0, own1 = near_part(potential_guess, *held)
    swap = [(b, b ^ 1) for b in range(BANDS)]
    swapped = lax.ppermute(pack(mine, halo, minus), "band", swap)
    return final_part(mine, swapped, halo, minus, own0, own1)


def solution(mesh):
    placed = (P("band", "dom", None, None), P("band"), P("band"), P("dom", None, None))
    return jax.shard_map(
        on_device,
        mesh=mesh,
        in_specs=placed,
        out_specs=(P("dom", None, None), P("dom", None, None)),
        check_vma=False,
    )
```

```python
import functools

import jax
import jax.numpy as jnp
from jax import lax
from jax.experimental import pallas as pl
from jax.experimental.pallas import tpu as pltpu
from jax.sharding import PartitionSpec as P

DEN = 16
BANDS = 8
DOMS = 64
REACH = 7
RING = 16
ROWS = 96
ROOT = 11
ALPHA = 1.0 / 9.0
SOURCE_SCALE = 0.6
F32 = jnp.float32


def lanes_of(shape):
    return lax.broadcasted_iota(jnp.int32, shape, len(shape) - 1)


def rows_of(shape):
    return lax.broadcasted_iota(jnp.int32, shape, len(shape) - 2)


def sides_z(v, step):
    lane = lanes_of(v.shape)
    ax = v.ndim - 1
    left = jnp.where(lane >= step, pltpu.roll(v, step, ax), 0.0)
    right = jnp.where(lane < 128 - step, pltpu.roll(v, 128 - step, ax), 0.0)
    return left + right


def from_below(v, step=1):
    return jnp.where(rows_of(v.shape) >= step, pltpu.roll(v, step, v.ndim - 2), 0.0)


def from_above(v, step=1):
    return jnp.where(rows_of(v.shape) < 8 - step, pltpu.roll(v, 8 - step, v.ndim - 2), 0.0)


def sides_y(v, step):
    if v.ndim == 2:
        return from_below(v, step) + from_above(v, step)
    parts = [v[q] for q in range(v.shape[0])]
    n = len(parts)
    out = []
    for q in range(n):
        lower = parts[q - 1] if q > 0 else from_below(parts[n - 1])
        upper = parts[q + 1] if q < n - 1 else from_above(parts[0])
        out.append(lower + upper)
    return jnp.stack(out, axis=0)


def smooth(low, v, high, zstep, ystep=1):
    around = sides_y(v, ystep) + sides_z(v, zstep)
    if low is not None:
        around = around + low
    if high is not None:
        around = around + high
    return v * (1.0 / 3.0) + around * ALPHA


def pair_z(v, step):
    lane = lanes_of(v.shape)
    ax = v.ndim - 1
    other = jnp.where((lane & step) == 0, pltpu.roll(v, 128 - step, ax), pltpu.roll(v, step, ax))
    return v + other


def pair_y(v, step):
    row = rows_of(v.shape)
    ax = v.ndim - 2
    other = jnp.where((row & step) == 0, pltpu.roll(v, 8 - step, ax), pltpu.roll(v, step, ax))
    return v + other


def run_T(src, planes, zstep, ystep=1, mask=None):
    out = {}
    for k in planes:
        v = src.get(k)
        low, high = src.get(k - 1), src.get(k + 1)
        if v is None:
            edge = low if low is not None else high
            got = edge * ALPHA
        else:
            got = smooth(low, v, high, zstep, ystep)
        out[k] = got if mask is None else mask(k, got)
    return out


class Held:
    def __init__(self, ref, first):
        self.ref, self.first, self.have = ref, first, set()

    def put(self, k, value):
        self.ref[k - self.first] = value
        self.have.add(k)

    def get(self, k):
        return self.ref[k - self.first] if k in self.have else None

    def __getitem__(self, k):
        return self.ref[k - self.first]


def hold_T(src, held, planes, zstep, mask):
    for k in planes:
        v = src.get(k)
        low, high = src.get(k - 1), src.get(k + 1)
        if v is None:
            got = (low if low is not None else high) * ALPHA
        else:
            got = smooth(low, v, high, zstep)
        held.put(k, mask(k, got))


def refine_z(coarse):
    row = lax.broadcasted_iota(jnp.int32, (128, 256), 0)
    col = lax.broadcasted_iota(jnp.int32, (128, 256), 1)
    own = col >> 1
    other = jnp.where((col & 1) == 0, own - 1, own + 1)
    inside = (other >> 6) == (col >> 7)
    matrix = jnp.where(row == own, 0.75, jnp.where((row == other) & inside, 0.25, 0.0))
    return jnp.dot(
        coarse, matrix, precision=lax.Precision.HIGHEST, preferred_element_type=F32
    )


def refine_y(pair):
    first, second = pair
    return jnp.stack(
        [
            0.75 * first + 0.25 * from_below(second),
            0.75 * first + 0.25 * second,
            0.75 * second + 0.25 * first,
            0.75 * second + 0.25 * from_above(first),
        ],
        axis=0,
    )


def refine_x(coarse, k):
    i = k // 2
    other = i - 1 if k % 2 == 0 else i + 1
    total = None
    for j, factor in ((i, 0.75), (other, 0.25)):
        if 0 <= j < 8:
            term = factor * coarse[j]
            total = term if total is None else total + term
    return total


def masks(dom):
    low_flag = jnp.where(dom > 0, 1.0, 0.0).astype(F32)
    high_flag = jnp.where(dom < DOMS - 1, 1.0, 0.0).astype(F32)

    def masked(last):
        def mask(k, v):
            if k < 0:
                return v * low_flag
            if k > last:
                return v * high_flag
            return v
        return mask

    return masked(15), masked(7)


def guess_planes(guess_ref):
    def guess(k):
        if not 0 <= k < 16:
            return None
        return jnp.stack([guess_ref[k, pl.ds(q, 8, stride=4), :] for q in range(4)], axis=0)
    return guess


def restricted(r, k):
    total = None
    for fine in (2 * k, 2 * k + 1):
        v = r.get(fine)
        if v is not None:
            total = v if total is None else total + v
    total = jnp.stack([total[0] + total[1], total[2] + total[3]], axis=0)
    return 0.5 * pair_z(total, 1)


def geometric(b, t, r, k, zstep):
    low, v, high = r.get(k - 1), r.get(k), r.get(k + 1)
    if v is None:
        last = (low if low is not None else high) * ALPHA
    else:
        last = smooth(low, v, high, zstep)
    for term in (r.get(k), t.get(k), b.get(k)):
        if term is not None:
            last = last + term
    return last * ALPHA


def copy_all(source, target, count, sems):
    copies = [pltpu.make_async_copy(source, target.at[i], sems.at[i]) for i in range(count)]
    for copy in copies:
        copy.start()
    return copies


def density_kernel(
    spin_hbm, occ_hbm, orb_hbm, part_ref, spin_ref, occ_ref, orb_ref, plane_ref, sems,
):
    loads = [
        pltpu.make_async_copy(spin_hbm, spin_ref, sems.at[8]),
        pltpu.make_async_copy(occ_hbm, occ_ref, sems.at[9]),
    ]
    loads += [pltpu.make_async_copy(orb_hbm.at[k], orb_ref.at[k], sems.at[k]) for k in range(8)]
    for load in loads:
        load.start()
    loads[0].wait()
    loads[1].wait()
    ups, downs = [0.0] * 8, [0.0] * 8
    for k in range(8):
        weight = occ_ref[k].astype(F32) * (0.125 / DEN)
        up = spin_ref[k] == 0
        up, down = jnp.where(up, weight, 0.0), jnp.where(up, 0.0, weight)
        loads[2 + k].wait()
        for x in range(8):
            square = orb_ref[k, x] * orb_ref[k, x]
            ups[x] = ups[x] + up * square
            downs[x] = downs[x] + down * square
    for x in range(8):
        plane_ref[x] = ups[x] + downs[x]
        plane_ref[8 + x] = ups[x] - downs[x]

    def halves(plane):
        return jnp.concatenate(
            [plane_ref[plane, pl.ds(p, 8, stride=2), :] for p in range(2)], axis=-1
        )

    for x in range(8):
        total, difference = halves(x), halves(8 + x)
        for b in range(BANDS):
            part_ref[b, pl.ds(8 * x, 8), :] = total
            if b % 2 == x // 4:
                part_ref[b, pl.ds(64 + 8 * (x % 4), 8), :] = difference


def density(spin_group, occupation, orbitals):
    hbm = pl.BlockSpec(memory_space=pltpu.HBM)
    return pl.pallas_call(
        density_kernel,
        out_shape=jax.ShapeDtypeStruct((BANDS, ROWS, 128), F32),
        in_specs=[hbm] * 3,
        out_specs=pl.BlockSpec(memory_space=pltpu.VMEM),
        scratch_shapes=[
            pltpu.SMEM((8,), jnp.int32), pltpu.SMEM((8,), jnp.int32),
            pltpu.VMEM((8, 8, 16, 64), F32), pltpu.VMEM((16, 16, 64), F32),
            pltpu.SemaphoreType.DMA((10,)),
        ],
        compiler_params=pltpu.CompilerParams(vmem_limit_bytes=57 * 2**20),
        name="density",
    )(spin_group, occupation, orbitals)


def plane_pair(wide, plane):
    rows = wide[8 * plane:8 * plane + 8]
    return rows[:, :128], rows[:, 128:]


def far_kernel(
    part_ref, guess_ref, far_hbm, halo_ref, minus_ref,
    d_ref, t_ref, r_ref, b1_ref, t1_ref, r1_ref, sum_ref, far_ref, sems,
):
    inside0, inside1 = masks(lax.axis_index("dom"))
    for i in range(ROWS // 16):
        rows = pl.ds(16 * i, 16)
        total = part_ref[0, rows, :]
        for band in range(1, BANDS):
            total = total + part_ref[band, rows, :]
        sum_ref[rows, :] = total
    wide = refine_z(sum_ref[...])
    plus = [SOURCE_SCALE * refine_y(plane_pair(wide, x)) for x in range(8)]
    for j in range(4):
        minus_ref[2 * j], minus_ref[2 * j + 1] = plane_pair(wide, 8 + j)
    d, t, r = Held(d_ref, -1), Held(t_ref, -2), Held(r_ref, -3)
    guess = guess_planes(guess_ref)
    for k in range(-1, 17):
        v, low, high = guess(k), guess(k - 1), guess(k + 1)
        around = None
        if v is not None:
            around = sides_y(v, 1) + sides_z(v, 1)
        for side in (low, high):
            if side is not None:
                around = side if around is None else around + side
        if v is not None:
            around = around - 6.0 * v
        d.put(k, inside0(k, refine_x(plus, k) + around))
    hold_T(d, t, range(-2, 18), 1, inside0)
    hold_T(t, r, range(-3, 19), 1, inside0)
    b1, t1, r1 = Held(b1_ref, -2), Held(t1_ref, -3), Held(r1_ref, -4)
    for k in range(-2, 10):
        b1.put(k, restricted(r, k))
    hold_T(b1, t1, range(-3, 11), 2, inside1)
    hold_T(t1, r1, range(-4, 12), 2, inside1)
    lane = lanes_of((8, 128)) & 3
    for group in range(2):
        packed = None
        for p in range(4):
            k = 4 * group + p - 2
            v = r1[2 * k] + r1[2 * k + 1]
            v = 0.5 * pair_z(v[0] + v[1], 2)
            packed = v if packed is None else jnp.where(lane == p, v, packed)
        far_ref[pl.ds(8 * group, 8), :] = packed
    copies = copy_all(far_ref, far_hbm, RING, sems)

    core = lax.axis_index("band") % 2
    even = (lanes_of((8, 128)) & 1) == 0

    def edges(first0, first1, plane):
        for k in range(4):
            halo_ref[pl.ds(4 * k, 4)] = geometric(d, t, r, first0 + k, 1)
        for pair in range(3):
            one = geometric(b1, t1, r1, first1 + 2 * pair, 2)
            two = geometric(b1, t1, r1, first1 + 2 * pair + 1, 2)
            for q in range(2):
                halo_ref[16 + 2 * pair + q] = jnp.where(even, one[q], two[q])
        halo_ref[pl.ds(22, 4)] = 0.25 * refine_y((minus_ref[2 * plane], minus_ref[2 * plane + 1]))

    @pl.when(core == 0)
    def _():
        edges(-4, -5, 0)

    @pl.when(core == 1)
    def _():
        edges(16, 7, 3)

    for copy in copies:
        copy.wait()


def far_part(parts, guess):
    vmem = pl.BlockSpec(memory_space=pltpu.VMEM)
    shape = lambda *s: jax.ShapeDtypeStruct(s, F32)
    return pl.pallas_call(
        far_kernel,
        out_shape=(
            shape(RING, 16, 128), shape(26, 8, 128), shape(8, 8, 128),
            shape(18, 4, 8, 128), shape(20, 4, 8, 128), shape(22, 4, 8, 128),
            shape(12, 2, 8, 128), shape(14, 2, 8, 128), shape(16, 2, 8, 128),
        ),
        in_specs=[vmem, vmem],
        out_specs=(pl.BlockSpec(memory_space=pltpu.HBM),) + (vmem,) * 8,
        scratch_shapes=[
            pltpu.VMEM((ROWS, 128), F32), pltpu.VMEM((16, 128), F32), pltpu.SemaphoreType.DMA((RING,)),
        ],
        compiler_params=pltpu.CompilerParams(vmem_limit_bytes=32 * 2**20),
        name="far",
    )(parts, guess)


class Given(Held):
    def __init__(self, ref, first):
        super().__init__(ref, first)
        self.have = set(range(first, first + ref.shape[0]))


def near_kernel(
    guess_ref, d_ref, t_ref, r_ref, b1_ref, t1_ref, r1_ref, own0_ref, own1_ref,
):
    d, t, r = Given(d_ref, -1), Given(t_ref, -2), Given(r_ref, -3)
    b1, t1, r1 = Given(b1_ref, -2), Given(t1_ref, -3), Given(r1_ref, -4)
    guess = guess_planes(guess_ref)
    for k in range(-1, 9):
        own1_ref[k + 1] = geometric(b1, t1, r1, k, 2)
    for k in range(16):
        own0_ref[k] = geometric(d, t, r, k, 1) + guess(k)


def near_part(guess, *held):
    vmem = pl.BlockSpec(memory_space=pltpu.VMEM)
    shape = lambda *s: jax.ShapeDtypeStruct(s, F32)
    return pl.pallas_call(
        near_kernel,
        out_shape=(shape(16, 4, 8, 128), shape(10, 2, 8, 128)),
        in_specs=[vmem] * 7,
        out_specs=(vmem,) * 2,
        compiler_params=pltpu.CompilerParams(vmem_limit_bytes=32 * 2**20),
        cost_estimate=pl.CostEstimate(flops=10**6, bytes_accessed=2**20, transcendentals=0),
        name="near",
    )(guess, *held)


def pack_kernel(mine_ref, halo_ref, minus_ref, out_ref):
    out_ref[pl.ds(0, 26)] = halo_ref[...]
    out_ref[pl.ds(26, 8)] = minus_ref[...]
    for i in range(RING):
        for half in range(2):
            out_ref[34 + 2 * i + half] = mine_ref[i, pl.ds(8 * half, 8), :]


def pack(mine, halo, minus):
    vmem = pl.BlockSpec(memory_space=pltpu.VMEM)
    return pl.pallas_call(
        pack_kernel,
        out_shape=jax.ShapeDtypeStruct((66, 8, 128), F32),
        in_specs=[vmem] * 3,
        out_specs=vmem,
        compiler_params=pltpu.CompilerParams(vmem_limit_bytes=32 * 2**20),
        name="pack",
    )(mine, halo, minus)


def final_kernel(
    mine_ref, swapped_ref, halo_ref, minus_ref, own0_ref, own1_ref, pot_hbm, mag_hbm,
    b2_ref, t2_ref, r2_ref, p1_ref, pot_ref, mag_ref, sems,
):
    dom = lax.axis_index("dom")
    lower = lax.axis_index("band") % 2 == 0

    def high(i):
        return jnp.where(lower, halo_ref[i], swapped_ref[i])

    def low(i):
        return jnp.where(lower, swapped_ref[i], halo_ref[i])

    minus = []
    for x in range(8):
        j = x % 4
        pair = []
        for p in range(2):
            own = minus_ref[2 * j + p]
            pair.append(jnp.where(lower == (x < 4), own, swapped_ref[26 + 2 * j + p]))
        minus.append(refine_y(pair))
    for k in range(16):
        mag = refine_x(minus, k)
        if k == 0:
            mag = mag + low(pl.ds(22, 4))
        if k == 15:
            mag = mag + high(pl.ds(22, 4))
        for q in range(4):
            mag_ref[k, pl.ds(q, 8, stride=4), :] = mag[q]
    copies = [pltpu.make_async_copy(mag_ref, mag_hbm, sems.at[4])]
    copies[0].start()

    def masked(count):
        first, last = -dom * count, (DOMS - dom) * count
        def mask(k, v):
            if 0 <= k < count:
                return v
            ok = (k >= first) & (k < last)
            return jnp.where(ok, v, 0.0)
        return mask

    lane = lanes_of((8, 128)) & 3
    spot = dom % RING
    first = dom - spot
    other_first = first + jnp.where(spot < RING // 2, -(RING // 2), RING // 2)

    def vector(i, half):
        wanted = dom - REACH + i
        at = wanted - first
        aligned = (at >= 0) & (at < RING)
        at = jnp.clip(jnp.where(aligned, at, wanted - other_first), 0, RING - 1)
        slot = (at + RING - jnp.where(aligned, ROOT, ROOT - RING // 2)) % RING
        v = jnp.where(
            aligned == lower, mine_ref[slot, pl.ds(8 * half, 8), :], swapped_ref[34 + 2 * slot + half]
        )
        return jnp.where((wanted >= 0) & (wanted < DOMS), v, 0.0)

    b2, t2, r2 = Held(b2_ref, -30), Held(t2_ref, -25), Held(r2_ref, -24)
    for i in range(16):
        packed = None
        for part in ((i, 0), (i - 1, 1)):
            if 0 <= part[0] < 15:
                v = vector(*part)
                packed = v if packed is None else packed + v
        for p in range(4):
            only = jnp.where(lane == p, packed, 0.0)
            only = only + pltpu.roll(only, 1 if p % 2 == 0 else 127, 1)
            only = only + pltpu.roll(only, 2 if p < 2 else 126, 1)
            b2.put(4 * (i - REACH) - 2 + p, only)
    inside2, inside3, inside4 = masked(4), masked(2), masked(1)
    hold_T(b2, t2, range(-25, 29), 4, inside2)
    hold_T(t2, r2, range(-24, 28), 4, lambda k, v: v)

    b3 = {}
    for k in range(-12, 14):
        v = pair_y(pair_z(r2[2 * k] + r2[2 * k + 1], 4), 1)
        b3[k] = inside3(k, 0.5 * v)
    t3 = run_T(b3, range(-11, 13), 8, 2, inside3)
    r3 = run_T(t3, range(-10, 12), 8, 2)

    b4 = {}
    for k in range(-5, 6):
        v = pair_y(pair_z(r3[2 * k] + r3[2 * k + 1], 8), 2)
        b4[k] = inside4(k, 0.5 * v)
    t4 = run_T(b4, range(-4, 5), 16, 4, inside4)
    r4 = run_T(t4, range(-3, 4), 16, 4, inside4)
    u4 = run_T(r4, range(-2, 3), 16, 4)
    e4 = {k: ALPHA * (b4[k] + t4[k] + r4[k] + u4[k]) for k in range(-2, 3)}
    e4 = {k: inside4(k, v) for k, v in e4.items()}

    v3 = {k: ALPHA * t3[k] + e4[k // 2] for k in range(-4, 6)}
    v3 = run_T(v3, range(-3, 5), 8, 2, inside3)
    w3 = run_T(v3, range(-2, 4), 8, 2)
    e3 = {k: inside3(k, w3[k] + ALPHA * (b3[k] + t3[k] + r3[k])) for k in range(-2, 4)}

    v2 = {k: ALPHA * t2[k] + e3[k // 2] for k in range(-4, 8)}
    v2 = run_T(v2, range(-3, 7), 4, 1, inside2)
    w2 = run_T(v2, range(-2, 6), 4, 1)
    e2 = {k: inside2(k, w2[k] + ALPHA * (b2[k] + t2[k] + r2[k])) for k in range(-2, 6)}

    inside1, inside0 = masked(8), masked(16)
    spread = {k: jnp.stack([e2[k // 2]] * 2, axis=0) for k in range(-4, 12)}
    v1 = run_T(spread, range(-2, 10), 2, 1, inside1)
    w1 = run_T(v1, range(-1, 9), 2, 1)
    even = (lanes_of((8, 128)) & 1) == 0
    for side, first in ((low, -1), (high, 3)):
        for pair in range(3):
            both = [side(16 + 2 * pair + q) for q in range(2)]
            one = jnp.stack([jnp.where(even, v, pltpu.roll(v, 1, 1)) for v in both], axis=0)
            two = jnp.stack([jnp.where(even, pltpu.roll(v, 127, 1), v) for v in both], axis=0)
            for k, v in ((first + 2 * pair, one), (first + 2 * pair + 1, two)):
                w1[k] = w1[k] + v
    e1 = {k: inside1(k, w1[k] + own1_ref[k + 1]) for k in range(-1, 9)}

    def prolonged(k):
        v = e1[k // 2]
        return jnp.stack([v[0], v[0], v[1], v[1]], axis=0)

    p1 = Held(p1_ref, -1)
    wide = {k: prolonged(k) for k in range(-2, 18)}
    hold_T(wide, p1, range(-1, 17), 1, inside0)
    for k in range(16):
        v = smooth(p1[k - 1], p1[k], p1[k + 1], 1) + own0_ref[k]
        if k < 4:
            v = v + low(pl.ds(4 * k, 4))
        if k >= 12:
            v = v + high(pl.ds(4 * (k - 12), 4))
        for q in range(4):
            pot_ref[k, pl.ds(q, 8, stride=4), :] = v[q]
        if k % 4 == 3:
            part = pl.ds(k - 3, 4)
            copies.append(pltpu.make_async_copy(pot_ref.at[part], pot_hbm.at[part], sems.at[k // 4]))
            copies[-1].start()
    for copy in copies:
        copy.wait()


def final_part(*operands):
    vmem = pl.BlockSpec(memory_space=pltpu.VMEM)
    hbm = pl.BlockSpec(memory_space=pltpu.HBM)
    shape = lambda *s: jax.ShapeDtypeStruct(s, F32)
    return pl.pallas_call(
        final_kernel,
        out_shape=(shape(16, 32, 128), shape(16, 32, 128)),
        in_specs=[vmem] * 6,
        out_specs=(hbm, hbm),
        scratch_shapes=[
            pltpu.VMEM((64, 8, 128), F32), pltpu.VMEM((54, 8, 128), F32),
            pltpu.VMEM((52, 8, 128), F32), pltpu.VMEM((18, 4, 8, 128), F32),
            pltpu.VMEM((16, 32, 128), F32), pltpu.VMEM((16, 32, 128), F32),
            pltpu.SemaphoreType.DMA((5,)),
        ],
        compiler_params=pltpu.CompilerParams(vmem_limit_bytes=32 * 2**20),
        name="final",
    )(*operands)


def on_device(orbitals, spin_group, occupation, potential_guess):
    parts = lax.all_to_all(density(spin_group, occupation, orbitals), "band", 0, 0)
    far, to_send, minus, *held = far_part(parts, potential_guess)
    rings = []
    for b in range(BANDS):
        half = RING // 2 * (b % 2)
        for first in range(half, DOMS - half, RING):
            rings.append([b * DOMS + first + (ROOT - half + i) % RING for i in range(RING)])
    for first in (0, 4, DOMS - 8, DOMS - 4):
        rings.append([b * DOMS + first + i for b in range(1, BANDS, 2) for i in range(4)])
    mine = lax.all_to_all(far, ("band", "dom"), 0, 0, axis_index_groups=rings)

    edges = [
        (b * DOMS + d + 1 - b % 2, b * DOMS + d + b % 2) for b in range(BANDS) for d in range(DOMS - 1)
    ]
    halo = lax.ppermute(to_send, ("band", "dom"), edges)
    own0, own1 = near_part(potential_guess, *held)
    swap = [(b, b ^ 1) for b in range(BANDS)]
    swapped = lax.ppermute(pack(mine, halo, minus), "band", swap)
    return final_part(mine, swapped, halo, minus, own0, own1)


def solution(mesh):
    placed = (P("band", "dom", None, None), P("band"), P("band"), P("dom", None, None))
    return jax.shard_map(
        on_device,
        mesh=mesh,
        in_specs=placed,
        out_specs=(P("dom", None, None), P("dom", None, None)),
        check_vma=False,
    )
```

```python
import functools

import jax
import jax.numpy as jnp
from jax import lax
from jax.experimental import pallas as pl
from jax.experimental.pallas import tpu as pltpu
from jax.sharding import PartitionSpec as P

DEN = 16
BANDS = 8
DOMS = 64
REACH = 7
RING = 16
ROWS = 96
ROOT = 11
ALPHA = 1.0 / 9.0
SOURCE_SCALE = 0.6
F32 = jnp.float32


def lanes_of(shape):
    return lax.broadcasted_iota(jnp.int32, shape, len(shape) - 1)


def rows_of(shape):
    return lax.broadcasted_iota(jnp.int32, shape, len(shape) - 2)


def sides_z(v, step):
    lane = lanes_of(v.shape)
    ax = v.ndim - 1
    left = jnp.where(lane >= step, pltpu.roll(v, step, ax), 0.0)
    right = jnp.where(lane < 128 - step, pltpu.roll(v, 128 - step, ax), 0.0)
    return left + right


def from_below(v, step=1):
    return jnp.where(rows_of(v.shape) >= step, pltpu.roll(v, step, v.ndim - 2), 0.0)


def from_above(v, step=1):
    return jnp.where(rows_of(v.shape) < 8 - step, pltpu.roll(v, 8 - step, v.ndim - 2), 0.0)


def sides_y(v, step):
    if v.ndim == 2:
        return from_below(v, step) + from_above(v, step)
    parts = [v[q] for q in range(v.shape[0])]
    n = len(parts)
    out = []
    for q in range(n):
        lower = parts[q - 1] if q > 0 else from_below(parts[n - 1])
        upper = parts[q + 1] if q < n - 1 else from_above(parts[0])
        out.append(lower + upper)
    return jnp.stack(out, axis=0)


def smooth(low, v, high, zstep, ystep=1):
    around = sides_y(v, ystep) + sides_z(v, zstep)
    if low is not None:
        around = around + low
    if high is not None:
        around = around + high
    return v * (1.0 / 3.0) + around * ALPHA


def pair_z(v, step):
    lane = lanes_of(v.shape)
    ax = v.ndim - 1
    other = jnp.where((lane & step) == 0, pltpu.roll(v, 128 - step, ax), pltpu.roll(v, step, ax))
    return v + other


def pair_y(v, step):
    row = rows_of(v.shape)
    ax = v.ndim - 2
    other = jnp.where((row & step) == 0, pltpu.roll(v, 8 - step, ax), pltpu.roll(v, step, ax))
    return v + other


def run_T(src, planes, zstep, ystep=1, mask=None):
    out = {}
    for k in planes:
        v = src.get(k)
        low, high = src.get(k - 1), src.get(k + 1)
        if v is None:
            edge = low if low is not None else high
            got = edge * ALPHA
        else:
            got = smooth(low, v, high, zstep, ystep)
        out[k] = got if mask is None else mask(k, got)
    return out


class Held:
    def __init__(self, ref, first):
        self.ref, self.first, self.have = ref, first, set()

    def put(self, k, value):
        self.ref[k - self.first] = value
        self.have.add(k)

    def get(self, k):
        return self.ref[k - self.first] if k in self.have else None

    def __getitem__(self, k):
        return self.ref[k - self.first]


def hold_T(src, held, planes, zstep, mask):
    for k in planes:
        v = src.get(k)
        low, high = src.get(k - 1), src.get(k + 1)
        if v is None:
            got = (low if low is not None else high) * ALPHA
        else:
            got = smooth(low, v, high, zstep)
        held.put(k, mask(k, got))


def refine_z(coarse):
    row = lax.broadcasted_iota(jnp.int32, (128, 256), 0)
    col = lax.broadcasted_iota(jnp.int32, (128, 256), 1)
    own = col >> 1
    other = jnp.where((col & 1) == 0, own - 1, own + 1)
    inside = (other >> 6) == (col >> 7)
    matrix = jnp.where(row == own, 0.75, jnp.where((row == other) & inside, 0.25, 0.0))
    return jnp.dot(
        coarse, matrix, precision=lax.Precision.HIGHEST, preferred_element_type=F32
    )


def refine_y(pair):
    first, second = pair
    return jnp.stack(
        [
            0.75 * first + 0.25 * from_below(second),
            0.75 * first + 0.25 * second,
            0.75 * second + 0.25 * first,
            0.75 * second + 0.25 * from_above(first),
        ],
        axis=0,
    )


def refine_x(coarse, k):
    i = k // 2
    other = i - 1 if k % 2 == 0 else i + 1
    total = None
    for j, factor in ((i, 0.75), (other, 0.25)):
        if 0 <= j < 8:
            term = factor * coarse[j]
            total = term if total is None else total + term
    return total


def masks(dom):
    low_flag = jnp.where(dom > 0, 1.0, 0.0).astype(F32)
    high_flag = jnp.where(dom < DOMS - 1, 1.0, 0.0).astype(F32)

    def masked(last):
        def mask(k, v):
            if k < 0:
                return v * low_flag
            if k > last:
                return v * high_flag
            return v
        return mask

    return masked(15), masked(7)


def guess_planes(guess_ref):
    def guess(k):
        if not 0 <= k < 16:
            return None
        return jnp.stack([guess_ref[k, pl.ds(q, 8, stride=4), :] for q in range(4)], axis=0)
    return guess


def restricted(r, k):
    total = None
    for fine in (2 * k, 2 * k + 1):
        v = r.get(fine)
        if v is not None:
            total = v if total is None else total + v
    total = jnp.stack([total[0] + total[1], total[2] + total[3]], axis=0)
    return 0.5 * pair_z(total, 1)


def geometric(b, t, r, k, zstep):
    low, v, high = r.get(k - 1), r.get(k), r.get(k + 1)
    if v is None:
        last = (low if low is not None else high) * ALPHA
    else:
        last = smooth(low, v, high, zstep)
    for term in (r.get(k), t.get(k), b.get(k)):
        if term is not None:
            last = last + term
    return last * ALPHA


def copy_all(source, target, count, sems):
    copies = [pltpu.make_async_copy(source, target.at[i], sems.at[i]) for i in range(count)]
    for copy in copies:
        copy.start()
    return copies


def density_kernel(
    spin_hbm, occ_hbm, orb_hbm, part_ref, spin_ref, occ_ref, orb_ref, plane_ref, sems,
):
    loads = [
        pltpu.make_async_copy(spin_hbm, spin_ref, sems.at[8]),
        pltpu.make_async_copy(occ_hbm, occ_ref, sems.at[9]),
    ]
    loads += [pltpu.make_async_copy(orb_hbm.at[k], orb_ref.at[k], sems.at[k]) for k in range(8)]
    for load in loads:
        load.start()
    loads[0].wait()
    loads[1].wait()
    ups, downs = [0.0] * 8, [0.0] * 8
    for k in range(8):
        weight = occ_ref[k].astype(F32) * (0.125 / DEN)
        up = spin_ref[k] == 0
        up, down = jnp.where(up, weight, 0.0), jnp.where(up, 0.0, weight)
        loads[2 + k].wait()
        for x in range(8):
            square = orb_ref[k, x] * orb_ref[k, x]
            ups[x] = ups[x] + up * square
            downs[x] = downs[x] + down * square
    for x in range(8):
        plane_ref[x] = ups[x] + downs[x]
        plane_ref[8 + x] = ups[x] - downs[x]

    def halves(plane):
        return jnp.concatenate(
            [plane_ref[plane, pl.ds(p, 8, stride=2), :] for p in range(2)], axis=-1
        )

    for x in range(8):
        total, difference = halves(x), halves(8 + x)
        for b in range(BANDS):
            part_ref[b, pl.ds(8 * x, 8), :] = total
            if b % 2 == x // 4:
                part_ref[b, pl.ds(64 + 8 * (x % 4), 8), :] = difference


def density(spin_group, occupation, orbitals):
    hbm = pl.BlockSpec(memory_space=pltpu.HBM)
    return pl.pallas_call(
        density_kernel,
        out_shape=jax.ShapeDtypeStruct((BANDS, ROWS, 128), F32),
        in_specs=[hbm] * 3,
        out_specs=pl.BlockSpec(memory_space=pltpu.VMEM),
        scratch_shapes=[
            pltpu.SMEM((8,), jnp.int32), pltpu.SMEM((8,), jnp.int32),
            pltpu.VMEM((8, 8, 16, 64), F32), pltpu.VMEM((16, 16, 64), F32),
            pltpu.SemaphoreType.DMA((10,)),
        ],
        compiler_params=pltpu.CompilerParams(vmem_limit_bytes=40 * 2**20),
        name="density",
    )(spin_group, occupation, orbitals)


def plane_pair(wide, plane):
    rows = wide[8 * plane:8 * plane + 8]
    return rows[:, :128], rows[:, 128:]


def far_kernel(
    part_ref, guess_ref, far_ref, halo_ref, minus_ref,
    d_ref, t_ref, r_ref, b1_ref, t1_ref, r1_ref, sum_ref,
):
    inside0, inside1 = masks(lax.axis_index("dom"))
    for i in range(ROWS // 16):
        rows = pl.ds(16 * i, 16)
        total = part_ref[0, rows, :]
        for band in range(1, BANDS):
            total = total + part_ref[band, rows, :]
        sum_ref[rows, :] = total
    wide = refine_z(sum_ref[...])
    plus = [SOURCE_SCALE * refine_y(plane_pair(wide, x)) for x in range(8)]
    for j in range(4):
        minus_ref[2 * j], minus_ref[2 * j + 1] = plane_pair(wide, 8 + j)
    d, t, r = Held(d_ref, -1), Held(t_ref, -2), Held(r_ref, -3)
    guess = guess_planes(guess_ref)
    for k in range(-1, 17):
        v, low, high = guess(k), guess(k - 1), guess(k + 1)
        around = None
        if v is not None:
            around = sides_y(v, 1) + sides_z(v, 1)
        for side in (low, high):
            if side is not None:
                around = side if around is None else around + side
        if v is not None:
            around = around - 6.0 * v
        d.put(k, inside0(k, refine_x(plus, k) + around))
    hold_T(d, t, range(-2, 18), 1, inside0)
    hold_T(t, r, range(-3, 19), 1, inside0)
    b1, t1, r1 = Held(b1_ref, -2), Held(t1_ref, -3), Held(r1_ref, -4)
    for k in range(-2, 10):
        b1.put(k, restricted(r, k))
    hold_T(b1, t1, range(-3, 11), 2, inside1)
    hold_T(t1, r1, range(-4, 12), 2, inside1)
    lane = lanes_of((8, 128)) & 3
    for group in range(2):
        packed = None
        for p in range(4):
            k = 4 * group + p - 2
            v = r1[2 * k] + r1[2 * k + 1]
            v = 0.5 * pair_z(v[0] + v[1], 2)
            packed = v if packed is None else jnp.where(lane == p, v, packed)
        for i in range(RING):
            far_ref[i, pl.ds(8 * group, 8), :] = packed

    core = lax.axis_index("band") % 2
    even = (lanes_of((8, 128)) & 1) == 0

    def edges(first0, first1, plane):
        for k in range(4):
            halo_ref[pl.ds(4 * k, 4)] = geometric(d, t, r, first0 + k, 1)
        for pair in range(3):
            one = geometric(b1, t1, r1, first1 + 2 * pair, 2)
            two = geometric(b1, t1, r1, first1 + 2 * pair + 1, 2)
            for q in range(2):
                halo_ref[16 + 2 * pair + q] = jnp.where(even, one[q], two[q])
        halo_ref[pl.ds(22, 4)] = 0.25 * refine_y((minus_ref[2 * plane], minus_ref[2 * plane + 1]))

    @pl.when(core == 0)
    def _():
        edges(-4, -5, 0)

    @pl.when(core == 1)
    def _():
        edges(16, 7, 3)


def far_part(parts, guess):
    vmem = pl.BlockSpec(memory_space=pltpu.VMEM)
    shape = lambda *s: jax.ShapeDtypeStruct(s, F32)
    return pl.pallas_call(
        far_kernel,
        out_shape=(
            shape(RING, 16, 128), shape(26, 8, 128), shape(8, 8, 128),
            shape(18, 4, 8, 128), shape(20, 4, 8, 128), shape(22, 4, 8, 128),
            shape(12, 2, 8, 128), shape(14, 2, 8, 128), shape(16, 2, 8, 128),
        ),
        in_specs=[vmem, vmem],
        out_specs=(vmem,) * 9,
        scratch_shapes=[pltpu.VMEM((ROWS, 128), F32)],
        compiler_params=pltpu.CompilerParams(vmem_limit_bytes=32 * 2**20),
        name="far",
    )(parts, guess)


class Given(Held):
    def __init__(self, ref, first):
        super().__init__(ref, first)
        self.have = set(range(first, first + ref.shape[0]))


def near_kernel(
    guess_ref, d_ref, t_ref, r_ref, b1_ref, t1_ref, r1_ref, own0_ref, own1_ref,
):
    d, t, r = Given(d_ref, -1), Given(t_ref, -2), Given(r_ref, -3)
    b1, t1, r1 = Given(b1_ref, -2), Given(t1_ref, -3), Given(r1_ref, -4)
    guess = guess_planes(guess_ref)
    for k in range(-1, 9):
        own1_ref[k + 1] = geometric(b1, t1, r1, k, 2)
    for k in range(16):
        own0_ref[k] = geometric(d, t, r, k, 1) + guess(k)


def near_part(guess, *held):
    vmem = pl.BlockSpec(memory_space=pltpu.VMEM)
    shape = lambda *s: jax.ShapeDtypeStruct(s, F32)
    return pl.pallas_call(
        near_kernel,
        out_shape=(shape(16, 4, 8, 128), shape(10, 2, 8, 128)),
        in_specs=[vmem] * 7,
        out_specs=(vmem,) * 2,
        compiler_params=pltpu.CompilerParams(vmem_limit_bytes=32 * 2**20),
        cost_estimate=pl.CostEstimate(flops=10**6, bytes_accessed=2**20, transcendentals=0),
        name="near",
    )(guess, *held)


def pack_kernel(mine_ref, halo_ref, minus_ref, out_ref):
    out_ref[pl.ds(0, 26)] = halo_ref[...]
    out_ref[pl.ds(26, 8)] = minus_ref[...]
    for i in range(RING):
        for half in range(2):
            out_ref[34 + 2 * i + half] = mine_ref[i, pl.ds(8 * half, 8), :]


def pack(mine, halo, minus):
    vmem = pl.BlockSpec(memory_space=pltpu.VMEM)
    return pl.pallas_call(
        pack_kernel,
        out_shape=jax.ShapeDtypeStruct((66, 8, 128), F32),
        in_specs=[vmem] * 3,
        out_specs=vmem,
        compiler_params=pltpu.CompilerParams(vmem_limit_bytes=32 * 2**20),
        name="pack",
    )(mine, halo, minus)


def final_kernel(
    mine_ref, swapped_ref, halo_ref, minus_ref, own0_ref, own1_ref, pot_hbm, mag_hbm,
    b2_ref, t2_ref, r2_ref, p1_ref, pot_ref, mag_ref, sems,
):
    dom = lax.axis_index("dom")
    lower = lax.axis_index("band") % 2 == 0

    def high(i):
        return jnp.where(lower, halo_ref[i], swapped_ref[i])

    def low(i):
        return jnp.where(lower, swapped_ref[i], halo_ref[i])

    minus = []
    for x in range(8):
        j = x % 4
        pair = []
        for p in range(2):
            own = minus_ref[2 * j + p]
            pair.append(jnp.where(lower == (x < 4), own, swapped_ref[26 + 2 * j + p]))
        minus.append(refine_y(pair))
    for k in range(16):
        mag = refine_x(minus, k)
        if k == 0:
            mag = mag + low(pl.ds(22, 4))
        if k == 15:
            mag = mag + high(pl.ds(22, 4))
        for q in range(4):
            mag_ref[k, pl.ds(q, 8, stride=4), :] = mag[q]
    copies = [pltpu.make_async_copy(mag_ref, mag_hbm, sems.at[4])]
    copies[0].start()

    def masked(count):
        first, last = -dom * count, (DOMS - dom) * count
        def mask(k, v):
            if 0 <= k < count:
                return v
            ok = (k >= first) & (k < last)
            return jnp.where(ok, v, 0.0)
        return mask

    lane = lanes_of((8, 128)) & 3
    spot = dom % RING
    first = dom - spot
    other_first = first + jnp.where(spot < RING // 2, -(RING // 2), RING // 2)

    def vector(i, half):
        wanted = dom - REACH + i
        at = wanted - first
        aligned = (at >= 0) & (at < RING)
        at = jnp.clip(jnp.where(aligned, at, wanted - other_first), 0, RING - 1)
        slot = (at + RING - jnp.where(aligned, ROOT, ROOT - RING // 2)) % RING
        v = jnp.where(
            aligned == lower, mine_ref[slot, pl.ds(8 * half, 8), :], swapped_ref[34 + 2 * slot + half]
        )
        return jnp.where((wanted >= 0) & (wanted < DOMS), v, 0.0)

    b2, t2, r2 = Held(b2_ref, -30), Held(t2_ref, -25), Held(r2_ref, -24)
    for i in range(16):
        packed = None
        for part in ((i, 0), (i - 1, 1)):
            if 0 <= part[0] < 15:
                v = vector(*part)
                packed = v if packed is None else packed + v
        for p in range(4):
            only = jnp.where(lane == p, packed, 0.0)
            only = only + pltpu.roll(only, 1 if p % 2 == 0 else 127, 1)
            only = only + pltpu.roll(only, 2 if p < 2 else 126, 1)
            b2.put(4 * (i - REACH) - 2 + p, only)
    inside2, inside3, inside4 = masked(4), masked(2), masked(1)
    hold_T(b2, t2, range(-25, 29), 4, inside2)
    hold_T(t2, r2, range(-24, 28), 4, lambda k, v: v)

    b3 = {}
    for k in range(-12, 14):
        v = pair_y(pair_z(r2[2 * k] + r2[2 * k + 1], 4), 1)
        b3[k] = inside3(k, 0.5 * v)
    t3 = run_T(b3, range(-11, 13), 8, 2, inside3)
    r3 = run_T(t3, range(-10, 12), 8, 2)

    b4 = {}
    for k in range(-5, 6):
        v = pair_y(pair_z(r3[2 * k] + r3[2 * k + 1], 8), 2)
        b4[k] = inside4(k, 0.5 * v)
    t4 = run_T(b4, range(-4, 5), 16, 4, inside4)
    r4 = run_T(t4, range(-3, 4), 16, 4, inside4)
    u4 = run_T(r4, range(-2, 3), 16, 4)
    e4 = {k: ALPHA * (b4[k] + t4[k] + r4[k] + u4[k]) for k in range(-2, 3)}
    e4 = {k: inside4(k, v) for k, v in e4.items()}

    v3 = {k: ALPHA * t3[k] + e4[k // 2] for k in range(-4, 6)}
    v3 = run_T(v3, range(-3, 5), 8, 2, inside3)
    w3 = run_T(v3, range(-2, 4), 8, 2)
    e3 = {k: inside3(k, w3[k] + ALPHA * (b3[k] + t3[k] + r3[k])) for k in range(-2, 4)}

    v2 = {k: ALPHA * t2[k] + e3[k // 2] for k in range(-4, 8)}
    v2 = run_T(v2, range(-3, 7), 4, 1, inside2)
    w2 = run_T(v2, range(-2, 6), 4, 1)
    e2 = {k: inside2(k, w2[k] + ALPHA * (b2[k] + t2[k] + r2[k])) for k in range(-2, 6)}

    inside1, inside0 = masked(8), masked(16)
    spread = {k: jnp.stack([e2[k // 2]] * 2, axis=0) for k in range(-4, 12)}
    v1 = run_T(spread, range(-2, 10), 2, 1, inside1)
    w1 = run_T(v1, range(-1, 9), 2, 1)
    even = (lanes_of((8, 128)) & 1) == 0
    for side, first in ((low, -1), (high, 3)):
        for pair in range(3):
            both = [side(16 + 2 * pair + q) for q in range(2)]
            one = jnp.stack([jnp.where(even, v, pltpu.roll(v, 1, 1)) for v in both], axis=0)
            two = jnp.stack([jnp.where(even, pltpu.roll(v, 127, 1), v) for v in both], axis=0)
            for k, v in ((first + 2 * pair, one), (first + 2 * pair + 1, two)):
                w1[k] = w1[k] + v
    e1 = {k: inside1(k, w1[k] + own1_ref[k + 1]) for k in range(-1, 9)}

    def prolonged(k):
        v = e1[k // 2]
        return jnp.stack([v[0], v[0], v[1], v[1]], axis=0)

    p1 = Held(p1_ref, -1)
    wide = {k: prolonged(k) for k in range(-2, 18)}
    hold_T(wide, p1, range(-1, 17), 1, inside0)
    for k in range(16):
        v = smooth(p1[k - 1], p1[k], p1[k + 1], 1) + own0_ref[k]
        if k < 4:
            v = v + low(pl.ds(4 * k, 4))
        if k >= 12:
            v = v + high(pl.ds(4 * (k - 12), 4))
        for q in range(4):
            pot_ref[k, pl.ds(q, 8, stride=4), :] = v[q]
        if k % 4 == 3:
            part = pl.ds(k - 3, 4)
            copies.append(pltpu.make_async_copy(pot_ref.at[part], pot_hbm.at[part], sems.at[k // 4]))
            copies[-1].start()
    for copy in copies:
        copy.wait()


def final_part(*operands):
    vmem = pl.BlockSpec(memory_space=pltpu.VMEM)
    hbm = pl.BlockSpec(memory_space=pltpu.HBM)
    shape = lambda *s: jax.ShapeDtypeStruct(s, F32)
    return pl.pallas_call(
        final_kernel,
        out_shape=(shape(16, 32, 128), shape(16, 32, 128)),
        in_specs=[vmem] * 6,
        out_specs=(hbm, hbm),
        scratch_shapes=[
            pltpu.VMEM((64, 8, 128), F32), pltpu.VMEM((54, 8, 128), F32),
            pltpu.VMEM((52, 8, 128), F32), pltpu.VMEM((18, 4, 8, 128), F32),
            pltpu.VMEM((16, 32, 128), F32), pltpu.VMEM((16, 32, 128), F32),
            pltpu.SemaphoreType.DMA((5,)),
        ],
        compiler_params=pltpu.CompilerParams(vmem_limit_bytes=32 * 2**20),
        name="final",
    )(*operands)


def on_device(orbitals, spin_group, occupation, potential_guess):
    orbitals, spin_group, occupation = (
        pltpu.with_memory_space_constraint(v, pltpu.HBM) for v in (orbitals, spin_group, occupation)
    )
    parts = lax.all_to_all(density(spin_group, occupation, orbitals), "band", 0, 0)
    far, to_send, minus, *held = far_part(parts, potential_guess)
    rings = []
    for b in range(BANDS):
        half = RING // 2 * (b % 2)
        for first in range(half, DOMS - half, RING):
            rings.append([b * DOMS + first + (ROOT - half + i) % RING for i in range(RING)])
    for first in (0, 4, DOMS - 8, DOMS - 4):
        rings.append([b * DOMS + first + i for b in range(1, BANDS, 2) for i in range(4)])
    mine = lax.all_to_all(far, ("band", "dom"), 0, 0, axis_index_groups=rings)

    edges = [
        (b * DOMS + d + 1 - b % 2, b * DOMS + d + b % 2) for b in range(BANDS) for d in range(DOMS - 1)
    ]
    halo = lax.ppermute(to_send, ("band", "dom"), edges)
    own0, own1 = near_part(potential_guess, *held)
    swap = [(b, b ^ 1) for b in range(BANDS)]
    swapped = lax.ppermute(pack(mine, halo, minus), "band", swap)
    return final_part(mine, swapped, halo, minus, own0, own1)


def solution(mesh):
    placed = (P("band", "dom", None, None), P("band"), P("band"), P("dom", None, None))
    return jax.shard_map(
        on_device,
        mesh=mesh,
        in_specs=placed,
        out_specs=(P("dom", None, None), P("dom", None, None)),
        check_vma=False,
    )
```

```python
import functools

import jax
import jax.numpy as jnp
from jax import lax
from jax.experimental import pallas as pl
from jax.experimental.pallas import tpu as pltpu
from jax.sharding import PartitionSpec as P

DEN = 16
BANDS = 8
DOMS = 64
REACH = 7
RING = 16
ROWS = 96
ROOT = 11
ALPHA = 1.0 / 9.0
SOURCE_SCALE = 0.6
F32 = jnp.float32


def lanes_of(shape):
    return lax.broadcasted_iota(jnp.int32, shape, len(shape) - 1)


def rows_of(shape):
    return lax.broadcasted_iota(jnp.int32, shape, len(shape) - 2)


def sides_z(v, step):
    lane = lanes_of(v.shape)
    ax = v.ndim - 1
    left = jnp.where(lane >= step, pltpu.roll(v, step, ax), 0.0)
    right = jnp.where(lane < 128 - step, pltpu.roll(v, 128 - step, ax), 0.0)
    return left + right


def from_below(v, step=1):
    return jnp.where(rows_of(v.shape) >= step, pltpu.roll(v, step, v.ndim - 2), 0.0)


def from_above(v, step=1):
    return jnp.where(rows_of(v.shape) < 8 - step, pltpu.roll(v, 8 - step, v.ndim - 2), 0.0)


def sides_y(v, step):
    if v.ndim == 2:
        return from_below(v, step) + from_above(v, step)
    parts = [v[q] for q in range(v.shape[0])]
    n = len(parts)
    out = []
    for q in range(n):
        lower = parts[q - 1] if q > 0 else from_below(parts[n - 1])
        upper = parts[q + 1] if q < n - 1 else from_above(parts[0])
        out.append(lower + upper)
    return jnp.stack(out, axis=0)


def smooth(low, v, high, zstep, ystep=1):
    around = sides_y(v, ystep) + sides_z(v, zstep)
    if low is not None:
        around = around + low
    if high is not None:
        around = around + high
    return v * (1.0 / 3.0) + around * ALPHA


def pair_z(v, step):
    lane = lanes_of(v.shape)
    ax = v.ndim - 1
    other = jnp.where((lane & step) == 0, pltpu.roll(v, 128 - step, ax), pltpu.roll(v, step, ax))
    return v + other


def pair_y(v, step):
    row = rows_of(v.shape)
    ax = v.ndim - 2
    other = jnp.where((row & step) == 0, pltpu.roll(v, 8 - step, ax), pltpu.roll(v, step, ax))
    return v + other


def run_T(src, planes, zstep, ystep=1, mask=None):
    out = {}
    for k in planes:
        v = src.get(k)
        low, high = src.get(k - 1), src.get(k + 1)
        if v is None:
            edge = low if low is not None else high
            got = edge * ALPHA
        else:
            got = smooth(low, v, high, zstep, ystep)
        out[k] = got if mask is None else mask(k, got)
    return out


class Held:
    def __init__(self, ref, first):
        self.ref, self.first, self.have = ref, first, set()

    def put(self, k, value):
        self.ref[k - self.first] = value
        self.have.add(k)

    def get(self, k):
        return self.ref[k - self.first] if k in self.have else None

    def __getitem__(self, k):
        return self.ref[k - self.first]


def hold_T(src, held, planes, zstep, mask):
    for k in planes:
        v = src.get(k)
        low, high = src.get(k - 1), src.get(k + 1)
        if v is None:
            got = (low if low is not None else high) * ALPHA
        else:
            got = smooth(low, v, high, zstep)
        held.put(k, mask(k, got))


def refine_z(coarse):
    row = lax.broadcasted_iota(jnp.int32, (128, 256), 0)
    col = lax.broadcasted_iota(jnp.int32, (128, 256), 1)
    own = col >> 1
    other = jnp.where((col & 1) == 0, own - 1, own + 1)
    inside = (other >> 6) == (col >> 7)
    matrix = jnp.where(row == own, 0.75, jnp.where((row == other) & inside, 0.25, 0.0))
    return jnp.dot(
        coarse, matrix, precision=lax.Precision.HIGHEST, preferred_element_type=F32
    )


def refine_y(pair):
    first, second = pair
    return jnp.stack(
        [
            0.75 * first + 0.25 * from_below(second),
            0.75 * first + 0.25 * second,
            0.75 * second + 0.25 * first,
            0.75 * second + 0.25 * from_above(first),
        ],
        axis=0,
    )


def refine_x(coarse, k):
    i = k // 2
    other = i - 1 if k % 2 == 0 else i + 1
    total = None
    for j, factor in ((i, 0.75), (other, 0.25)):
        if 0 <= j < 8:
            term = factor * coarse[j]
            total = term if total is None else total + term
    return total


def masks(dom):
    low_flag = jnp.where(dom > 0, 1.0, 0.0).astype(F32)
    high_flag = jnp.where(dom < DOMS - 1, 1.0, 0.0).astype(F32)

    def masked(last):
        def mask(k, v):
            if k < 0:
                return v * low_flag
            if k > last:
                return v * high_flag
            return v
        return mask

    return masked(15), masked(7), masked(3)


def guess_planes(guess_ref):
    def guess(k):
        if not 0 <= k < 16:
            return None
        return jnp.stack([guess_ref[k, pl.ds(q, 8, stride=4), :] for q in range(4)], axis=0)
    return guess


def restricted(r, k):
    total = None
    for fine in (2 * k, 2 * k + 1):
        v = r.get(fine)
        if v is not None:
            total = v if total is None else total + v
    total = jnp.stack([total[0] + total[1], total[2] + total[3]], axis=0)
    return 0.5 * pair_z(total, 1)


def geometric(b, t, r, k, zstep):
    low, v, high = r.get(k - 1), r.get(k), r.get(k + 1)
    if v is None:
        last = (low if low is not None else high) * ALPHA
    else:
        last = smooth(low, v, high, zstep)
    for term in (r.get(k), t.get(k), b.get(k)):
        if term is not None:
            last = last + term
    return last * ALPHA


def copy_all(source, target, count, sems):
    copies = [pltpu.make_async_copy(source, target.at[i], sems.at[i]) for i in range(count)]
    for copy in copies:
        copy.start()
    return copies


def density_kernel(
    spin_hbm, occ_hbm, orb_hbm, part_ref, spin_ref, occ_ref, orb_ref, plane_ref, sems,
):
    loads = [
        pltpu.make_async_copy(spin_hbm, spin_ref, sems.at[8]),
        pltpu.make_async_copy(occ_hbm, occ_ref, sems.at[9]),
    ]
    loads += [pltpu.make_async_copy(orb_hbm.at[k], orb_ref.at[k], sems.at[k]) for k in range(8)]
    for load in loads:
        load.start()
    loads[0].wait()
    loads[1].wait()
    ups, downs = [0.0] * 8, [0.0] * 8
    for k in range(8):
        weight = occ_ref[k].astype(F32) * (0.125 / DEN)
        up = spin_ref[k] == 0
        up, down = jnp.where(up, weight, 0.0), jnp.where(up, 0.0, weight)
        loads[2 + k].wait()
        for x in range(8):
            square = orb_ref[k, x] * orb_ref[k, x]
            ups[x] = ups[x] + up * square
            downs[x] = downs[x] + down * square
    for x in range(8):
        plane_ref[x] = ups[x] + downs[x]
        plane_ref[8 + x] = ups[x] - downs[x]

    def halves(plane):
        return jnp.concatenate(
            [plane_ref[plane, pl.ds(p, 8, stride=2), :] for p in range(2)], axis=-1
        )

    for x in range(8):
        total, difference = halves(x), halves(8 + x)
        for b in range(BANDS):
            part_ref[b, pl.ds(8 * x, 8), :] = total
            if b % 2 == x // 4:
                part_ref[b, pl.ds(64 + 8 * (x % 4), 8), :] = difference


def density(spin_group, occupation, orbitals):
    hbm = pl.BlockSpec(memory_space=pltpu.HBM)
    return pl.pallas_call(
        density_kernel,
        out_shape=jax.ShapeDtypeStruct((BANDS, ROWS, 128), F32),
        in_specs=[hbm] * 3,
        out_specs=pl.BlockSpec(memory_space=pltpu.VMEM),
        scratch_shapes=[
            pltpu.SMEM((8,), jnp.int32), pltpu.SMEM((8,), jnp.int32),
            pltpu.VMEM((8, 8, 16, 64), F32), pltpu.VMEM((16, 16, 64), F32),
            pltpu.SemaphoreType.DMA((10,)),
        ],
        compiler_params=pltpu.CompilerParams(vmem_limit_bytes=40 * 2**20),
        name="density",
    )(spin_group, occupation, orbitals)


def plane_pair(wide, plane):
    rows = wide[8 * plane:8 * plane + 8]
    return rows[:, :128], rows[:, 128:]


def far_kernel(
    part_ref, guess_ref, far_ref, halo_ref, minus_ref, b2_ref,
    d_ref, t_ref, r_ref, b1_ref, t1_ref, r1_ref, sum_ref,
):
    inside0, inside1, inside2 = masks(lax.axis_index("dom"))
    for i in range(ROWS // 16):
        rows = pl.ds(16 * i, 16)
        total = part_ref[0, rows, :]
        for band in range(1, BANDS):
            total = total + part_ref[band, rows, :]
        sum_ref[rows, :] = total
    wide = refine_z(sum_ref[...])
    plus = [SOURCE_SCALE * refine_y(plane_pair(wide, x)) for x in range(8)]
    for j in range(4):
        minus_ref[2 * j], minus_ref[2 * j + 1] = plane_pair(wide, 8 + j)
    d, t, r = Held(d_ref, -1), Held(t_ref, -2), Held(r_ref, -3)
    guess = guess_planes(guess_ref)
    for k in range(-1, 17):
        v, low, high = guess(k), guess(k - 1), guess(k + 1)
        around = None
        if v is not None:
            around = sides_y(v, 1) + sides_z(v, 1)
        for side in (low, high):
            if side is not None:
                around = side if around is None else around + side
        if v is not None:
            around = around - 6.0 * v
        d.put(k, inside0(k, refine_x(plus, k) + around))
    hold_T(d, t, range(-2, 18), 1, inside0)
    hold_T(t, r, range(-3, 19), 1, inside0)
    b1, t1, r1 = Held(b1_ref, -2), Held(t1_ref, -3), Held(r1_ref, -4)
    for k in range(-2, 10):
        b1.put(k, restricted(r, k))
    hold_T(b1, t1, range(-3, 11), 2, inside1)
    hold_T(t1, r1, range(-4, 12), 2, inside1)
    b2 = {}
    for k in range(-2, 6):
        v = r1[2 * k] + r1[2 * k + 1]
        b2[k] = 0.5 * pair_z(v[0] + v[1], 2)
        b2_ref[k + 2] = b2[k]
    t2 = run_T(b2, range(-3, 7), 4, mask=inside2)
    r2 = run_T(t2, range(-4, 8), 4, mask=inside2)
    b3 = [0.5 * pair_y(pair_z(r2[2 * k] + r2[2 * k + 1], 4), 1) for k in range(-2, 4)]

    lane, row = lanes_of((8, 128)), rows_of((8, 128))
    parity = row & 1
    common = b3[0]
    for n in range(1, 4):
        here = ((lane & 7) == 3 + 4 * (n % 2)) & (parity == n // 2)
        common = jnp.where(here, b3[n], common)
    above, below = common, common
    for p in range(3):
        above = jnp.where((lane & 3) == p, b2[3 + p], above)
        below = jnp.where((lane & 3) == p, b2[p - 2], below)
    line = lanes_of((1, 128)) & 7
    last = b3[4][0:1]
    for n in (4, 5):
        for y in range(4):
            last = jnp.where(line == 4 * (n - 4) + y, b3[n][2 * y:2 * y + 1], last)
    core = lax.axis_index("band") % 2
    half = RING // 2 * core
    me = (lax.axis_index("dom") + half) % RING
    for i in range(RING):
        target = (ROOT - half + i) % RING
        far_ref[pl.ds(9 * i, 8), :] = jnp.where(target > me, above, below)
        far_ref[pl.ds(9 * i + 8, 1), :] = last

    for group in range(2):
        packed = b2[4 * group - 2]
        for p in range(1, 4):
            packed = jnp.where((lane & 3) == p, b2[4 * group - 2 + p], packed)
        halo_ref[26 + group] = packed

    even = (lane & 1) == 0

    def edges(first0, first1, plane):
        for k in range(4):
            halo_ref[pl.ds(4 * k, 4)] = geometric(d, t, r, first0 + k, 1)
        for pair in range(3):
            one = geometric(b1, t1, r1, first1 + 2 * pair, 2)
            two = geometric(b1, t1, r1, first1 + 2 * pair + 1, 2)
            for q in range(2):
                halo_ref[16 + 2 * pair + q] = jnp.where(even, one[q], two[q])
        halo_ref[pl.ds(22, 4)] = 0.25 * refine_y((minus_ref[2 * plane], minus_ref[2 * plane + 1]))

    @pl.when(core == 0)
    def _():
        edges(-4, -5, 0)

    @pl.when(core == 1)
    def _():
        edges(16, 7, 3)


def far_part(parts, guess):
    vmem = pl.BlockSpec(memory_space=pltpu.VMEM)
    shape = lambda *s: jax.ShapeDtypeStruct(s, F32)
    return pl.pallas_call(
        far_kernel,
        out_shape=(
            shape(9 * RING, 128), shape(28, 8, 128), shape(8, 8, 128), shape(8, 8, 128),
            shape(18, 4, 8, 128), shape(20, 4, 8, 128), shape(22, 4, 8, 128),
            shape(12, 2, 8, 128), shape(14, 2, 8, 128), shape(16, 2, 8, 128),
        ),
        in_specs=[vmem, vmem],
        out_specs=(vmem,) * 10,
        scratch_shapes=[pltpu.VMEM((ROWS, 128), F32)],
        compiler_params=pltpu.CompilerParams(vmem_limit_bytes=32 * 2**20),
        name="far",
    )(parts, guess)


class Given(Held):
    def __init__(self, ref, first):
        super().__init__(ref, first)
        self.have = set(range(first, first + ref.shape[0]))


def near_kernel(
    guess_ref, d_ref, t_ref, r_ref, b1_ref, t1_ref, r1_ref, own0_ref, own1_ref,
):
    d, t, r = Given(d_ref, -1), Given(t_ref, -2), Given(r_ref, -3)
    b1, t1, r1 = Given(b1_ref, -2), Given(t1_ref, -3), Given(r1_ref, -4)
    guess = guess_planes(guess_ref)
    for k in range(-1, 9):
        own1_ref[k + 1] = geometric(b1, t1, r1, k, 2)
    for k in range(16):
        own0_ref[k] = geometric(d, t, r, k, 1) + guess(k)


def near_part(guess, *held):
    vmem = pl.BlockSpec(memory_space=pltpu.VMEM)
    shape = lambda *s: jax.ShapeDtypeStruct(s, F32)
    return pl.pallas_call(
        near_kernel,
        out_shape=(shape(16, 4, 8, 128), shape(10, 2, 8, 128)),
        in_specs=[vmem] * 7,
        out_specs=(vmem,) * 2,
        compiler_params=pltpu.CompilerParams(vmem_limit_bytes=32 * 2**20),
        cost_estimate=pl.CostEstimate(flops=10**6, bytes_accessed=2**20, transcendentals=0),
        name="near",
    )(guess, *held)


def pack_kernel(mine_ref, halo_ref, minus_ref, out_ref):
    out_ref[pl.ds(0, 28)] = halo_ref[...]
    out_ref[pl.ds(28, 8)] = minus_ref[...]
    for i in range(RING):
        out_ref[36 + 2 * i] = mine_ref[pl.ds(9 * i, 8), :]
        out_ref[37 + 2 * i, pl.ds(0, 1), :] = mine_ref[pl.ds(9 * i + 8, 1), :]


def pack(mine, halo, minus):
    vmem = pl.BlockSpec(memory_space=pltpu.VMEM)
    return pl.pallas_call(
        pack_kernel,
        out_shape=jax.ShapeDtypeStruct((36 + 2 * RING, 8, 128), F32),
        in_specs=[vmem] * 3,
        out_specs=vmem,
        compiler_params=pltpu.CompilerParams(vmem_limit_bytes=32 * 2**20),
        name="pack",
    )(mine, halo, minus)


def final_kernel(
    packed_ref, swapped_ref, mine2_ref, own0_ref, own1_ref, pot_hbm, mag_hbm,
    p1_ref, pot_ref, mag_ref, sems,
):
    dom = lax.axis_index("dom")
    lower = lax.axis_index("band") % 2 == 0

    def high(i):
        return jnp.where(lower, packed_ref[i], swapped_ref[i])

    def low(i):
        return jnp.where(lower, swapped_ref[i], packed_ref[i])

    minus = []
    for x in range(8):
        j = x % 4
        pair = []
        for p in range(2):
            own = packed_ref[28 + 2 * j + p]
            pair.append(jnp.where(lower == (x < 4), own, swapped_ref[28 + 2 * j + p]))
        minus.append(refine_y(pair))
    for k in range(16):
        mag = refine_x(minus, k)
        if k == 0:
            mag = mag + low(pl.ds(22, 4))
        if k == 15:
            mag = mag + high(pl.ds(22, 4))
        for q in range(4):
            mag_ref[k, pl.ds(q, 8, stride=4), :] = mag[q]
    copies = [pltpu.make_async_copy(mag_ref, mag_hbm, sems.at[4])]
    copies[0].start()

    def masked(count):
        first, last = -dom * count, (DOMS - dom) * count
        def mask(k, v):
            if 0 <= k < count:
                return v
            ok = (k >= first) & (k < last)
            return jnp.where(ok, v, 0.0)
        return mask

    lane, row = lanes_of((8, 128)), rows_of((8, 128))
    spot = dom % RING
    first = dom - spot
    other_first = first + jnp.where(spot < RING // 2, -(RING // 2), RING // 2)
    body, last = {}, {}
    for step in range(-REACH, REACH + 1):
        wanted = dom + step
        at = wanted - first
        aligned = (at >= 0) & (at < RING)
        at = jnp.clip(jnp.where(aligned, at, wanted - other_first), 0, RING - 1)
        slot = (at + RING - jnp.where(aligned, ROOT, ROOT - RING // 2)) % RING
        there = (wanted >= 0) & (wanted < DOMS)
        for part, ref in ((0, body), (1, last)):
            rows = pl.ds(0, 1 if part else 8)
            v = jnp.where(
                aligned == lower,
                packed_ref[36 + 2 * slot + part, rows, :],
                swapped_ref[36 + 2 * slot + part, rows, :],
            )
            ref[step] = jnp.where(there, v, 0.0)

    def unpack4(v, p):
        return pair_z(pair_z(jnp.where((lane & 3) == p, v, 0.0), 1), 2)

    inside2, inside3, inside4 = masked(4), masked(2), masked(1)
    b2 = {k: mine2_ref[k + 2] for k in range(-2, 6)}
    below, above = [low(26), low(27)], [high(26), high(27)]
    for n in range(7):
        up, down = n - 5, n + 2
        v = unpack4(below[(n + 1) // 4], (n + 1) % 4)
        if n < 3:
            v = v + unpack4(body[-2], n)
        b2[up] = b2[up] + v if up in b2 else v
        v = unpack4(above[n // 4], n % 4)
        if n > 3:
            v = v + unpack4(body[2], n - 4)
        b2[down] = b2[down] + v if down in b2 else v
    t2 = run_T(b2, range(-4, 8), 4, mask=inside2)
    r2 = run_T(t2, range(-2, 6), 4)

    b3 = {}
    for pair in range(-6, 7):
        both = jnp.where((row & 1) == 0, body[pair + 1], body[pair])
        both = pair_y(jnp.where((lane & 3) == 3, both, 0.0), 1)
        tail = jnp.broadcast_to(last[pair - 1], (8, 128))
        for n in range(2):
            v = jnp.where((lane & 7) == 4 * n + 3, both, 0.0)
            v = v + jnp.where((lane & 7) == 4 * n + (row >> 1), tail, 0.0)
            b3[2 * pair + n] = pair_z(pair_z(pair_z(v, 1), 2), 4)
    t3 = run_T(b3, range(-11, 13), 8, 2, inside3)
    r3 = run_T(t3, range(-10, 12), 8, 2)

    b4 = {}
    for k in range(-5, 6):
        v = pair_y(pair_z(r3[2 * k] + r3[2 * k + 1], 8), 2)
        b4[k] = inside4(k, 0.5 * v)
    t4 = run_T(b4, range(-4, 5), 16, 4, inside4)
    r4 = run_T(t4, range(-3, 4), 16, 4, inside4)
    u4 = run_T(r4, range(-2, 3), 16, 4)
    e4 = {k: ALPHA * (b4[k] + t4[k] + r4[k] + u4[k]) for k in range(-2, 3)}
    e4 = {k: inside4(k, v) for k, v in e4.items()}

    v3 = {k: ALPHA * t3[k] + e4[k // 2] for k in range(-4, 6)}
    v3 = run_T(v3, range(-3, 5), 8, 2, inside3)
    w3 = run_T(v3, range(-2, 4), 8, 2)
    e3 = {k: inside3(k, w3[k] + ALPHA * (b3[k] + t3[k] + r3[k])) for k in range(-2, 4)}

    v2 = {k: ALPHA * t2[k] + e3[k // 2] for k in range(-4, 8)}
    v2 = run_T(v2, range(-3, 7), 4, 1, inside2)
    w2 = run_T(v2, range(-2, 6), 4, 1)
    e2 = {k: inside2(k, w2[k] + ALPHA * (b2[k] + t2[k] + r2[k])) for k in range(-2, 6)}

    inside1, inside0 = masked(8), masked(16)
    spread = {k: jnp.stack([e2[k // 2]] * 2, axis=0) for k in range(-4, 12)}
    v1 = run_T(spread, range(-2, 10), 2, 1, inside1)
    w1 = run_T(v1, range(-1, 9), 2, 1)
    even = (lanes_of((8, 128)) & 1) == 0
    for side, first in ((low, -1), (high, 3)):
        for pair in range(3):
            both = [side(16 + 2 * pair + q) for q in range(2)]
            one = jnp.stack([jnp.where(even, v, pltpu.roll(v, 1, 1)) for v in both], axis=0)
            two = jnp.stack([jnp.where(even, pltpu.roll(v, 127, 1), v) for v in both], axis=0)
            for k, v in ((first + 2 * pair, one), (first + 2 * pair + 1, two)):
                w1[k] = w1[k] + v
    e1 = {k: inside1(k, w1[k] + own1_ref[k + 1]) for k in range(-1, 9)}

    def prolonged(k):
        v = e1[k // 2]
        return jnp.stack([v[0], v[0], v[1], v[1]], axis=0)

    p1 = Held(p1_ref, -1)
    wide = {k: prolonged(k) for k in range(-2, 18)}
    hold_T(wide, p1, range(-1, 17), 1, inside0)
    for k in range(16):
        v = smooth(p1[k - 1], p1[k], p1[k + 1], 1) + own0_ref[k]
        if k < 4:
            v = v + low(pl.ds(4 * k, 4))
        if k >= 12:
            v = v + high(pl.ds(4 * (k - 12), 4))
        for q in range(4):
            pot_ref[k, pl.ds(q, 8, stride=4), :] = v[q]
        if k % 4 == 3:
            part = pl.ds(k - 3, 4)
            copies.append(pltpu.make_async_copy(pot_ref.at[part], pot_hbm.at[part], sems.at[k // 4]))
            copies[-1].start()
    for copy in copies:
        copy.wait()


def final_part(*operands):
    vmem = pl.BlockSpec(memory_space=pltpu.VMEM)
    hbm = pl.BlockSpec(memory_space=pltpu.HBM)
    shape = lambda *s: jax.ShapeDtypeStruct(s, F32)
    return pl.pallas_call(
        final_kernel,
        out_shape=(shape(16, 32, 128), shape(16, 32, 128)),
        in_specs=[vmem] * 5,
        out_specs=(hbm, hbm),
        scratch_shapes=[
            pltpu.VMEM((18, 4, 8, 128), F32),
            pltpu.VMEM((16, 32, 128), F32), pltpu.VMEM((16, 32, 128), F32),
            pltpu.SemaphoreType.DMA((5,)),
        ],
        compiler_params=pltpu.CompilerParams(vmem_limit_bytes=32 * 2**20),
        name="final",
    )(*operands)


def on_device(orbitals, spin_group, occupation, potential_guess):
    orbitals, spin_group, occupation = (
        pltpu.with_memory_space_constraint(v, pltpu.HBM) for v in (orbitals, spin_group, occupation)
    )
    parts = lax.all_to_all(density(spin_group, occupation, orbitals), "band", 0, 0)
    far, to_send, minus, mine2, *held = far_part(parts, potential_guess)
    rings = []
    for b in range(BANDS):
        half = RING // 2 * (b % 2)
        for first in range(half, DOMS - half, RING):
            rings.append([b * DOMS + first + (ROOT - half + i) % RING for i in range(RING)])
    for first in (0, 4, DOMS - 8, DOMS - 4):
        rings.append([b * DOMS + first + i for b in range(1, BANDS, 2) for i in range(4)])
    mine = lax.all_to_all(
        far.reshape(RING, 9 * 128), ("band", "dom"), 0, 0, axis_index_groups=rings
    ).reshape(9 * RING, 128)

    edges = [
        (b * DOMS + d + 1 - b % 2, b * DOMS + d + b % 2) for b in range(BANDS) for d in range(DOMS - 1)
    ]
    halo = lax.ppermute(to_send, ("band", "dom"), edges)
    own0, own1 = near_part(potential_guess, *held)
    swap = [(b, b ^ 1) for b in range(BANDS)]
    packed = pack(mine, halo, minus)
    swapped = lax.ppermute(packed, "band", swap)
    return final_part(packed, swapped, mine2, own0, own1)


def solution(mesh):
    placed = (P("band", "dom", None, None), P("band"), P("band"), P("dom", None, None))
    return jax.shard_map(
        on_device,
        mesh=mesh,
        in_specs=placed,
        out_specs=(P("dom", None, None), P("dom", None, None)),
        check_vma=False,
    )
```

```python
import functools

import jax
import jax.numpy as jnp
from jax import lax
from jax.experimental import pallas as pl
from jax.experimental.pallas import tpu as pltpu
from jax.sharding import PartitionSpec as P

DEN = 16
BANDS = 8
DOMS = 64
REACH = 7
RING = 16
ROWS = 96
ROOT = 11
ALPHA = 1.0 / 9.0
SOURCE_SCALE = 0.6
F32 = jnp.float32


def lanes_of(shape):
    return lax.broadcasted_iota(jnp.int32, shape, len(shape) - 1)


def rows_of(shape):
    return lax.broadcasted_iota(jnp.int32, shape, len(shape) - 2)


def sides_z(v, step):
    lane = lanes_of(v.shape)
    ax = v.ndim - 1
    left = jnp.where(lane >= step, pltpu.roll(v, step, ax), 0.0)
    right = jnp.where(lane < 128 - step, pltpu.roll(v, 128 - step, ax), 0.0)
    return left + right


def from_below(v, step=1):
    return jnp.where(rows_of(v.shape) >= step, pltpu.roll(v, step, v.ndim - 2), 0.0)


def from_above(v, step=1):
    return jnp.where(rows_of(v.shape) < 8 - step, pltpu.roll(v, 8 - step, v.ndim - 2), 0.0)


def sides_y(v, step):
    if v.ndim == 2:
        return from_below(v, step) + from_above(v, step)
    parts = [v[q] for q in range(v.shape[0])]
    n = len(parts)
    out = []
    for q in range(n):
        lower = parts[q - 1] if q > 0 else from_below(parts[n - 1])
        upper = parts[q + 1] if q < n - 1 else from_above(parts[0])
        out.append(lower + upper)
    return jnp.stack(out, axis=0)


def smooth(low, v, high, zstep, ystep=1):
    around = sides_y(v, ystep) + sides_z(v, zstep)
    if low is not None:
        around = around + low
    if high is not None:
        around = around + high
    return v * (1.0 / 3.0) + around * ALPHA


def pair_z(v, step):
    lane = lanes_of(v.shape)
    ax = v.ndim - 1
    other = jnp.where((lane & step) == 0, pltpu.roll(v, 128 - step, ax), pltpu.roll(v, step, ax))
    return v + other


def pair_y(v, step):
    row = rows_of(v.shape)
    ax = v.ndim - 2
    other = jnp.where((row & step) == 0, pltpu.roll(v, 8 - step, ax), pltpu.roll(v, step, ax))
    return v + other


def run_T(src, planes, zstep, ystep=1, mask=None):
    out = {}
    for k in planes:
        v = src.get(k)
        low, high = src.get(k - 1), src.get(k + 1)
        if v is None:
            edge = low if low is not None else high
            got = edge * ALPHA
        else:
            got = smooth(low, v, high, zstep, ystep)
        out[k] = got if mask is None else mask(k, got)
    return out


class Held:
    def __init__(self, ref, first):
        self.ref, self.first, self.have = ref, first, set()

    def put(self, k, value):
        self.ref[k - self.first] = value
        self.have.add(k)

    def get(self, k):
        return self.ref[k - self.first] if k in self.have else None

    def __getitem__(self, k):
        return self.ref[k - self.first]


def hold_T(src, held, planes, zstep, mask):
    for k in planes:
        v = src.get(k)
        low, high = src.get(k - 1), src.get(k + 1)
        if v is None:
            got = (low if low is not None else high) * ALPHA
        else:
            got = smooth(low, v, high, zstep)
        held.put(k, mask(k, got))


def refine_z(coarse):
    row = lax.broadcasted_iota(jnp.int32, (128, 256), 0)
    col = lax.broadcasted_iota(jnp.int32, (128, 256), 1)
    own = col >> 1
    other = jnp.where((col & 1) == 0, own - 1, own + 1)
    inside = (other >> 6) == (col >> 7)
    matrix = jnp.where(row == own, 0.75, jnp.where((row == other) & inside, 0.25, 0.0))
    return jnp.dot(
        coarse, matrix, precision=lax.Precision.HIGHEST, preferred_element_type=F32
    )


def refine_y(pair):
    first, second = pair
    return jnp.stack(
        [
            0.75 * first + 0.25 * from_below(second),
            0.75 * first + 0.25 * second,
            0.75 * second + 0.25 * first,
            0.75 * second + 0.25 * from_above(first),
        ],
        axis=0,
    )


def refine_x(coarse, k):
    i = k // 2
    other = i - 1 if k % 2 == 0 else i + 1
    total = None
    for j, factor in ((i, 0.75), (other, 0.25)):
        if 0 <= j < 8:
            term = factor * coarse[j]
            total = term if total is None else total + term
    return total


def masks(dom):
    low_flag = jnp.where(dom > 0, 1.0, 0.0).astype(F32)
    high_flag = jnp.where(dom < DOMS - 1, 1.0, 0.0).astype(F32)

    def masked(last):
        def mask(k, v):
            if k < 0:
                return v * low_flag
            if k > last:
                return v * high_flag
            return v
        return mask

    return masked(15), masked(7), masked(3)


def guess_planes(guess_ref):
    def guess(k):
        if not 0 <= k < 16:
            return None
        return jnp.stack([guess_ref[k, pl.ds(q, 8, stride=4), :] for q in range(4)], axis=0)
    return guess


def restricted(r, k):
    total = None
    for fine in (2 * k, 2 * k + 1):
        v = r.get(fine)
        if v is not None:
            total = v if total is None else total + v
    total = jnp.stack([total[0] + total[1], total[2] + total[3]], axis=0)
    return 0.5 * pair_z(total, 1)


def geometric(b, t, r, k, zstep):
    low, v, high = r.get(k - 1), r.get(k), r.get(k + 1)
    if v is None:
        last = (low if low is not None else high) * ALPHA
    else:
        last = smooth(low, v, high, zstep)
    for term in (r.get(k), t.get(k), b.get(k)):
        if term is not None:
            last = last + term
    return last * ALPHA


def copy_all(source, target, count, sems):
    copies = [pltpu.make_async_copy(source, target.at[i], sems.at[i]) for i in range(count)]
    for copy in copies:
        copy.start()
    return copies


def density_kernel(
    spin_hbm, occ_hbm, orb_hbm, part_ref, spin_ref, occ_ref, orb_ref, plane_ref, sems,
):
    loads = [
        pltpu.make_async_copy(spin_hbm, spin_ref, sems.at[8]),
        pltpu.make_async_copy(occ_hbm, occ_ref, sems.at[9]),
    ]
    loads += [pltpu.make_async_copy(orb_hbm.at[k], orb_ref.at[k], sems.at[k]) for k in range(8)]
    for load in loads:
        load.start()
    loads[0].wait()
    loads[1].wait()
    ups, downs = [0.0] * 8, [0.0] * 8
    for k in range(8):
        weight = occ_ref[k].astype(F32) * (0.125 / DEN)
        up = spin_ref[k] == 0
        up, down = jnp.where(up, weight, 0.0), jnp.where(up, 0.0, weight)
        loads[2 + k].wait()
        for x in range(8):
            square = orb_ref[k, x] * orb_ref[k, x]
            ups[x] = ups[x] + up * square
            downs[x] = downs[x] + down * square
    for x in range(8):
        plane_ref[x] = ups[x] + downs[x]
        plane_ref[8 + x] = ups[x] - downs[x]

    def halves(plane):
        return jnp.concatenate(
            [plane_ref[plane, pl.ds(p, 8, stride=2), :] for p in range(2)], axis=-1
        )

    for x in range(8):
        total, difference = halves(x), halves(8 + x)
        for b in range(BANDS):
            part_ref[b, pl.ds(8 * x, 8), :] = total
            if b % 2 == x // 4:
                part_ref[b, pl.ds(64 + 8 * (x % 4), 8), :] = difference


def density(spin_group, occupation, orbitals):
    hbm = pl.BlockSpec(memory_space=pltpu.HBM)
    return pl.pallas_call(
        density_kernel,
        out_shape=jax.ShapeDtypeStruct((BANDS, ROWS, 128), F32),
        in_specs=[hbm] * 3,
        out_specs=pl.BlockSpec(memory_space=pltpu.VMEM),
        scratch_shapes=[
            pltpu.SMEM((8,), jnp.int32), pltpu.SMEM((8,), jnp.int32),
            pltpu.VMEM((8, 8, 16, 64), F32), pltpu.VMEM((16, 16, 64), F32),
            pltpu.SemaphoreType.DMA((10,)),
        ],
        compiler_params=pltpu.CompilerParams(vmem_limit_bytes=40 * 2**20),
        name="density",
    )(spin_group, occupation, orbitals)


def plane_pair(wide, plane):
    rows = wide[8 * plane:8 * plane + 8]
    return rows[:, :128], rows[:, 128:]


def far_kernel(
    part_ref, guess_ref, far_ref, halo_ref, minus_ref, b2_ref,
    d_ref, t_ref, r_ref, b1_ref, t1_ref, r1_ref, sum_ref,
):
    inside0, inside1, inside2 = masks(lax.axis_index("dom"))
    for i in range(ROWS // 16):
        rows = pl.ds(16 * i, 16)
        total = part_ref[0, rows, :]
        for band in range(1, BANDS):
            total = total + part_ref[band, rows, :]
        sum_ref[rows, :] = total
    wide = refine_z(sum_ref[...])
    plus = [SOURCE_SCALE * refine_y(plane_pair(wide, x)) for x in range(8)]
    for j in range(4):
        minus_ref[2 * j], minus_ref[2 * j + 1] = plane_pair(wide, 8 + j)
    d, t, r = Held(d_ref, -1), Held(t_ref, -2), Held(r_ref, -3)
    guess = guess_planes(guess_ref)
    for k in range(-1, 17):
        v, low, high = guess(k), guess(k - 1), guess(k + 1)
        around = None
        if v is not None:
            around = sides_y(v, 1) + sides_z(v, 1)
        for side in (low, high):
            if side is not None:
                around = side if around is None else around + side
        if v is not None:
            around = around - 6.0 * v
        d.put(k, inside0(k, refine_x(plus, k) + around))
    hold_T(d, t, range(-2, 18), 1, inside0)
    hold_T(t, r, range(-3, 19), 1, inside0)
    b1, t1, r1 = Held(b1_ref, -2), Held(t1_ref, -3), Held(r1_ref, -4)
    for k in range(-2, 10):
        b1.put(k, restricted(r, k))
    hold_T(b1, t1, range(-3, 11), 2, inside1)
    hold_T(t1, r1, range(-4, 12), 2, inside1)
    b2 = {}
    for k in range(-2, 6):
        v = r1[2 * k] + r1[2 * k + 1]
        b2[k] = 0.5 * pair_z(v[0] + v[1], 2)
        b2_ref[k + 2] = b2[k]
    t2 = run_T(b2, range(-3, 7), 4, mask=inside2)
    r2 = run_T(t2, range(-4, 8), 4, mask=inside2)
    b3 = [0.5 * pair_y(pair_z(r2[2 * k] + r2[2 * k + 1], 4), 1) for k in range(-2, 4)]

    lane, row = lanes_of((8, 128)), rows_of((8, 128))
    parity = row & 1
    common = b3[0]
    for n in range(1, 4):
        here = ((lane & 7) == 3 + 4 * (n % 2)) & (parity == n // 2)
        common = jnp.where(here, b3[n], common)
    above, below = common, common
    for p in range(3):
        above = jnp.where((lane & 3) == p, b2[3 + p], above)
        below = jnp.where((lane & 3) == p, b2[p - 2], below)
    line = lanes_of((1, 128)) & 7
    last = b3[4][0:1]
    for n in (4, 5):
        for y in range(4):
            last = jnp.where(line == 4 * (n - 4) + y, b3[n][2 * y:2 * y + 1], last)
    core = lax.axis_index("band") % 2
    half = RING // 2 * core
    me = (lax.axis_index("dom") + half) % RING
    for i in range(RING):
        target = (ROOT - half + i) % RING
        far_ref[pl.ds(9 * i, 8), :] = jnp.where(target > me, above, below)
        far_ref[pl.ds(9 * i + 8, 1), :] = last

    for group in range(2):
        packed = b2[4 * group - 2]
        for p in range(1, 4):
            packed = jnp.where((lane & 3) == p, b2[4 * group - 2 + p], packed)
        halo_ref[26 + group] = packed

    even = (lane & 1) == 0

    def edges(first0, first1, plane):
        for k in range(4):
            halo_ref[pl.ds(4 * k, 4)] = geometric(d, t, r, first0 + k, 1)
        for pair in range(3):
            one = geometric(b1, t1, r1, first1 + 2 * pair, 2)
            two = geometric(b1, t1, r1, first1 + 2 * pair + 1, 2)
            for q in range(2):
                halo_ref[16 + 2 * pair + q] = jnp.where(even, one[q], two[q])
        halo_ref[pl.ds(22, 4)] = 0.25 * refine_y((minus_ref[2 * plane], minus_ref[2 * plane + 1]))

    @pl.when(core == 0)
    def _():
        edges(-4, -5, 0)

    @pl.when(core == 1)
    def _():
        edges(16, 7, 3)


def far_part(parts, guess):
    vmem = pl.BlockSpec(memory_space=pltpu.VMEM)
    shape = lambda *s: jax.ShapeDtypeStruct(s, F32)
    return pl.pallas_call(
        far_kernel,
        out_shape=(
            shape(9 * RING, 128), shape(28, 8, 128), shape(8, 8, 128), shape(8, 8, 128),
            shape(18, 4, 8, 128), shape(20, 4, 8, 128), shape(22, 4, 8, 128),
            shape(12, 2, 8, 128), shape(14, 2, 8, 128), shape(16, 2, 8, 128),
        ),
        in_specs=[vmem, vmem],
        out_specs=(vmem,) * 10,
        scratch_shapes=[pltpu.VMEM((ROWS, 128), F32)],
        compiler_params=pltpu.CompilerParams(vmem_limit_bytes=32 * 2**20),
        name="far",
    )(parts, guess)


class Given(Held):
    def __init__(self, ref, first):
        super().__init__(ref, first)
        self.have = set(range(first, first + ref.shape[0]))


def near_kernel(
    guess_ref, d_ref, t_ref, r_ref, b1_ref, t1_ref, r1_ref, own0_ref, own1_ref,
):
    d, t, r = Given(d_ref, -1), Given(t_ref, -2), Given(r_ref, -3)
    b1, t1, r1 = Given(b1_ref, -2), Given(t1_ref, -3), Given(r1_ref, -4)
    guess = guess_planes(guess_ref)
    for k in range(-1, 9):
        own1_ref[k + 1] = geometric(b1, t1, r1, k, 2)
    for k in range(16):
        own0_ref[k] = geometric(d, t, r, k, 1) + guess(k)


def near_part(guess, *held):
    vmem = pl.BlockSpec(memory_space=pltpu.VMEM)
    shape = lambda *s: jax.ShapeDtypeStruct(s, F32)
    return pl.pallas_call(
        near_kernel,
        out_shape=(shape(16, 4, 8, 128), shape(10, 2, 8, 128)),
        in_specs=[vmem] * 7,
        out_specs=(vmem,) * 2,
        compiler_params=pltpu.CompilerParams(vmem_limit_bytes=32 * 2**20),
        cost_estimate=pl.CostEstimate(flops=10**6, bytes_accessed=2**20, transcendentals=0),
        name="near",
    )(guess, *held)


def pack_kernel(mine_ref, halo_ref, minus_ref, out_ref):
    out_ref[pl.ds(0, 28)] = halo_ref[...]
    out_ref[pl.ds(28, 8)] = minus_ref[...]
    for i in range(RING):
        out_ref[36 + 2 * i] = mine_ref[pl.ds(9 * i, 8), :]
        out_ref[37 + 2 * i, pl.ds(0, 1), :] = mine_ref[pl.ds(9 * i + 8, 1), :]


def pack(mine, halo, minus):
    vmem = pl.BlockSpec(memory_space=pltpu.VMEM)
    return pl.pallas_call(
        pack_kernel,
        out_shape=jax.ShapeDtypeStruct((36 + 2 * RING, 8, 128), F32),
        in_specs=[vmem] * 3,
        out_specs=vmem,
        compiler_params=pltpu.CompilerParams(vmem_limit_bytes=32 * 2**20),
        name="pack",
    )(mine, halo, minus)


def final_kernel(
    packed_ref, swapped_ref, mine2_ref, own0_ref, own1_ref, pot_hbm, mag_hbm,
    p1_ref, pot_ref, mag_ref, sems,
):
    dom = lax.axis_index("dom")
    lower = lax.axis_index("band") % 2 == 0

    def high(i):
        return jnp.where(lower, packed_ref[i], swapped_ref[i])

    def low(i):
        return jnp.where(lower, swapped_ref[i], packed_ref[i])

    minus = []
    for x in range(8):
        j = x % 4
        pair = []
        for p in range(2):
            own = packed_ref[28 + 2 * j + p]
            pair.append(jnp.where(lower == (x < 4), own, swapped_ref[28 + 2 * j + p]))
        minus.append(refine_y(pair))
    for k in range(16):
        mag = refine_x(minus, k)
        if k == 0:
            mag = mag + low(pl.ds(22, 4))
        if k == 15:
            mag = mag + high(pl.ds(22, 4))
        for q in range(4):
            mag_ref[k, pl.ds(q, 8, stride=4), :] = mag[q]
    copies = [pltpu.make_async_copy(mag_ref, mag_hbm, sems.at[4])]
    copies[0].start()

    def masked(count):
        first, last = -dom * count, (DOMS - dom) * count
        def mask(k, v):
            if 0 <= k < count:
                return v
            ok = (k >= first) & (k < last)
            return jnp.where(ok, v, 0.0)
        return mask

    lane, row = lanes_of((8, 128)), rows_of((8, 128))
    spot = dom % RING
    first = dom - spot
    other_first = first + jnp.where(spot < RING // 2, -(RING // 2), RING // 2)
    body, last = {}, {}
    for step in range(-REACH, REACH + 1):
        wanted = dom + step
        at = wanted - first
        aligned = (at >= 0) & (at < RING)
        at = jnp.clip(jnp.where(aligned, at, wanted - other_first), 0, RING - 1)
        slot = (at + RING - jnp.where(aligned, ROOT, ROOT - RING // 2)) % RING
        there = (wanted >= 0) & (wanted < DOMS)
        for part, ref in ((0, body), (1, last)):
            rows = pl.ds(0, 1 if part else 8)
            v = jnp.where(
                aligned == lower,
                packed_ref[36 + 2 * slot + part, rows, :],
                swapped_ref[36 + 2 * slot + part, rows, :],
            )
            ref[step] = jnp.where(there, v, 0.0)

    def unpack4(v, p):
        v = jnp.where((lane & 3) == p, v, 0.0)
        v = v + pltpu.roll(v, 1 if p % 2 == 0 else 127, 1)
        return v + pltpu.roll(v, 2 if p < 2 else 126, 1)

    inside2, inside3, inside4 = masked(4), masked(2), masked(1)
    b2 = {k: mine2_ref[k + 2] for k in range(-2, 6)}
    tiles = (
        (-5, 3, pltpu.roll(low(26), 127, 1) + body[-2]), (-2, 4, low(27)),
        (2, 4, high(26)), (6, 3, high(27) + body[2]),
    )
    for start, count, tile in tiles:
        for p in range(count):
            k, v = start + p, unpack4(tile, p)
            b2[k] = b2[k] + v if k in b2 else v
    t2 = run_T(b2, range(-4, 8), 4, mask=inside2)
    r2 = run_T(t2, range(-2, 6), 4)

    b3 = {}
    for pair in range(-6, 7):
        both = jnp.where((row & 1) == 0, body[pair + 1], body[pair])
        both = pair_y(jnp.where((lane & 3) == 3, both, 0.0), 1)
        tail = jnp.broadcast_to(last[pair - 1], (8, 128))
        for n in range(2):
            v = jnp.where((lane & 7) == 4 * n + 3, both, 0.0)
            v = v + jnp.where((lane & 7) == 4 * n + (row >> 1), tail, 0.0)
            b3[2 * pair + n] = pair_z(pair_z(pair_z(v, 1), 2), 4)
    t3 = run_T(b3, range(-11, 13), 8, 2, inside3)
    r3 = run_T(t3, range(-10, 12), 8, 2)

    b4 = {}
    for k in range(-5, 6):
        v = pair_y(pair_z(r3[2 * k] + r3[2 * k + 1], 8), 2)
        b4[k] = inside4(k, 0.5 * v)
    t4 = run_T(b4, range(-4, 5), 16, 4, inside4)
    r4 = run_T(t4, range(-3, 4), 16, 4, inside4)
    u4 = run_T(r4, range(-2, 3), 16, 4)
    e4 = {k: ALPHA * (b4[k] + t4[k] + r4[k] + u4[k]) for k in range(-2, 3)}
    e4 = {k: inside4(k, v) for k, v in e4.items()}

    v3 = {k: ALPHA * t3[k] + e4[k // 2] for k in range(-4, 6)}
    v3 = run_T(v3, range(-3, 5), 8, 2, inside3)
    w3 = run_T(v3, range(-2, 4), 8, 2)
    e3 = {k: inside3(k, w3[k] + ALPHA * (b3[k] + t3[k] + r3[k])) for k in range(-2, 4)}

    v2 = {k: ALPHA * t2[k] + e3[k // 2] for k in range(-4, 8)}
    v2 = run_T(v2, range(-3, 7), 4, 1, inside2)
    w2 = run_T(v2, range(-2, 6), 4, 1)
    e2 = {k: inside2(k, w2[k] + ALPHA * (b2[k] + t2[k] + r2[k])) for k in range(-2, 6)}

    inside1, inside0 = masked(8), masked(16)
    sides, base = {}, {}
    for i in range(-1, 5):
        v = e2[i]
        sides[i] = sides_z(v, 2) + v + jnp.stack([from_below(v), from_above(v)], axis=0)
        base[i] = v * (1.0 / 3.0) + sides[i] * ALPHA
    v1, w1 = {}, {}
    for k in range(-2, 10):
        i, j = k // 2, k // 2 + (1 if k % 2 else -1)
        v1[k] = inside1(k, base[i] + (e2[i] + e2[j]) * ALPHA)
    for i in range(-1, 5):
        around = sides_y(base[i], 1) + sides_z(base[i], 2)
        for k in (2 * i, 2 * i + 1):
            j = i + (1 if k % 2 else -1)
            if -1 <= k < 9:
                total = around + (sides[i] + sides[j]) * ALPHA + v1[k - 1] + v1[k + 1]
                w1[k] = v1[k] * (1.0 / 3.0) + total * ALPHA
    even = (lanes_of((8, 128)) & 1) == 0
    for side, first in ((low, -1), (high, 3)):
        for pair in range(3):
            both = [side(16 + 2 * pair + q) for q in range(2)]
            one = jnp.stack([jnp.where(even, v, pltpu.roll(v, 1, 1)) for v in both], axis=0)
            two = jnp.stack([jnp.where(even, pltpu.roll(v, 127, 1), v) for v in both], axis=0)
            for k, v in ((first + 2 * pair, one), (first + 2 * pair + 1, two)):
                w1[k] = w1[k] + v
    e1 = {k: inside1(k, w1[k] + own1_ref[k + 1]) for k in range(-1, 9)}

    wide, sides, base = {}, {}, {}
    for i in range(-1, 9):
        one, two = e1[i][0], e1[i][1]
        wide[i] = jnp.stack([one, one, two, two], axis=0)
        z_one, z_two, both = sides_z(one, 1), sides_z(two, 1), one + two
        sides[i] = jnp.stack(
            [
                z_one + one + from_below(two), z_one + both,
                z_two + both, z_two + two + from_above(one),
            ],
            axis=0,
        )
        base[i] = wide[i] * (1.0 / 3.0) + sides[i] * ALPHA
    p1 = Held(p1_ref, -1)
    for k in range(-1, 17):
        i, j = k // 2, k // 2 + (1 if k % 2 else -1)
        p1.put(k, inside0(k, base[i] + (wide[i] + wide[j]) * ALPHA))
    for k in range(16):
        i, j = k // 2, k // 2 + (1 if k % 2 else -1)
        if k % 2 == 0:
            around = sides_y(base[i], 1) + sides_z(base[i], 1)
        total = around + (sides[i] + sides[j]) * ALPHA + p1[k - 1] + p1[k + 1]
        v = p1[k] * (1.0 / 3.0) + total * ALPHA + own0_ref[k]
        if k < 4:
            v = v + low(pl.ds(4 * k, 4))
        if k >= 12:
            v = v + high(pl.ds(4 * (k - 12), 4))
        for q in range(4):
            pot_ref[k, pl.ds(q, 8, stride=4), :] = v[q]
        if k % 4 == 3:
            part = pl.ds(k - 3, 4)
            copies.append(pltpu.make_async_copy(pot_ref.at[part], pot_hbm.at[part], sems.at[k // 4]))
            copies[-1].start()
    for copy in copies:
        copy.wait()


def final_part(*operands):
    vmem = pl.BlockSpec(memory_space=pltpu.VMEM)
    hbm = pl.BlockSpec(memory_space=pltpu.HBM)
    shape = lambda *s: jax.ShapeDtypeStruct(s, F32)
    return pl.pallas_call(
        final_kernel,
        out_shape=(shape(16, 32, 128), shape(16, 32, 128)),
        in_specs=[vmem] * 5,
        out_specs=(hbm, hbm),
        scratch_shapes=[
            pltpu.VMEM((18, 4, 8, 128), F32),
            pltpu.VMEM((16, 32, 128), F32), pltpu.VMEM((16, 32, 128), F32),
            pltpu.SemaphoreType.DMA((5,)),
        ],
        compiler_params=pltpu.CompilerParams(vmem_limit_bytes=32 * 2**20),
        name="final",
    )(*operands)


def on_device(orbitals, spin_group, occupation, potential_guess):
    orbitals, spin_group, occupation = (
        pltpu.with_memory_space_constraint(v, pltpu.HBM) for v in (orbitals, spin_group, occupation)
    )
    parts = lax.all_to_all(density(spin_group, occupation, orbitals), "band", 0, 0)
    far, to_send, minus, mine2, *held = far_part(parts, potential_guess)
    rings = []
    for b in range(BANDS):
        half = RING // 2 * (b % 2)
        for first in range(half, DOMS - half, RING):
            rings.append([b * DOMS + first + (ROOT - half + i) % RING for i in range(RING)])
    for first in (0, 4, DOMS - 8, DOMS - 4):
        rings.append([b * DOMS + first + i for b in range(1, BANDS, 2) for i in range(4)])
    mine = lax.all_to_all(
        far.reshape(RING, 9 * 128), ("band", "dom"), 0, 0, axis_index_groups=rings
    ).reshape(9 * RING, 128)

    edges = [
        (b * DOMS + d + 1 - b % 2, b * DOMS + d + b % 2) for b in range(BANDS) for d in range(DOMS - 1)
    ]
    halo = lax.ppermute(to_send, ("band", "dom"), edges)
    own0, own1 = near_part(potential_guess, *held)
    swap = [(b, b ^ 1) for b in range(BANDS)]
    packed = pack(mine, halo, minus)
    swapped = lax.ppermute(packed, "band", swap)
    return final_part(packed, swapped, mine2, own0, own1)


def solution(mesh):
    placed = (P("band", "dom", None, None), P("band"), P("band"), P("dom", None, None))
    return jax.shard_map(
        on_device,
        mesh=mesh,
        in_specs=placed,
        out_specs=(P("dom", None, None), P("dom", None, None)),
        check_vma=False,
    )
```

```python
import functools

import jax
import jax.numpy as jnp
from jax import lax
from jax.experimental import pallas as pl
from jax.experimental.pallas import tpu as pltpu
from jax.sharding import PartitionSpec as P

DEN = 16
BANDS = 8
DOMS = 64
REACH = 7
RING = 16
ROWS = 96
ROOT = 11
ALPHA = 1.0 / 9.0
SOURCE_SCALE = 0.6
F32 = jnp.float32


def lanes_of(shape):
    return lax.broadcasted_iota(jnp.int32, shape, len(shape) - 1)


def rows_of(shape):
    return lax.broadcasted_iota(jnp.int32, shape, len(shape) - 2)


def sides_z(v, step):
    lane = lanes_of(v.shape)
    ax = v.ndim - 1
    left = jnp.where(lane >= step, pltpu.roll(v, step, ax), 0.0)
    right = jnp.where(lane < 128 - step, pltpu.roll(v, 128 - step, ax), 0.0)
    return left + right


def from_below(v, step=1):
    return jnp.where(rows_of(v.shape) >= step, pltpu.roll(v, step, v.ndim - 2), 0.0)


def from_above(v, step=1):
    return jnp.where(rows_of(v.shape) < 8 - step, pltpu.roll(v, 8 - step, v.ndim - 2), 0.0)


def sides_y(v, step):
    if v.ndim == 2:
        return from_below(v, step) + from_above(v, step)
    parts = [v[q] for q in range(v.shape[0])]
    n = len(parts)
    out = []
    for q in range(n):
        lower = parts[q - 1] if q > 0 else from_below(parts[n - 1])
        upper = parts[q + 1] if q < n - 1 else from_above(parts[0])
        out.append(lower + upper)
    return jnp.stack(out, axis=0)


def smooth(low, v, high, zstep, ystep=1):
    around = sides_y(v, ystep) + sides_z(v, zstep)
    if low is not None:
        around = around + low
    if high is not None:
        around = around + high
    return v * (1.0 / 3.0) + around * ALPHA


def pair_z(v, step):
    lane = lanes_of(v.shape)
    ax = v.ndim - 1
    other = jnp.where((lane & step) == 0, pltpu.roll(v, 128 - step, ax), pltpu.roll(v, step, ax))
    return v + other


def pair_y(v, step):
    row = rows_of(v.shape)
    ax = v.ndim - 2
    other = jnp.where((row & step) == 0, pltpu.roll(v, 8 - step, ax), pltpu.roll(v, step, ax))
    return v + other


def run_T(src, planes, zstep, ystep=1, mask=None):
    out = {}
    for k in planes:
        v = src.get(k)
        low, high = src.get(k - 1), src.get(k + 1)
        if v is None:
            edge = low if low is not None else high
            got = edge * ALPHA
        else:
            got = smooth(low, v, high, zstep, ystep)
        out[k] = got if mask is None else mask(k, got)
    return out


class Held:
    def __init__(self, ref, first):
        self.ref, self.first, self.have = ref, first, set()

    def put(self, k, value):
        self.ref[k - self.first] = value
        self.have.add(k)

    def get(self, k):
        return self.ref[k - self.first] if k in self.have else None

    def __getitem__(self, k):
        return self.ref[k - self.first]


def hold_T(src, held, planes, zstep, mask):
    for k in planes:
        v = src.get(k)
        low, high = src.get(k - 1), src.get(k + 1)
        if v is None:
            got = (low if low is not None else high) * ALPHA
        else:
            got = smooth(low, v, high, zstep)
        held.put(k, mask(k, got))


def refine_z(coarse):
    row = lax.broadcasted_iota(jnp.int32, (128, 256), 0)
    col = lax.broadcasted_iota(jnp.int32, (128, 256), 1)
    own = col >> 1
    other = jnp.where((col & 1) == 0, own - 1, own + 1)
    inside = (other >> 6) == (col >> 7)
    matrix = jnp.where(row == own, 0.75, jnp.where((row == other) & inside, 0.25, 0.0))
    return jnp.dot(
        coarse, matrix, precision=lax.Precision.HIGHEST, preferred_element_type=F32
    )


def refine_y(pair):
    first, second = pair
    return jnp.stack(
        [
            0.75 * first + 0.25 * from_below(second),
            0.75 * first + 0.25 * second,
            0.75 * second + 0.25 * first,
            0.75 * second + 0.25 * from_above(first),
        ],
        axis=0,
    )


def refine_x(coarse, k):
    i = k // 2
    other = i - 1 if k % 2 == 0 else i + 1
    total = None
    for j, factor in ((i, 0.75), (other, 0.25)):
        if 0 <= j < 8:
            term = factor * coarse[j]
            total = term if total is None else total + term
    return total


def masks(dom):
    low_flag = jnp.where(dom > 0, 1.0, 0.0).astype(F32)
    high_flag = jnp.where(dom < DOMS - 1, 1.0, 0.0).astype(F32)

    def masked(last):
        def mask(k, v):
            if k < 0:
                return v * low_flag
            if k > last:
                return v * high_flag
            return v
        return mask

    return masked(15), masked(7), masked(3)


def guess_planes(guess_ref):
    def guess(k):
        if not 0 <= k < 16:
            return None
        return jnp.stack([guess_ref[k, pl.ds(q, 8, stride=4), :] for q in range(4)], axis=0)
    return guess


def restricted(r, k):
    total = None
    for fine in (2 * k, 2 * k + 1):
        v = r.get(fine)
        if v is not None:
            total = v if total is None else total + v
    total = jnp.stack([total[0] + total[1], total[2] + total[3]], axis=0)
    return 0.5 * pair_z(total, 1)


def geometric(b, t, r, k, zstep):
    low, v, high = r.get(k - 1), r.get(k), r.get(k + 1)
    if v is None:
        last = (low if low is not None else high) * ALPHA
    else:
        last = smooth(low, v, high, zstep)
    for term in (r.get(k), t.get(k), b.get(k)):
        if term is not None:
            last = last + term
    return last * ALPHA


def copy_all(source, target, count, sems):
    copies = [pltpu.make_async_copy(source, target.at[i], sems.at[i]) for i in range(count)]
    for copy in copies:
        copy.start()
    return copies


def density_kernel(
    spin_hbm, occ_hbm, orb_hbm, part_ref, spin_ref, occ_ref, orb_ref, plane_ref, sems,
):
    loads = [
        pltpu.make_async_copy(spin_hbm, spin_ref, sems.at[8]),
        pltpu.make_async_copy(occ_hbm, occ_ref, sems.at[9]),
    ]
    loads += [pltpu.make_async_copy(orb_hbm.at[k], orb_ref.at[k], sems.at[k]) for k in range(8)]
    for load in loads:
        load.start()
    loads[0].wait()
    loads[1].wait()
    ups, downs = [0.0] * 8, [0.0] * 8
    for k in range(8):
        weight = occ_ref[k].astype(F32) * (0.125 / DEN)
        up = spin_ref[k] == 0
        up, down = jnp.where(up, weight, 0.0), jnp.where(up, 0.0, weight)
        loads[2 + k].wait()
        for x in range(8):
            square = orb_ref[k, x] * orb_ref[k, x]
            ups[x] = ups[x] + up * square
            downs[x] = downs[x] + down * square
    for x in range(8):
        plane_ref[x] = ups[x] + downs[x]
        plane_ref[8 + x] = ups[x] - downs[x]

    def halves(plane):
        return jnp.concatenate(
            [plane_ref[plane, pl.ds(p, 8, stride=2), :] for p in range(2)], axis=-1
        )

    for x in range(8):
        total, difference = halves(x), halves(8 + x)
        for b in range(BANDS):
            part_ref[b, pl.ds(8 * x, 8), :] = total
            if b % 2 == x // 4:
                part_ref[b, pl.ds(64 + 8 * (x % 4), 8), :] = difference


def density(spin_group, occupation, orbitals):
    hbm = pl.BlockSpec(memory_space=pltpu.HBM)
    return pl.pallas_call(
        density_kernel,
        out_shape=jax.ShapeDtypeStruct((BANDS, ROWS, 128), F32),
        in_specs=[hbm] * 3,
        out_specs=pl.BlockSpec(memory_space=pltpu.VMEM),
        scratch_shapes=[
            pltpu.SMEM((8,), jnp.int32), pltpu.SMEM((8,), jnp.int32),
            pltpu.VMEM((8, 8, 16, 64), F32), pltpu.VMEM((16, 16, 64), F32),
            pltpu.SemaphoreType.DMA((10,)),
        ],
        compiler_params=pltpu.CompilerParams(vmem_limit_bytes=40 * 2**20),
        name="density",
    )(spin_group, occupation, orbitals)


def plane_pair(wide, plane):
    rows = wide[8 * plane:8 * plane + 8]
    return rows[:, :128], rows[:, 128:]


def far_kernel(
    part_ref, guess_ref, far_hbm, halo_ref, minus_ref, b2_ref,
    d_ref, t_ref, r_ref, b1_ref, t1_ref, r1_ref, sum_ref, far_ref, sem,
):
    inside0, inside1, inside2 = masks(lax.axis_index("dom"))
    for i in range(ROWS // 16):
        rows = pl.ds(16 * i, 16)
        total = part_ref[0, rows, :]
        for band in range(1, BANDS):
            total = total + part_ref[band, rows, :]
        sum_ref[rows, :] = total
    wide = refine_z(sum_ref[...])
    plus = [SOURCE_SCALE * refine_y(plane_pair(wide, x)) for x in range(8)]
    for j in range(4):
        minus_ref[2 * j], minus_ref[2 * j + 1] = plane_pair(wide, 8 + j)
    d, t, r = Held(d_ref, -1), Held(t_ref, -2), Held(r_ref, -3)
    guess = guess_planes(guess_ref)
    for k in range(-1, 17):
        v, low, high = guess(k), guess(k - 1), guess(k + 1)
        around = None
        if v is not None:
            around = sides_y(v, 1) + sides_z(v, 1)
        for side in (low, high):
            if side is not None:
                around = side if around is None else around + side
        if v is not None:
            around = around - 6.0 * v
        d.put(k, inside0(k, refine_x(plus, k) + around))
    hold_T(d, t, range(-2, 18), 1, inside0)
    hold_T(t, r, range(-3, 19), 1, inside0)
    b1, t1, r1 = Held(b1_ref, -2), Held(t1_ref, -3), Held(r1_ref, -4)
    for k in range(-2, 10):
        b1.put(k, restricted(r, k))
    hold_T(b1, t1, range(-3, 11), 2, inside1)
    hold_T(t1, r1, range(-4, 12), 2, inside1)
    b2 = {}
    for k in range(-2, 6):
        v = r1[2 * k] + r1[2 * k + 1]
        b2[k] = 0.5 * pair_z(v[0] + v[1], 2)
        b2_ref[k + 2] = b2[k]
    t2 = run_T(b2, range(-3, 7), 4, mask=inside2)
    r2 = run_T(t2, range(-4, 8), 4, mask=inside2)
    b3 = [0.5 * pair_y(pair_z(r2[2 * k] + r2[2 * k + 1], 4), 1) for k in range(-2, 4)]

    lane, row = lanes_of((8, 128)), rows_of((8, 128))
    parity = row & 1
    common = b3[0]
    for n in range(1, 4):
        here = ((lane & 7) == 3 + 4 * (n % 2)) & (parity == n // 2)
        common = jnp.where(here, b3[n], common)
    above, below = common, common
    for p in range(3):
        above = jnp.where((lane & 3) == p, b2[3 + p], above)
        below = jnp.where((lane & 3) == p, b2[p - 2], below)
    line = lanes_of((1, 128)) & 7
    last = b3[4][0:1]
    for n in (4, 5):
        for y in range(4):
            last = jnp.where(line == 4 * (n - 4) + y, b3[n][2 * y:2 * y + 1], last)
    core = lax.axis_index("band") % 2
    half = RING // 2 * core
    me = (lax.axis_index("dom") + half) % RING
    for i in range(RING):
        target = (ROOT - half + i) % RING
        far_ref[pl.ds(9 * i, 8), :] = jnp.where(target > me, above, below)
        far_ref[pl.ds(9 * i + 8, 1), :] = last
    copy = pltpu.make_async_copy(far_ref, far_hbm, sem)
    copy.start()

    for group in range(2):
        packed = b2[4 * group - 2]
        for p in range(1, 4):
            packed = jnp.where((lane & 3) == p, b2[4 * group - 2 + p], packed)
        halo_ref[24 + group] = packed

    even = (lane & 1) == 0

    def edges(first0, first1, plane):
        for k in range(4):
            halo_ref[pl.ds(4 * k, 4)] = geometric(d, t, r, first0 + k, 1)
        for pair in range(3):
            one = geometric(b1, t1, r1, first1 + 2 * pair, 2)
            two = geometric(b1, t1, r1, first1 + 2 * pair + 1, 2)
            for q in range(2):
                halo_ref[16 + 2 * pair + q] = jnp.where(even, one[q], two[q])
        halo_ref[22], halo_ref[23] = minus_ref[2 * plane], minus_ref[2 * plane + 1]

    @pl.when(core == 0)
    def _():
        edges(-4, -5, 0)

    @pl.when(core == 1)
    def _():
        edges(16, 7, 3)

    copy.wait()


def far_part(parts, guess):
    vmem = pl.BlockSpec(memory_space=pltpu.VMEM)
    shape = lambda *s: jax.ShapeDtypeStruct(s, F32)
    return pl.pallas_call(
        far_kernel,
        out_shape=(
            shape(9 * RING, 128), shape(26, 8, 128), shape(8, 8, 128), shape(8, 8, 128),
            shape(18, 4, 8, 128), shape(20, 4, 8, 128), shape(22, 4, 8, 128),
            shape(12, 2, 8, 128), shape(14, 2, 8, 128), shape(16, 2, 8, 128),
        ),
        in_specs=[vmem, vmem],
        out_specs=(pl.BlockSpec(memory_space=pltpu.HBM),) + (vmem,) * 9,
        scratch_shapes=[
            pltpu.VMEM((ROWS, 128), F32), pltpu.VMEM((9 * RING, 128), F32), pltpu.SemaphoreType.DMA,
        ],
        compiler_params=pltpu.CompilerParams(vmem_limit_bytes=32 * 2**20),
        name="far",
    )(parts, guess)


class Given(Held):
    def __init__(self, ref, first):
        super().__init__(ref, first)
        self.have = set(range(first, first + ref.shape[0]))


def near_kernel(
    guess_ref, d_ref, t_ref, r_ref, b1_ref, t1_ref, r1_ref, own0_ref, own1_ref,
):
    d, t, r = Given(d_ref, -1), Given(t_ref, -2), Given(r_ref, -3)
    b1, t1, r1 = Given(b1_ref, -2), Given(t1_ref, -3), Given(r1_ref, -4)
    guess = guess_planes(guess_ref)
    for k in range(-1, 9):
        own1_ref[k + 1] = geometric(b1, t1, r1, k, 2)
    for k in range(16):
        own0_ref[k] = geometric(d, t, r, k, 1) + guess(k)


def near_part(guess, *held):
    vmem = pl.BlockSpec(memory_space=pltpu.VMEM)
    shape = lambda *s: jax.ShapeDtypeStruct(s, F32)
    return pl.pallas_call(
        near_kernel,
        out_shape=(shape(16, 4, 8, 128), shape(10, 2, 8, 128)),
        in_specs=[vmem] * 7,
        out_specs=(vmem,) * 2,
        compiler_params=pltpu.CompilerParams(vmem_limit_bytes=32 * 2**20),
        cost_estimate=pl.CostEstimate(flops=10**6, bytes_accessed=2**20, transcendentals=0),
        name="near",
    )(guess, *held)


def pack_kernel(mine_ref, halo_ref, minus_ref, out_ref):
    out_ref[pl.ds(0, 26)] = halo_ref[...]
    out_ref[pl.ds(26, 8)] = minus_ref[...]
    for i in range(RING):
        out_ref[34 + i] = mine_ref[pl.ds(9 * i, 8), :]
        out_ref[50 + i // 8, pl.ds(i % 8, 1), :] = mine_ref[pl.ds(9 * i + 8, 1), :]


def pack(mine, halo, minus):
    vmem = pl.BlockSpec(memory_space=pltpu.VMEM)
    return pl.pallas_call(
        pack_kernel,
        out_shape=jax.ShapeDtypeStruct((52, 8, 128), F32),
        in_specs=[vmem] * 3,
        out_specs=vmem,
        compiler_params=pltpu.CompilerParams(vmem_limit_bytes=32 * 2**20),
        name="pack",
    )(mine, halo, minus)


def final_kernel(
    packed_ref, swapped_ref, mine2_ref, own0_ref, own1_ref, pot_hbm, mag_hbm,
    p1_ref, pot_ref, mag_ref, sems,
):
    dom = lax.axis_index("dom")
    lower = lax.axis_index("band") % 2 == 0

    def high(i):
        return jnp.where(lower, packed_ref[i], swapped_ref[i])

    def low(i):
        return jnp.where(lower, swapped_ref[i], packed_ref[i])

    minus = []
    for x in range(8):
        j = x % 4
        pair = []
        for p in range(2):
            own = packed_ref[26 + 2 * j + p]
            pair.append(jnp.where(lower == (x < 4), own, swapped_ref[26 + 2 * j + p]))
        minus.append(refine_y(pair))
    for k in range(16):
        mag = refine_x(minus, k)
        if k == 0:
            mag = mag + 0.25 * refine_y((low(22), low(23)))
        if k == 15:
            mag = mag + 0.25 * refine_y((high(22), high(23)))
        for q in range(4):
            mag_ref[k, pl.ds(q, 8, stride=4), :] = mag[q]
    copies = [pltpu.make_async_copy(mag_ref, mag_hbm, sems.at[4])]
    copies[0].start()

    def masked(count):
        first, last = -dom * count, (DOMS - dom) * count
        def mask(k, v):
            if 0 <= k < count:
                return v
            ok = (k >= first) & (k < last)
            return jnp.where(ok, v, 0.0)
        return mask

    lane, row = lanes_of((8, 128)), rows_of((8, 128))
    spot = dom % RING
    first = dom - spot
    other_first = first + jnp.where(spot < RING // 2, -(RING // 2), RING // 2)
    body, last = {}, {}
    for step in range(-REACH, REACH + 1):
        wanted = dom + step
        at = wanted - first
        aligned = (at >= 0) & (at < RING)
        at = jnp.clip(jnp.where(aligned, at, wanted - other_first), 0, RING - 1)
        slot = (at + RING - jnp.where(aligned, ROOT, ROOT - RING // 2)) % RING
        there = (wanted >= 0) & (wanted < DOMS)
        places = ((body, 34 + slot, pl.ds(0, 8)), (last, 50 + slot // 8, pl.ds(slot % 8, 1)))
        for ref, tile, rows in places:
            v = jnp.where(aligned == lower, packed_ref[tile, rows, :], swapped_ref[tile, rows, :])
            ref[step] = jnp.where(there, v, 0.0)

    def unpack4(v, p):
        v = jnp.where((lane & 3) == p, v, 0.0)
        v = v + pltpu.roll(v, 1 if p % 2 == 0 else 127, 1)
        return v + pltpu.roll(v, 2 if p < 2 else 126, 1)

    inside2, inside3, inside4 = masked(4), masked(2), masked(1)
    b2 = {k: mine2_ref[k + 2] for k in range(-2, 6)}
    tiles = (
        (-5, 3, pltpu.roll(low(24), 127, 1) + body[-2]), (-2, 4, low(25)),
        (2, 4, high(24)), (6, 3, high(25) + body[2]),
    )
    for start, count, tile in tiles:
        for p in range(count):
            k, v = start + p, unpack4(tile, p)
            b2[k] = b2[k] + v if k in b2 else v
    t2 = run_T(b2, range(-4, 8), 4, mask=inside2)
    r2 = run_T(t2, range(-2, 6), 4)

    b3 = {}
    for pair in range(-6, 7):
        both = jnp.where((row & 1) == 0, body[pair + 1], body[pair])
        both = pair_y(jnp.where((lane & 3) == 3, both, 0.0), 1)
        tail = jnp.broadcast_to(last[pair - 1], (8, 128))
        for n in range(2):
            v = jnp.where((lane & 7) == 4 * n + 3, both, 0.0)
            v = v + jnp.where((lane & 7) == 4 * n + (row >> 1), tail, 0.0)
            b3[2 * pair + n] = pair_z(pair_z(pair_z(v, 1), 2), 4)
    t3 = run_T(b3, range(-11, 13), 8, 2, inside3)
    r3 = run_T(t3, range(-10, 12), 8, 2)

    b4 = {}
    for k in range(-5, 6):
        v = pair_y(pair_z(r3[2 * k] + r3[2 * k + 1], 8), 2)
        b4[k] = inside4(k, 0.5 * v)
    t4 = run_T(b4, range(-4, 5), 16, 4, inside4)
    r4 = run_T(t4, range(-3, 4), 16, 4, inside4)
    u4 = run_T(r4, range(-2, 3), 16, 4)
    e4 = {k: ALPHA * (b4[k] + t4[k] + r4[k] + u4[k]) for k in range(-2, 3)}
    e4 = {k: inside4(k, v) for k, v in e4.items()}

    v3 = {k: ALPHA * t3[k] + e4[k // 2] for k in range(-4, 6)}
    v3 = run_T(v3, range(-3, 5), 8, 2, inside3)
    w3 = run_T(v3, range(-2, 4), 8, 2)
    e3 = {k: inside3(k, w3[k] + ALPHA * (b3[k] + t3[k] + r3[k])) for k in range(-2, 4)}

    v2 = {k: ALPHA * t2[k] + e3[k // 2] for k in range(-4, 8)}
    v2 = run_T(v2, range(-3, 7), 4, 1, inside2)
    w2 = run_T(v2, range(-2, 6), 4, 1)
    e2 = {k: inside2(k, w2[k] + ALPHA * (b2[k] + t2[k] + r2[k])) for k in range(-2, 6)}

    inside1, inside0 = masked(8), masked(16)
    sides, base = {}, {}
    for i in range(-1, 5):
        v = e2[i]
        sides[i] = sides_z(v, 2) + v + jnp.stack([from_below(v), from_above(v)], axis=0)
        base[i] = v * (1.0 / 3.0) + sides[i] * ALPHA
    v1, w1 = {}, {}
    for k in range(-2, 10):
        i, j = k // 2, k // 2 + (1 if k % 2 else -1)
        v1[k] = inside1(k, base[i] + (e2[i] + e2[j]) * ALPHA)
    for i in range(-1, 5):
        around = sides_y(base[i], 1) + sides_z(base[i], 2)
        for k in (2 * i, 2 * i + 1):
            j = i + (1 if k % 2 else -1)
            if -1 <= k < 9:
                total = around + (sides[i] + sides[j]) * ALPHA + v1[k - 1] + v1[k + 1]
                w1[k] = v1[k] * (1.0 / 3.0) + total * ALPHA
    even = (lanes_of((8, 128)) & 1) == 0
    for side, first in ((low, -1), (high, 3)):
        for pair in range(3):
            both = [side(16 + 2 * pair + q) for q in range(2)]
            one = jnp.stack([jnp.where(even, v, pltpu.roll(v, 1, 1)) for v in both], axis=0)
            two = jnp.stack([jnp.where(even, pltpu.roll(v, 127, 1), v) for v in both], axis=0)
            for k, v in ((first + 2 * pair, one), (first + 2 * pair + 1, two)):
                w1[k] = w1[k] + v
    e1 = {k: inside1(k, w1[k] + own1_ref[k + 1]) for k in range(-1, 9)}

    wide, sides, base = {}, {}, {}
    for i in range(-1, 9):
        one, two = e1[i][0], e1[i][1]
        wide[i] = jnp.stack([one, one, two, two], axis=0)
        z_one, z_two, both = sides_z(one, 1), sides_z(two, 1), one + two
        sides[i] = jnp.stack(
            [
                z_one + one + from_below(two), z_one + both,
                z_two + both, z_two + two + from_above(one),
            ],
            axis=0,
        )
        base[i] = wide[i] * (1.0 / 3.0) + sides[i] * ALPHA
    p1 = Held(p1_ref, -1)
    for k in range(-1, 17):
        i, j = k // 2, k // 2 + (1 if k % 2 else -1)
        p1.put(k, inside0(k, base[i] + (wide[i] + wide[j]) * ALPHA))
    for k in range(16):
        i, j = k // 2, k // 2 + (1 if k % 2 else -1)
        if k % 2 == 0:
            around = sides_y(base[i], 1) + sides_z(base[i], 1)
        total = around + (sides[i] + sides[j]) * ALPHA + p1[k - 1] + p1[k + 1]
        v = p1[k] * (1.0 / 3.0) + total * ALPHA + own0_ref[k]
        if k < 4:
            v = v + low(pl.ds(4 * k, 4))
        if k >= 12:
            v = v + high(pl.ds(4 * (k - 12), 4))
        for q in range(4):
            pot_ref[k, pl.ds(q, 8, stride=4), :] = v[q]
        if k % 4 == 3:
            part = pl.ds(k - 3, 4)
            copies.append(pltpu.make_async_copy(pot_ref.at[part], pot_hbm.at[part], sems.at[k // 4]))
            copies[-1].start()
    for copy in copies:
        copy.wait()


def final_part(*operands):
    vmem = pl.BlockSpec(memory_space=pltpu.VMEM)
    hbm = pl.BlockSpec(memory_space=pltpu.HBM)
    shape = lambda *s: jax.ShapeDtypeStruct(s, F32)
    return pl.pallas_call(
        final_kernel,
        out_shape=(shape(16, 32, 128), shape(16, 32, 128)),
        in_specs=[vmem] * 5,
        out_specs=(hbm, hbm),
        scratch_shapes=[
            pltpu.VMEM((18, 4, 8, 128), F32),
            pltpu.VMEM((16, 32, 128), F32), pltpu.VMEM((16, 32, 128), F32),
            pltpu.SemaphoreType.DMA((5,)),
        ],
        compiler_params=pltpu.CompilerParams(vmem_limit_bytes=32 * 2**20),
        name="final",
    )(*operands)


def on_device(orbitals, spin_group, occupation, potential_guess):
    orbitals, spin_group, occupation = (
        pltpu.with_memory_space_constraint(v, pltpu.HBM) for v in (orbitals, spin_group, occupation)
    )
    parts = lax.all_to_all(density(spin_group, occupation, orbitals), "band", 0, 0)
    far, to_send, minus, mine2, *held = far_part(parts, potential_guess)
    rings = []
    for b in range(BANDS):
        half = RING // 2 * (b % 2)
        for first in range(half, DOMS - half, RING):
            rings.append([b * DOMS + first + (ROOT - half + i) % RING for i in range(RING)])
    for first in (0, 4, DOMS - 8, DOMS - 4):
        rings.append([b * DOMS + first + i for b in range(1, BANDS, 2) for i in range(4)])
    mine = lax.all_to_all(
        far.reshape(RING, 9 * 128), ("band", "dom"), 0, 0, axis_index_groups=rings
    ).reshape(9 * RING, 128)

    edges = [
        (b * DOMS + d + 1 - b % 2, b * DOMS + d + b % 2) for b in range(BANDS) for d in range(DOMS - 1)
    ]
    halo = lax.ppermute(to_send, ("band", "dom"), edges)
    own0, own1 = near_part(potential_guess, *held)
    swap = [(b, b ^ 1) for b in range(BANDS)]
    packed = pack(mine, halo, minus)
    swapped = lax.ppermute(packed, "band", swap)
    return final_part(packed, swapped, mine2, own0, own1)


def solution(mesh):
    placed = (P("band", "dom", None, None), P("band"), P("band"), P("dom", None, None))
    return jax.shard_map(
        on_device,
        mesh=mesh,
        in_specs=placed,
        out_specs=(P("dom", None, None), P("dom", None, None)),
        check_vma=False,
    )
```

```python
import functools

import jax
import jax.numpy as jnp
from jax import lax
from jax.experimental import pallas as pl
from jax.experimental.pallas import tpu as pltpu
from jax.sharding import PartitionSpec as P

DEN = 16
BANDS = 8
DOMS = 64
REACH = 7
RING = 16
ROWS = 96
ROOT = 11
ALPHA = 1.0 / 9.0
SOURCE_SCALE = 0.6
F32 = jnp.float32


def lanes_of(shape):
    return lax.broadcasted_iota(jnp.int32, shape, len(shape) - 1)


def rows_of(shape):
    return lax.broadcasted_iota(jnp.int32, shape, len(shape) - 2)


def sides_z(v, step):
    lane = lanes_of(v.shape)
    ax = v.ndim - 1
    left = jnp.where(lane >= step, pltpu.roll(v, step, ax), 0.0)
    right = jnp.where(lane < 128 - step, pltpu.roll(v, 128 - step, ax), 0.0)
    return left + right


def from_below(v, step=1):
    return jnp.where(rows_of(v.shape) >= step, pltpu.roll(v, step, v.ndim - 2), 0.0)


def from_above(v, step=1):
    return jnp.where(rows_of(v.shape) < 8 - step, pltpu.roll(v, 8 - step, v.ndim - 2), 0.0)


def sides_y(v, step):
    if v.ndim == 2:
        return from_below(v, step) + from_above(v, step)
    parts = [v[q] for q in range(v.shape[0])]
    n = len(parts)
    out = []
    for q in range(n):
        lower = parts[q - 1] if q > 0 else from_below(parts[n - 1])
        upper = parts[q + 1] if q < n - 1 else from_above(parts[0])
        out.append(lower + upper)
    return jnp.stack(out, axis=0)


def smooth(low, v, high, zstep, ystep=1):
    around = sides_y(v, ystep) + sides_z(v, zstep)
    if low is not None:
        around = around + low
    if high is not None:
        around = around + high
    return v * (1.0 / 3.0) + around * ALPHA


def pair_z(v, step):
    lane = lanes_of(v.shape)
    ax = v.ndim - 1
    other = jnp.where((lane & step) == 0, pltpu.roll(v, 128 - step, ax), pltpu.roll(v, step, ax))
    return v + other


def pair_y(v, step):
    row = rows_of(v.shape)
    ax = v.ndim - 2
    other = jnp.where((row & step) == 0, pltpu.roll(v, 8 - step, ax), pltpu.roll(v, step, ax))
    return v + other


def run_T(src, planes, zstep, ystep=1, mask=None):
    out = {}
    for k in planes:
        v = src.get(k)
        low, high = src.get(k - 1), src.get(k + 1)
        if v is None:
            edge = low if low is not None else high
            got = edge * ALPHA
        else:
            got = smooth(low, v, high, zstep, ystep)
        out[k] = got if mask is None else mask(k, got)
    return out


class Held:
    def __init__(self, ref, first):
        self.ref, self.first, self.have = ref, first, set()

    def put(self, k, value):
        self.ref[k - self.first] = value
        self.have.add(k)

    def get(self, k):
        return self.ref[k - self.first] if k in self.have else None

    def __getitem__(self, k):
        return self.ref[k - self.first]


def hold_T(src, held, planes, zstep, mask):
    for k in planes:
        v = src.get(k)
        low, high = src.get(k - 1), src.get(k + 1)
        if v is None:
            got = (low if low is not None else high) * ALPHA
        else:
            got = smooth(low, v, high, zstep)
        held.put(k, mask(k, got))


def refine_z(coarse):
    row = lax.broadcasted_iota(jnp.int32, (128, 256), 0)
    col = lax.broadcasted_iota(jnp.int32, (128, 256), 1)
    own = col >> 1
    other = jnp.where((col & 1) == 0, own - 1, own + 1)
    inside = (other >> 6) == (col >> 7)
    matrix = jnp.where(row == own, 0.75, jnp.where((row == other) & inside, 0.25, 0.0))
    return jnp.dot(
        coarse, matrix, precision=lax.Precision.HIGHEST, preferred_element_type=F32
    )


def refine_y(pair):
    first, second = pair
    return jnp.stack(
        [
            0.75 * first + 0.25 * from_below(second),
            0.75 * first + 0.25 * second,
            0.75 * second + 0.25 * first,
            0.75 * second + 0.25 * from_above(first),
        ],
        axis=0,
    )


def refine_x(coarse, k):
    i = k // 2
    other = i - 1 if k % 2 == 0 else i + 1
    total = None
    for j, factor in ((i, 0.75), (other, 0.25)):
        if 0 <= j < 8:
            term = factor * coarse[j]
            total = term if total is None else total + term
    return total


def masks(dom):
    low_flag = jnp.where(dom > 0, 1.0, 0.0).astype(F32)
    high_flag = jnp.where(dom < DOMS - 1, 1.0, 0.0).astype(F32)

    def masked(last):
        def mask(k, v):
            if k < 0:
                return v * low_flag
            if k > last:
                return v * high_flag
            return v
        return mask

    return masked(15), masked(7), masked(3)


def guess_planes(guess_ref):
    def guess(k):
        if not 0 <= k < 16:
            return None
        return jnp.stack([guess_ref[k, pl.ds(q, 8, stride=4), :] for q in range(4)], axis=0)
    return guess


def restricted(r, k):
    total = None
    for fine in (2 * k, 2 * k + 1):
        v = r.get(fine)
        if v is not None:
            total = v if total is None else total + v
    total = jnp.stack([total[0] + total[1], total[2] + total[3]], axis=0)
    return 0.5 * pair_z(total, 1)


def geometric(b, t, r, k, zstep):
    low, v, high = r.get(k - 1), r.get(k), r.get(k + 1)
    if v is None:
        last = (low if low is not None else high) * ALPHA
    else:
        last = smooth(low, v, high, zstep)
    for term in (r.get(k), t.get(k), b.get(k)):
        if term is not None:
            last = last + term
    return last * ALPHA


def copy_all(source, target, count, sems):
    copies = [pltpu.make_async_copy(source, target.at[i], sems.at[i]) for i in range(count)]
    for copy in copies:
        copy.start()
    return copies


def density_kernel(
    spin_hbm, occ_hbm, orb_hbm, part_ref, spin_ref, occ_ref, orb_ref, plane_ref, sems,
):
    loads = [
        pltpu.make_async_copy(spin_hbm, spin_ref, sems.at[8]),
        pltpu.make_async_copy(occ_hbm, occ_ref, sems.at[9]),
    ]
    loads += [pltpu.make_async_copy(orb_hbm.at[k], orb_ref.at[k], sems.at[k]) for k in range(8)]
    for load in loads:
        load.start()
    loads[0].wait()
    loads[1].wait()
    ups, downs = [0.0] * 8, [0.0] * 8
    for k in range(8):
        weight = occ_ref[k].astype(F32) * (0.125 / DEN)
        up = spin_ref[k] == 0
        up, down = jnp.where(up, weight, 0.0), jnp.where(up, 0.0, weight)
        loads[2 + k].wait()
        for x in range(8):
            square = orb_ref[k, x] * orb_ref[k, x]
            ups[x] = ups[x] + up * square
            downs[x] = downs[x] + down * square
    for x in range(8):
        plane_ref[x] = ups[x] + downs[x]
        plane_ref[8 + x] = ups[x] - downs[x]

    def halves(plane):
        return jnp.concatenate(
            [plane_ref[plane, pl.ds(p, 8, stride=2), :] for p in range(2)], axis=-1
        )

    for x in range(8):
        total, difference = halves(x), halves(8 + x)
        for b in range(BANDS):
            part_ref[b, pl.ds(8 * x, 8), :] = total
            if b % 2 == x // 4:
                part_ref[b, pl.ds(64 + 8 * (x % 4), 8), :] = difference


def density(spin_group, occupation, orbitals):
    hbm = pl.BlockSpec(memory_space=pltpu.HBM)
    return pl.pallas_call(
        density_kernel,
        out_shape=jax.ShapeDtypeStruct((BANDS, ROWS, 128), F32),
        in_specs=[hbm] * 3,
        out_specs=pl.BlockSpec(memory_space=pltpu.VMEM),
        scratch_shapes=[
            pltpu.SMEM((8,), jnp.int32), pltpu.SMEM((8,), jnp.int32),
            pltpu.VMEM((8, 8, 16, 64), F32), pltpu.VMEM((16, 16, 64), F32),
            pltpu.SemaphoreType.DMA((10,)),
        ],
        compiler_params=pltpu.CompilerParams(vmem_limit_bytes=40 * 2**20),
        name="density",
    )(spin_group, occupation, orbitals)


def plane_pair(wide, plane):
    rows = wide[8 * plane:8 * plane + 8]
    return rows[:, :128], rows[:, 128:]


def far_kernel(
    part_ref, guess_ref, far_hbm, halo_ref, minus_ref, b2_ref,
    d_ref, t_ref, r_ref, b1_ref, t1_ref, r1_ref, sum_ref, far_ref, sem,
):
    inside0, inside1, inside2 = masks(lax.axis_index("dom"))
    for i in range(ROWS // 16):
        rows = pl.ds(16 * i, 16)
        total = part_ref[0, rows, :]
        for band in range(1, BANDS):
            total = total + part_ref[band, rows, :]
        sum_ref[rows, :] = total
    wide = refine_z(sum_ref[...])
    plus = [SOURCE_SCALE * refine_y(plane_pair(wide, x)) for x in range(8)]
    for j in range(4):
        minus_ref[2 * j], minus_ref[2 * j + 1] = plane_pair(wide, 8 + j)
    d, t, r = Held(d_ref, -1), Held(t_ref, -2), Held(r_ref, -3)
    guess = guess_planes(guess_ref)
    for k in range(-1, 17):
        v, low, high = guess(k), guess(k - 1), guess(k + 1)
        around = None
        if v is not None:
            around = sides_y(v, 1) + sides_z(v, 1)
        for side in (low, high):
            if side is not None:
                around = side if around is None else around + side
        if v is not None:
            around = around - 6.0 * v
        d.put(k, inside0(k, refine_x(plus, k) + around))
    hold_T(d, t, range(-2, 18), 1, inside0)
    hold_T(t, r, range(-3, 19), 1, inside0)
    b1, t1, r1 = Held(b1_ref, -2), Held(t1_ref, -3), Held(r1_ref, -4)
    for k in range(-2, 10):
        b1.put(k, restricted(r, k))
    hold_T(b1, t1, range(-3, 11), 2, inside1)
    hold_T(t1, r1, range(-4, 12), 2, inside1)
    b2 = {}
    for k in range(-2, 6):
        v = r1[2 * k] + r1[2 * k + 1]
        b2[k] = 0.5 * pair_z(v[0] + v[1], 2)
        b2_ref[k + 2] = b2[k]
    t2 = run_T(b2, range(-3, 7), 4, mask=inside2)
    r2 = run_T(t2, range(-4, 8), 4, mask=inside2)
    b3 = [0.5 * pair_y(pair_z(r2[2 * k] + r2[2 * k + 1], 4), 1) for k in range(-2, 4)]

    lane, row = lanes_of((8, 128)), rows_of((8, 128))
    parity = row & 1
    common = b3[0]
    for n in range(1, 4):
        here = ((lane & 7) == 3 + 4 * (n % 2)) & (parity == n // 2)
        common = jnp.where(here, b3[n], common)
    above, below = common, common
    for p in range(3):
        above = jnp.where((lane & 3) == p, b2[3 + p], above)
        below = jnp.where((lane & 3) == p, b2[p - 2], below)
    line = lanes_of((1, 128)) & 7
    last = b3[4][0:1]
    for n in (4, 5):
        for y in range(4):
            last = jnp.where(line == 4 * (n - 4) + y, b3[n][2 * y:2 * y + 1], last)
    core = lax.axis_index("band") % 2
    half = RING // 2 * core
    me = (lax.axis_index("dom") + half) % RING
    for i in range(RING):
        target = (ROOT - half + i) % RING
        far_ref[pl.ds(9 * i, 8), :] = jnp.where(target > me, above, below)
        far_ref[pl.ds(9 * i + 8, 1), :] = last
    copy = pltpu.make_async_copy(far_ref, far_hbm, sem)
    copy.start()

    for group in range(2):
        packed = b2[4 * group - 2]
        for p in range(1, 4):
            packed = jnp.where((lane & 3) == p, b2[4 * group - 2 + p], packed)
        halo_ref[24 + group] = packed

    even = (lane & 1) == 0

    def edges(first0, first1, plane):
        for k in range(4):
            halo_ref[pl.ds(4 * k, 4)] = geometric(d, t, r, first0 + k, 1)
        for pair in range(3):
            one = geometric(b1, t1, r1, first1 + 2 * pair, 2)
            two = geometric(b1, t1, r1, first1 + 2 * pair + 1, 2)
            for q in range(2):
                halo_ref[16 + 2 * pair + q] = jnp.where(even, one[q], two[q])
        halo_ref[22], halo_ref[23] = minus_ref[2 * plane], minus_ref[2 * plane + 1]

    @pl.when(core == 0)
    def _():
        edges(-4, -5, 0)

    @pl.when(core == 1)
    def _():
        edges(16, 7, 3)

    copy.wait()


def far_part(parts, guess):
    vmem = pl.BlockSpec(memory_space=pltpu.VMEM)
    shape = lambda *s: jax.ShapeDtypeStruct(s, F32)
    return pl.pallas_call(
        far_kernel,
        out_shape=(
            shape(9 * RING, 128), shape(26, 8, 128), shape(8, 8, 128), shape(8, 8, 128),
            shape(18, 4, 8, 128), shape(20, 4, 8, 128), shape(22, 4, 8, 128),
            shape(12, 2, 8, 128), shape(14, 2, 8, 128), shape(16, 2, 8, 128),
        ),
        in_specs=[vmem, vmem],
        out_specs=(pl.BlockSpec(memory_space=pltpu.HBM),) + (vmem,) * 9,
        scratch_shapes=[
            pltpu.VMEM((ROWS, 128), F32), pltpu.VMEM((9 * RING, 128), F32), pltpu.SemaphoreType.DMA,
        ],
        compiler_params=pltpu.CompilerParams(vmem_limit_bytes=32 * 2**20),
        name="far",
    )(parts, guess)


class Given(Held):
    def __init__(self, ref, first):
        super().__init__(ref, first)
        self.have = set(range(first, first + ref.shape[0]))


def near_kernel(
    guess_ref, d_ref, t_ref, r_ref, b1_ref, t1_ref, r1_ref, own0_ref, own1_ref,
):
    d, t, r = Given(d_ref, -1), Given(t_ref, -2), Given(r_ref, -3)
    b1, t1, r1 = Given(b1_ref, -2), Given(t1_ref, -3), Given(r1_ref, -4)
    guess = guess_planes(guess_ref)
    for k in range(-1, 9):
        own1_ref[k + 1] = geometric(b1, t1, r1, k, 2)
    for k in range(16):
        own0_ref[k] = geometric(d, t, r, k, 1) + guess(k)


def near_part(guess, *held):
    vmem = pl.BlockSpec(memory_space=pltpu.VMEM)
    shape = lambda *s: jax.ShapeDtypeStruct(s, F32)
    return pl.pallas_call(
        near_kernel,
        out_shape=(shape(16, 4, 8, 128), shape(10, 2, 8, 128)),
        in_specs=[vmem] * 7,
        out_specs=(vmem,) * 2,
        compiler_params=pltpu.CompilerParams(vmem_limit_bytes=32 * 2**20),
        cost_estimate=pl.CostEstimate(flops=10**6, bytes_accessed=2**20, transcendentals=0),
        name="near",
    )(guess, *held)


def pack_kernel(mine_ref, halo_ref, minus_ref, out_ref):
    out_ref[pl.ds(0, 26)] = halo_ref[...]
    out_ref[pl.ds(26, 8)] = minus_ref[...]
    for i in range(RING):
        out_ref[34 + i] = mine_ref[pl.ds(9 * i, 8), :]
        out_ref[50 + i // 8, pl.ds(i % 8, 1), :] = mine_ref[pl.ds(9 * i + 8, 1), :]


def pack(mine, halo, minus):
    vmem = pl.BlockSpec(memory_space=pltpu.VMEM)
    return pl.pallas_call(
        pack_kernel,
        out_shape=jax.ShapeDtypeStruct((52, 8, 128), F32),
        in_specs=[vmem] * 3,
        out_specs=vmem,
        compiler_params=pltpu.CompilerParams(vmem_limit_bytes=32 * 2**20),
        name="pack",
    )(mine, halo, minus)


def final_kernel(
    packed_ref, swapped_ref, mine2_ref, own0_ref, own1_ref, pot_hbm, mag_hbm,
    p1_ref, pot_ref, mag_ref, sems,
):
    dom = lax.axis_index("dom")
    lower = lax.axis_index("band") % 2 == 0

    def high(i):
        return jnp.where(lower, packed_ref[i], swapped_ref[i])

    def low(i):
        return jnp.where(lower, swapped_ref[i], packed_ref[i])

    def masked(count):
        first, last = -dom * count, (DOMS - dom) * count
        def mask(k, v):
            if 0 <= k < count:
                return v
            ok = (k >= first) & (k < last)
            return jnp.where(ok, v, 0.0)
        return mask

    lane, row = lanes_of((8, 128)), rows_of((8, 128))
    spot = dom % RING
    first = dom - spot
    other_first = first + jnp.where(spot < RING // 2, -(RING // 2), RING // 2)
    body, last = {}, {}
    for step in range(-REACH, REACH + 1):
        wanted = dom + step
        at = wanted - first
        aligned = (at >= 0) & (at < RING)
        at = jnp.clip(jnp.where(aligned, at, wanted - other_first), 0, RING - 1)
        slot = (at + RING - jnp.where(aligned, ROOT, ROOT - RING // 2)) % RING
        there = (wanted >= 0) & (wanted < DOMS)
        places = ((body, 34 + slot, pl.ds(0, 8)), (last, 50 + slot // 8, pl.ds(slot % 8, 1)))
        for ref, tile, rows in places:
            v = jnp.where(aligned == lower, packed_ref[tile, rows, :], swapped_ref[tile, rows, :])
            ref[step] = jnp.where(there, v, 0.0)

    def unpack4(v, p):
        v = jnp.where((lane & 3) == p, v, 0.0)
        v = v + pltpu.roll(v, 1 if p % 2 == 0 else 127, 1)
        return v + pltpu.roll(v, 2 if p < 2 else 126, 1)

    inside2, inside3, inside4 = masked(4), masked(2), masked(1)
    b2 = {k: mine2_ref[k + 2] for k in range(-2, 6)}
    tiles = (
        (-5, 3, pltpu.roll(low(24), 127, 1) + body[-2]), (-2, 4, low(25)),
        (2, 4, high(24)), (6, 3, high(25) + body[2]),
    )
    for start, count, tile in tiles:
        for p in range(count):
            k, v = start + p, unpack4(tile, p)
            b2[k] = b2[k] + v if k in b2 else v
    t2 = run_T(b2, range(-4, 8), 4, mask=inside2)
    r2 = run_T(t2, range(-2, 6), 4)

    b3 = {}
    for pair in range(-6, 7):
        both = jnp.where((row & 1) == 0, body[pair + 1], body[pair])
        both = pair_y(jnp.where((lane & 3) == 3, both, 0.0), 1)
        tail = jnp.broadcast_to(last[pair - 1], (8, 128))
        for n in range(2):
            v = jnp.where((lane & 7) == 4 * n + 3, both, 0.0)
            v = v + jnp.where((lane & 7) == 4 * n + (row >> 1), tail, 0.0)
            b3[2 * pair + n] = pair_z(pair_z(pair_z(v, 1), 2), 4)
    t3 = run_T(b3, range(-11, 13), 8, 2, inside3)
    r3 = run_T(t3, range(-10, 12), 8, 2)

    minus = []
    for x in range(8):
        j = x % 4
        pair = []
        for p in range(2):
            own = packed_ref[26 + 2 * j + p]
            pair.append(jnp.where(lower == (x < 4), own, swapped_ref[26 + 2 * j + p]))
        minus.append(refine_y(pair))
    for k in range(16):
        mag = refine_x(minus, k)
        if k == 0:
            mag = mag + 0.25 * refine_y((low(22), low(23)))
        if k == 15:
            mag = mag + 0.25 * refine_y((high(22), high(23)))
        for q in range(4):
            mag_ref[k, pl.ds(q, 8, stride=4), :] = mag[q]
    copies = [pltpu.make_async_copy(mag_ref, mag_hbm, sems.at[4])]
    copies[0].start()

    b4 = {}
    for k in range(-5, 6):
        v = pair_y(pair_z(r3[2 * k] + r3[2 * k + 1], 8), 2)
        b4[k] = inside4(k, 0.5 * v)
    t4 = run_T(b4, range(-4, 5), 16, 4, inside4)
    r4 = run_T(t4, range(-3, 4), 16, 4, inside4)
    u4 = run_T(r4, range(-2, 3), 16, 4)
    e4 = {k: ALPHA * (b4[k] + t4[k] + r4[k] + u4[k]) for k in range(-2, 3)}
    e4 = {k: inside4(k, v) for k, v in e4.items()}

    v3 = {k: ALPHA * t3[k] + e4[k // 2] for k in range(-4, 6)}
    v3 = run_T(v3, range(-3, 5), 8, 2, inside3)
    w3 = run_T(v3, range(-2, 4), 8, 2)
    e3 = {k: inside3(k, w3[k] + ALPHA * (b3[k] + t3[k] + r3[k])) for k in range(-2, 4)}

    v2 = {k: ALPHA * t2[k] + e3[k // 2] for k in range(-4, 8)}
    v2 = run_T(v2, range(-3, 7), 4, 1, inside2)
    w2 = run_T(v2, range(-2, 6), 4, 1)
    e2 = {k: inside2(k, w2[k] + ALPHA * (b2[k] + t2[k] + r2[k])) for k in range(-2, 6)}

    inside1, inside0 = masked(8), masked(16)
    sides, base = {}, {}
    for i in range(-1, 5):
        v = e2[i]
        sides[i] = sides_z(v, 2) + v + jnp.stack([from_below(v), from_above(v)], axis=0)
        base[i] = v * (1.0 / 3.0) + sides[i] * ALPHA
    v1, w1 = {}, {}
    for k in range(-2, 10):
        i, j = k // 2, k // 2 + (1 if k % 2 else -1)
        v1[k] = inside1(k, base[i] + (e2[i] + e2[j]) * ALPHA)
    for i in range(-1, 5):
        around = sides_y(base[i], 1) + sides_z(base[i], 2)
        for k in (2 * i, 2 * i + 1):
            j = i + (1 if k % 2 else -1)
            if -1 <= k < 9:
                total = around + (sides[i] + sides[j]) * ALPHA + v1[k - 1] + v1[k + 1]
                w1[k] = v1[k] * (1.0 / 3.0) + total * ALPHA
    even = (lanes_of((8, 128)) & 1) == 0
    for side, first in ((low, -1), (high, 3)):
        for pair in range(3):
            both = [side(16 + 2 * pair + q) for q in range(2)]
            one = jnp.stack([jnp.where(even, v, pltpu.roll(v, 1, 1)) for v in both], axis=0)
            two = jnp.stack([jnp.where(even, pltpu.roll(v, 127, 1), v) for v in both], axis=0)
            for k, v in ((first + 2 * pair, one), (first + 2 * pair + 1, two)):
                w1[k] = w1[k] + v
    e1 = {k: inside1(k, w1[k] + own1_ref[k + 1]) for k in range(-1, 9)}

    wide, sides, base = {}, {}, {}
    for i in range(-1, 9):
        one, two = e1[i][0], e1[i][1]
        wide[i] = jnp.stack([one, one, two, two], axis=0)
        z_one, z_two, both = sides_z(one, 1), sides_z(two, 1), one + two
        sides[i] = jnp.stack(
            [
                z_one + one + from_below(two), z_one + both,
                z_two + both, z_two + two + from_above(one),
            ],
            axis=0,
        )
        base[i] = wide[i] * (1.0 / 3.0) + sides[i] * ALPHA
    p1 = Held(p1_ref, -1)
    for k in range(-1, 17):
        i, j = k // 2, k // 2 + (1 if k % 2 else -1)
        p1.put(k, inside0(k, base[i] + (wide[i] + wide[j]) * ALPHA))
    for k in range(16):
        i, j = k // 2, k // 2 + (1 if k % 2 else -1)
        if k % 2 == 0:
            around = sides_y(base[i], 1) + sides_z(base[i], 1)
        total = around + (sides[i] + sides[j]) * ALPHA + p1[k - 1] + p1[k + 1]
        v = p1[k] * (1.0 / 3.0) + total * ALPHA + own0_ref[k]
        if k < 4:
            v = v + low(pl.ds(4 * k, 4))
        if k >= 12:
            v = v + high(pl.ds(4 * (k - 12), 4))
        for q in range(4):
            pot_ref[k, pl.ds(q, 8, stride=4), :] = v[q]
        if k % 4 == 3:
            part = pl.ds(k - 3, 4)
            copies.append(pltpu.make_async_copy(pot_ref.at[part], pot_hbm.at[part], sems.at[k // 4]))
            copies[-1].start()
    for copy in copies:
        copy.wait()


def final_part(*operands):
    vmem = pl.BlockSpec(memory_space=pltpu.VMEM)
    hbm = pl.BlockSpec(memory_space=pltpu.HBM)
    shape = lambda *s: jax.ShapeDtypeStruct(s, F32)
    return pl.pallas_call(
        final_kernel,
        out_shape=(shape(16, 32, 128), shape(16, 32, 128)),
        in_specs=[vmem] * 5,
        out_specs=(hbm, hbm),
        scratch_shapes=[
            pltpu.VMEM((18, 4, 8, 128), F32),
            pltpu.VMEM((16, 32, 128), F32), pltpu.VMEM((16, 32, 128), F32),
            pltpu.SemaphoreType.DMA((5,)),
        ],
        compiler_params=pltpu.CompilerParams(vmem_limit_bytes=32 * 2**20),
        name="final",
    )(*operands)


def on_device(orbitals, spin_group, occupation, potential_guess):
    orbitals, spin_group, occupation = (
        pltpu.with_memory_space_constraint(v, pltpu.HBM) for v in (orbitals, spin_group, occupation)
    )
    parts = lax.all_to_all(density(spin_group, occupation, orbitals), "band", 0, 0)
    far, to_send, minus, mine2, *held = far_part(parts, potential_guess)
    rings = []
    for b in range(BANDS):
        half = RING // 2 * (b % 2)
        for first in range(half, DOMS - half, RING):
            rings.append([b * DOMS + first + (ROOT - half + i) % RING for i in range(RING)])
    for first in (0, 4, DOMS - 8, DOMS - 4):
        rings.append([b * DOMS + first + i for b in range(1, BANDS, 2) for i in range(4)])
    mine = lax.all_to_all(
        far.reshape(RING, 9 * 128), ("band", "dom"), 0, 0, axis_index_groups=rings
    ).reshape(9 * RING, 128)

    edges = [
        (b * DOMS + d + 1 - b % 2, b * DOMS + d + b % 2) for b in range(BANDS) for d in range(DOMS - 1)
    ]
    halo = lax.ppermute(to_send, ("band", "dom"), edges)
    own0, own1 = near_part(potential_guess, *held)
    swap = [(b, b ^ 1) for b in range(BANDS)]
    packed = pack(mine, halo, minus)
    swapped = lax.ppermute(packed, "band", swap)
    return final_part(packed, swapped, mine2, own0, own1)


def solution(mesh):
    placed = (P("band", "dom", None, None), P("band"), P("band"), P("dom", None, None))
    return jax.shard_map(
        on_device,
        mesh=mesh,
        in_specs=placed,
        out_specs=(P("dom", None, None), P("dom", None, None)),
        check_vma=False,
    )
```

```python
import functools

import jax
import jax.numpy as jnp
from jax import lax
from jax.experimental import pallas as pl
from jax.experimental.pallas import tpu as pltpu
from jax.sharding import PartitionSpec as P

DEN = 16
BANDS = 8
DOMS = 64
REACH = 7
RING = 16
ROWS = 96
ROOT = 11
ALPHA = 1.0 / 9.0
SOURCE_SCALE = 0.6
F32 = jnp.float32


def lanes_of(shape):
    return lax.broadcasted_iota(jnp.int32, shape, len(shape) - 1)


def rows_of(shape):
    return lax.broadcasted_iota(jnp.int32, shape, len(shape) - 2)


def sides_z(v, step):
    lane = lanes_of(v.shape)
    ax = v.ndim - 1
    left = jnp.where(lane >= step, pltpu.roll(v, step, ax), 0.0)
    right = jnp.where(lane < 128 - step, pltpu.roll(v, 128 - step, ax), 0.0)
    return left + right


def from_below(v, step=1):
    return jnp.where(rows_of(v.shape) >= step, pltpu.roll(v, step, v.ndim - 2), 0.0)


def from_above(v, step=1):
    return jnp.where(rows_of(v.shape) < 8 - step, pltpu.roll(v, 8 - step, v.ndim - 2), 0.0)


def sides_y(v, step):
    if v.ndim == 2:
        return from_below(v, step) + from_above(v, step)
    parts = [v[q] for q in range(v.shape[0])]
    n = len(parts)
    out = []
    for q in range(n):
        lower = parts[q - 1] if q > 0 else from_below(parts[n - 1])
        upper = parts[q + 1] if q < n - 1 else from_above(parts[0])
        out.append(lower + upper)
    return jnp.stack(out, axis=0)


def smooth(low, v, high, zstep, ystep=1):
    around = sides_y(v, ystep) + sides_z(v, zstep)
    if low is not None:
        around = around + low
    if high is not None:
        around = around + high
    return v * (1.0 / 3.0) + around * ALPHA


def pair_z(v, step):
    lane = lanes_of(v.shape)
    ax = v.ndim - 1
    other = jnp.where((lane & step) == 0, pltpu.roll(v, 128 - step, ax), pltpu.roll(v, step, ax))
    return v + other


def pair_y(v, step):
    row = rows_of(v.shape)
    ax = v.ndim - 2
    other = jnp.where((row & step) == 0, pltpu.roll(v, 8 - step, ax), pltpu.roll(v, step, ax))
    return v + other


def run_T(src, planes, zstep, ystep=1, mask=None):
    out = {}
    for k in planes:
        v = src.get(k)
        low, high = src.get(k - 1), src.get(k + 1)
        if v is None:
            edge = low if low is not None else high
            got = edge * ALPHA
        else:
            got = smooth(low, v, high, zstep, ystep)
        out[k] = got if mask is None else mask(k, got)
    return out


class Held:
    def __init__(self, ref, first):
        self.ref, self.first, self.have = ref, first, set()

    def put(self, k, value):
        self.ref[k - self.first] = value
        self.have.add(k)

    def get(self, k):
        return self.ref[k - self.first] if k in self.have else None

    def __getitem__(self, k):
        return self.ref[k - self.first]


def hold_T(src, held, planes, zstep, mask):
    for k in planes:
        v = src.get(k)
        low, high = src.get(k - 1), src.get(k + 1)
        if v is None:
            got = (low if low is not None else high) * ALPHA
        else:
            got = smooth(low, v, high, zstep)
        held.put(k, mask(k, got))


def refine_z(coarse):
    row = lax.broadcasted_iota(jnp.int32, (128, 256), 0)
    col = lax.broadcasted_iota(jnp.int32, (128, 256), 1)
    own = col >> 1
    other = jnp.where((col & 1) == 0, own - 1, own + 1)
    inside = (other >> 6) == (col >> 7)
    matrix = jnp.where(row == own, 0.75, jnp.where((row == other) & inside, 0.25, 0.0))
    return jnp.dot(
        coarse, matrix, precision=lax.Precision.HIGHEST, preferred_element_type=F32
    )


def refine_y(pair):
    first, second = pair
    return jnp.stack(
        [
            0.75 * first + 0.25 * from_below(second),
            0.75 * first + 0.25 * second,
            0.75 * second + 0.25 * first,
            0.75 * second + 0.25 * from_above(first),
        ],
        axis=0,
    )


def refine_x(coarse, k):
    i = k // 2
    other = i - 1 if k % 2 == 0 else i + 1
    total = None
    for j, factor in ((i, 0.75), (other, 0.25)):
        if 0 <= j < 8:
            term = factor * coarse[j]
            total = term if total is None else total + term
    return total


def masks(dom):
    low_flag = jnp.where(dom > 0, 1.0, 0.0).astype(F32)
    high_flag = jnp.where(dom < DOMS - 1, 1.0, 0.0).astype(F32)

    def masked(last):
        def mask(k, v):
            if k < 0:
                return v * low_flag
            if k > last:
                return v * high_flag
            return v
        return mask

    return masked(15), masked(7), masked(3)


def guess_planes(guess_ref):
    def guess(k):
        if not 0 <= k < 16:
            return None
        return jnp.stack([guess_ref[k, pl.ds(q, 8, stride=4), :] for q in range(4)], axis=0)
    return guess


def restricted(r, k):
    total = None
    for fine in (2 * k, 2 * k + 1):
        v = r.get(fine)
        if v is not None:
            total = v if total is None else total + v
    total = jnp.stack([total[0] + total[1], total[2] + total[3]], axis=0)
    return 0.5 * pair_z(total, 1)


def geometric(b, t, r, k, zstep):
    low, v, high = r.get(k - 1), r.get(k), r.get(k + 1)
    if v is None:
        last = (low if low is not None else high) * ALPHA
    else:
        last = smooth(low, v, high, zstep)
    for term in (r.get(k), t.get(k), b.get(k)):
        if term is not None:
            last = last + term
    return last * ALPHA


def copy_all(source, target, count, sems):
    copies = [pltpu.make_async_copy(source, target.at[i], sems.at[i]) for i in range(count)]
    for copy in copies:
        copy.start()
    return copies


def density_kernel(
    spin_hbm, occ_hbm, orb_hbm, part_ref, spin_ref, occ_ref, orb_ref, plane_ref, sems,
):
    loads = [
        pltpu.make_async_copy(spin_hbm, spin_ref, sems.at[8]),
        pltpu.make_async_copy(occ_hbm, occ_ref, sems.at[9]),
    ]
    loads += [pltpu.make_async_copy(orb_hbm.at[k], orb_ref.at[k], sems.at[k]) for k in range(8)]
    for load in loads:
        load.start()
    loads[0].wait()
    loads[1].wait()
    ups, downs = [0.0] * 8, [0.0] * 8
    for k in range(8):
        weight = occ_ref[k].astype(F32) * (0.125 / DEN)
        up = spin_ref[k] == 0
        up, down = jnp.where(up, weight, 0.0), jnp.where(up, 0.0, weight)
        loads[2 + k].wait()
        for x in range(8):
            square = orb_ref[k, x] * orb_ref[k, x]
            ups[x] = ups[x] + up * square
            downs[x] = downs[x] + down * square
    for x in range(8):
        plane_ref[x] = ups[x] + downs[x]
        plane_ref[8 + x] = ups[x] - downs[x]

    def halves(plane):
        return jnp.concatenate(
            [plane_ref[plane, pl.ds(p, 8, stride=2), :] for p in range(2)], axis=-1
        )

    for x in range(8):
        total, difference = halves(x), halves(8 + x)
        for b in range(BANDS):
            part_ref[b, pl.ds(8 * x, 8), :] = total
            if b % 2 == x // 4:
                part_ref[b, pl.ds(64 + 8 * (x % 4), 8), :] = difference


def density(spin_group, occupation, orbitals):
    hbm = pl.BlockSpec(memory_space=pltpu.HBM)
    return pl.pallas_call(
        density_kernel,
        out_shape=jax.ShapeDtypeStruct((BANDS, ROWS, 128), F32),
        in_specs=[hbm] * 3,
        out_specs=pl.BlockSpec(memory_space=pltpu.VMEM),
        scratch_shapes=[
            pltpu.SMEM((8,), jnp.int32), pltpu.SMEM((8,), jnp.int32),
            pltpu.VMEM((8, 8, 16, 64), F32), pltpu.VMEM((16, 16, 64), F32),
            pltpu.SemaphoreType.DMA((10,)),
        ],
        compiler_params=pltpu.CompilerParams(vmem_limit_bytes=40 * 2**20),
        name="density",
    )(spin_group, occupation, orbitals)


def plane_pair(wide, plane):
    rows = wide[8 * plane:8 * plane + 8]
    return rows[:, :128], rows[:, 128:]


def far_kernel(
    part_ref, guess_ref, far_hbm, halo_ref, minus_ref, b2_ref,
    d_ref, t_ref, r_ref, b1_ref, t1_ref, r1_ref, sum_ref, far_ref, sem,
):
    inside0, inside1, inside2 = masks(lax.axis_index("dom"))
    for i in range(ROWS // 16):
        rows = pl.ds(16 * i, 16)
        total = part_ref[0, rows, :]
        for band in range(1, BANDS):
            total = total + part_ref[band, rows, :]
        sum_ref[rows, :] = total
    wide = refine_z(sum_ref[...])
    plus = [SOURCE_SCALE * refine_y(plane_pair(wide, x)) for x in range(8)]
    for j in range(4):
        minus_ref[2 * j], minus_ref[2 * j + 1] = plane_pair(wide, 8 + j)
    d, t, r = Held(d_ref, -1), Held(t_ref, -2), Held(r_ref, -3)
    guess = guess_planes(guess_ref)
    for k in range(-1, 17):
        v, low, high = guess(k), guess(k - 1), guess(k + 1)
        around = None
        if v is not None:
            around = sides_y(v, 1) + sides_z(v, 1)
        for side in (low, high):
            if side is not None:
                around = side if around is None else around + side
        if v is not None:
            around = around - 6.0 * v
        d.put(k, inside0(k, refine_x(plus, k) + around))
    hold_T(d, t, range(-2, 18), 1, inside0)
    hold_T(t, r, range(-3, 19), 1, inside0)
    b1, t1, r1 = Held(b1_ref, -2), Held(t1_ref, -3), Held(r1_ref, -4)
    for k in range(-2, 10):
        b1.put(k, restricted(r, k))
    hold_T(b1, t1, range(-3, 11), 2, inside1)
    hold_T(t1, r1, range(-4, 12), 2, inside1)
    b2 = {}
    for k in range(-2, 6):
        v = r1[2 * k] + r1[2 * k + 1]
        b2[k] = 0.5 * pair_z(v[0] + v[1], 2)
        b2_ref[k + 2] = b2[k]
    t2 = run_T(b2, range(-3, 7), 4, mask=inside2)
    r2 = run_T(t2, range(-4, 8), 4, mask=inside2)
    b3 = [0.5 * pair_y(pair_z(r2[2 * k] + r2[2 * k + 1], 4), 1) for k in range(-2, 4)]

    lane, row = lanes_of((8, 128)), rows_of((8, 128))
    parity = row & 1
    common = b3[0]
    for n in range(1, 4):
        here = ((lane & 7) == 3 + 4 * (n % 2)) & (parity == n // 2)
        common = jnp.where(here, b3[n], common)
    above, below = common, common
    for p in range(3):
        above = jnp.where((lane & 3) == p, b2[3 + p], above)
        below = jnp.where((lane & 3) == p, b2[p - 2], below)
    line = lanes_of((1, 128)) & 7
    last = b3[4][0:1]
    for n in (4, 5):
        for y in range(4):
            last = jnp.where(line == 4 * (n - 4) + y, b3[n][2 * y:2 * y + 1], last)
    core = lax.axis_index("band") % 2
    half = RING // 2 * core
    me = (lax.axis_index("dom") + half) % RING
    for i in range(RING):
        target = (ROOT - half + i) % RING
        far_ref[pl.ds(9 * i, 8), :] = jnp.where(target > me, above, below)
        far_ref[pl.ds(9 * i + 8, 1), :] = last
    copy = pltpu.make_async_copy(far_ref, far_hbm, sem)
    copy.start()

    for group in range(2):
        packed = b2[4 * group - 2]
        for p in range(1, 4):
            packed = jnp.where((lane & 3) == p, b2[4 * group - 2 + p], packed)
        halo_ref[24 + group] = packed

    even = (lane & 1) == 0

    def edges(first0, first1, plane):
        for k in range(4):
            halo_ref[pl.ds(4 * k, 4)] = geometric(d, t, r, first0 + k, 1)
        for pair in range(3):
            one = geometric(b1, t1, r1, first1 + 2 * pair, 2)
            two = geometric(b1, t1, r1, first1 + 2 * pair + 1, 2)
            for q in range(2):
                halo_ref[16 + 2 * pair + q] = jnp.where(even, one[q], two[q])
        halo_ref[22], halo_ref[23] = minus_ref[2 * plane], minus_ref[2 * plane + 1]

    @pl.when(core == 0)
    def _():
        edges(-4, -5, 0)

    @pl.when(core == 1)
    def _():
        edges(16, 7, 3)

    copy.wait()


def far_part(parts, guess):
    vmem = pl.BlockSpec(memory_space=pltpu.VMEM)
    shape = lambda *s: jax.ShapeDtypeStruct(s, F32)
    return pl.pallas_call(
        far_kernel,
        out_shape=(
            shape(9 * RING, 128), shape(26, 8, 128), shape(8, 8, 128), shape(8, 8, 128),
            shape(18, 4, 8, 128), shape(20, 4, 8, 128), shape(22, 4, 8, 128),
            shape(12, 2, 8, 128), shape(14, 2, 8, 128), shape(16, 2, 8, 128),
        ),
        in_specs=[vmem, vmem],
        out_specs=(pl.BlockSpec(memory_space=pltpu.HBM),) + (vmem,) * 9,
        scratch_shapes=[
            pltpu.VMEM((ROWS, 128), F32), pltpu.VMEM((9 * RING, 128), F32), pltpu.SemaphoreType.DMA,
        ],
        compiler_params=pltpu.CompilerParams(vmem_limit_bytes=32 * 2**20),
        name="far",
    )(parts, guess)


class Given(Held):
    def __init__(self, ref, first):
        super().__init__(ref, first)
        self.have = set(range(first, first + ref.shape[0]))


def near_kernel(
    guess_ref, d_ref, t_ref, r_ref, b1_ref, t1_ref, r1_ref, own0_ref, own1_ref,
):
    d, t, r = Given(d_ref, -1), Given(t_ref, -2), Given(r_ref, -3)
    b1, t1, r1 = Given(b1_ref, -2), Given(t1_ref, -3), Given(r1_ref, -4)
    guess = guess_planes(guess_ref)
    for k in range(-1, 9):
        own1_ref[k + 1] = geometric(b1, t1, r1, k, 2)
    for k in range(16):
        own0_ref[k] = geometric(d, t, r, k, 1) + guess(k)


def near_part(guess, *held):
    vmem = pl.BlockSpec(memory_space=pltpu.VMEM)
    shape = lambda *s: jax.ShapeDtypeStruct(s, F32)
    return pl.pallas_call(
        near_kernel,
        out_shape=(shape(16, 4, 8, 128), shape(10, 2, 8, 128)),
        in_specs=[vmem] * 7,
        out_specs=(vmem,) * 2,
        compiler_params=pltpu.CompilerParams(vmem_limit_bytes=32 * 2**20),
        cost_estimate=pl.CostEstimate(flops=10**6, bytes_accessed=2**20, transcendentals=0),
        name="near",
    )(guess, *held)


def pack_kernel(mine_ref, halo_ref, minus_ref, out_ref):
    out_ref[pl.ds(0, 26)] = halo_ref[...]
    out_ref[pl.ds(26, 8)] = minus_ref[...]
    for i in range(RING):
        out_ref[34 + i] = mine_ref[pl.ds(9 * i, 8), :]
        out_ref[50 + i // 8, pl.ds(i % 8, 1), :] = mine_ref[pl.ds(9 * i + 8, 1), :]


def pack(mine, halo, minus):
    vmem = pl.BlockSpec(memory_space=pltpu.VMEM)
    return pl.pallas_call(
        pack_kernel,
        out_shape=jax.ShapeDtypeStruct((52, 8, 128), F32),
        in_specs=[vmem] * 3,
        out_specs=vmem,
        compiler_params=pltpu.CompilerParams(vmem_limit_bytes=32 * 2**20),
        name="pack",
    )(mine, halo, minus)


def final_kernel(
    packed_ref, swapped_ref, mine2_ref, own0_ref, own1_ref, pot_hbm, mag_hbm,
    p1_ref, pot_ref, mag_ref, sems,
):
    dom = lax.axis_index("dom")
    lower = lax.axis_index("band") % 2 == 0

    def high(i):
        return jnp.where(lower, packed_ref[i], swapped_ref[i])

    def low(i):
        return jnp.where(lower, swapped_ref[i], packed_ref[i])

    minus = []
    for x in range(8):
        j = x % 4
        pair = []
        for p in range(2):
            own = packed_ref[26 + 2 * j + p]
            pair.append(jnp.where(lower == (x < 4), own, swapped_ref[26 + 2 * j + p]))
        minus.append(refine_y(pair))
    for k in range(16):
        mag = refine_x(minus, k)
        if k == 0:
            mag = mag + 0.25 * refine_y((low(22), low(23)))
        if k == 15:
            mag = mag + 0.25 * refine_y((high(22), high(23)))
        for q in range(4):
            mag_ref[k, pl.ds(q, 8, stride=4), :] = mag[q]
    copies = [pltpu.make_async_copy(mag_ref, mag_hbm, sems.at[4])]
    copies[0].start()

    def masked(count):
        first, last = -dom * count, (DOMS - dom) * count
        def mask(k, v):
            if 0 <= k < count:
                return v
            ok = (k >= first) & (k < last)
            return jnp.where(ok, v, 0.0)
        return mask

    lane, row = lanes_of((8, 128)), rows_of((8, 128))
    spot = dom % RING
    first = dom - spot
    other_first = first + jnp.where(spot < RING // 2, -(RING // 2), RING // 2)
    body, last = {}, {}
    for step in range(-REACH, REACH + 1):
        wanted = dom + step
        at = wanted - first
        aligned = (at >= 0) & (at < RING)
        at = jnp.clip(jnp.where(aligned, at, wanted - other_first), 0, RING - 1)
        slot = (at + RING - jnp.where(aligned, ROOT, ROOT - RING // 2)) % RING
        there = (wanted >= 0) & (wanted < DOMS)
        places = ((body, 34 + slot, pl.ds(0, 8)), (last, 50 + slot // 8, pl.ds(slot % 8, 1)))
        for ref, tile, rows in places:
            v = jnp.where(aligned == lower, packed_ref[tile, rows, :], swapped_ref[tile, rows, :])
            ref[step] = jnp.where(there, v, 0.0)

    def unpack4(v, p):
        v = jnp.where((lane & 3) == p, v, 0.0)
        v = v + pltpu.roll(v, 1 if p % 2 == 0 else 127, 1)
        return v + pltpu.roll(v, 2 if p < 2 else 126, 1)

    inside2, inside3, inside4 = masked(4), masked(2), masked(1)
    b2 = {k: mine2_ref[k + 2] for k in range(-2, 6)}
    tiles = (
        (-5, 3, pltpu.roll(low(24), 127, 1) + body[-2]), (-2, 4, low(25)),
        (2, 4, high(24)), (6, 3, high(25) + body[2]),
    )
    for start, count, tile in tiles:
        for p in range(count):
            k, v = start + p, unpack4(tile, p)
            b2[k] = b2[k] + v if k in b2 else v
    t2 = run_T(b2, range(-4, 8), 4, mask=inside2)
    r2 = run_T(t2, range(-2, 6), 4)

    b3 = {}
    for pair in range(-6, 7):
        both = jnp.where((row & 1) == 0, body[pair + 1], body[pair])
        both = pair_y(jnp.where((lane & 3) == 3, both, 0.0), 1)
        tail = jnp.broadcast_to(last[pair - 1], (8, 128))
        spot8 = (lane & 7) - 4 * (row & 1)
        v = jnp.where(spot8 == 3, both, 0.0) + jnp.where(spot8 == (row >> 1), tail, 0.0)
        v = pair_z(pair_z(pair_z(v, 1), 2), 4)
        even = (row & 1) == 0
        w = jnp.where(even, pltpu.roll(v, 7, 0), pltpu.roll(v, 1, 0))
        b3[2 * pair], b3[2 * pair + 1] = jnp.where(even, v, w), jnp.where(even, w, v)
    t3 = run_T(b3, range(-11, 13), 8, 2, inside3)
    r3 = run_T(t3, range(-10, 12), 8, 2)

    b4 = {}
    for k in range(-5, 6):
        v = pair_y(pair_z(r3[2 * k] + r3[2 * k + 1], 8), 2)
        b4[k] = inside4(k, 0.5 * v)
    t4 = run_T(b4, range(-4, 5), 16, 4, inside4)
    r4 = run_T(t4, range(-3, 4), 16, 4, inside4)
    u4 = run_T(r4, range(-2, 3), 16, 4)
    e4 = {k: ALPHA * (b4[k] + t4[k] + r4[k] + u4[k]) for k in range(-2, 3)}
    e4 = {k: inside4(k, v) for k, v in e4.items()}

    v3 = {k: ALPHA * t3[k] + e4[k // 2] for k in range(-4, 6)}
    v3 = run_T(v3, range(-3, 5), 8, 2, inside3)
    w3 = run_T(v3, range(-2, 4), 8, 2)
    e3 = {k: inside3(k, w3[k] + ALPHA * (b3[k] + t3[k] + r3[k])) for k in range(-2, 4)}

    v2 = {k: ALPHA * t2[k] + e3[k // 2] for k in range(-4, 8)}
    v2 = run_T(v2, range(-3, 7), 4, 1, inside2)
    w2 = run_T(v2, range(-2, 6), 4, 1)
    e2 = {k: inside2(k, w2[k] + ALPHA * (b2[k] + t2[k] + r2[k])) for k in range(-2, 6)}

    inside1, inside0 = masked(8), masked(16)
    sides, base = {}, {}
    for i in range(-1, 5):
        v = e2[i]
        sides[i] = sides_z(v, 2) + v + jnp.stack([from_below(v), from_above(v)], axis=0)
        base[i] = v * (1.0 / 3.0) + sides[i] * ALPHA
    v1, w1 = {}, {}
    for k in range(-2, 10):
        i, j = k // 2, k // 2 + (1 if k % 2 else -1)
        v1[k] = inside1(k, base[i] + (e2[i] + e2[j]) * ALPHA)
    for i in range(-1, 5):
        around = sides_y(base[i], 1) + sides_z(base[i], 2)
        for k in (2 * i, 2 * i + 1):
            j = i + (1 if k % 2 else -1)
            if -1 <= k < 9:
                total = around + (sides[i] + sides[j]) * ALPHA + v1[k - 1] + v1[k + 1]
                w1[k] = v1[k] * (1.0 / 3.0) + total * ALPHA
    even = (lanes_of((8, 128)) & 1) == 0
    for side, first in ((low, -1), (high, 3)):
        for pair in range(3):
            both = [side(16 + 2 * pair + q) for q in range(2)]
            one = jnp.stack([jnp.where(even, v, pltpu.roll(v, 1, 1)) for v in both], axis=0)
            two = jnp.stack([jnp.where(even, pltpu.roll(v, 127, 1), v) for v in both], axis=0)
            for k, v in ((first + 2 * pair, one), (first + 2 * pair + 1, two)):
                w1[k] = w1[k] + v
    e1 = {k: inside1(k, w1[k] + own1_ref[k + 1]) for k in range(-1, 9)}

    wide, sides, base = {}, {}, {}
    for i in range(-1, 9):
        one, two = e1[i][0], e1[i][1]
        wide[i] = jnp.stack([one, one, two, two], axis=0)
        z_one, z_two, both = sides_z(one, 1), sides_z(two, 1), one + two
        sides[i] = jnp.stack(
            [
                z_one + one + from_below(two), z_one + both,
                z_two + both, z_two + two + from_above(one),
            ],
            axis=0,
        )
        base[i] = wide[i] * (1.0 / 3.0) + sides[i] * ALPHA
    p1 = Held(p1_ref, -1)
    for k in range(-1, 17):
        i, j = k // 2, k // 2 + (1 if k % 2 else -1)
        p1.put(k, inside0(k, base[i] + (wide[i] + wide[j]) * ALPHA))
    for k in range(16):
        i, j = k // 2, k // 2 + (1 if k % 2 else -1)
        if k % 2 == 0:
            around = sides_y(base[i], 1) + sides_z(base[i], 1)
        total = around + (sides[i] + sides[j]) * ALPHA + p1[k - 1] + p1[k + 1]
        v = p1[k] * (1.0 / 3.0) + total * ALPHA + own0_ref[k]
        if k < 4:
            v = v + low(pl.ds(4 * k, 4))
        if k >= 12:
            v = v + high(pl.ds(4 * (k - 12), 4))
        for q in range(4):
            pot_ref[k, pl.ds(q, 8, stride=4), :] = v[q]
        if k % 4 == 3:
            part = pl.ds(k - 3, 4)
            copies.append(pltpu.make_async_copy(pot_ref.at[part], pot_hbm.at[part], sems.at[k // 4]))
            copies[-1].start()
    for copy in copies:
        copy.wait()


def final_part(*operands):
    vmem = pl.BlockSpec(memory_space=pltpu.VMEM)
    hbm = pl.BlockSpec(memory_space=pltpu.HBM)
    shape = lambda *s: jax.ShapeDtypeStruct(s, F32)
    return pl.pallas_call(
        final_kernel,
        out_shape=(shape(16, 32, 128), shape(16, 32, 128)),
        in_specs=[vmem] * 5,
        out_specs=(hbm, hbm),
        scratch_shapes=[
            pltpu.VMEM((18, 4, 8, 128), F32),
            pltpu.VMEM((16, 32, 128), F32), pltpu.VMEM((16, 32, 128), F32),
            pltpu.SemaphoreType.DMA((5,)),
        ],
        compiler_params=pltpu.CompilerParams(vmem_limit_bytes=32 * 2**20),
        name="final",
    )(*operands)


def on_device(orbitals, spin_group, occupation, potential_guess):
    orbitals, spin_group, occupation = (
        pltpu.with_memory_space_constraint(v, pltpu.HBM) for v in (orbitals, spin_group, occupation)
    )
    parts = lax.all_to_all(density(spin_group, occupation, orbitals), "band", 0, 0)
    far, to_send, minus, mine2, *held = far_part(parts, potential_guess)
    rings = []
    for b in range(BANDS):
        half = RING // 2 * (b % 2)
        for first in range(half, DOMS - half, RING):
            rings.append([b * DOMS + first + (ROOT - half + i) % RING for i in range(RING)])
    for first in (0, 4, DOMS - 8, DOMS - 4):
        rings.append([b * DOMS + first + i for b in range(1, BANDS, 2) for i in range(4)])
    mine = lax.all_to_all(
        far.reshape(RING, 9 * 128), ("band", "dom"), 0, 0, axis_index_groups=rings
    ).reshape(9 * RING, 128)

    edges = [
        (b * DOMS + d + 1 - b % 2, b * DOMS + d + b % 2) for b in range(BANDS) for d in range(DOMS - 1)
    ]
    halo = lax.ppermute(to_send, ("band", "dom"), edges)
    own0, own1 = near_part(potential_guess, *held)
    swap = [(b, b ^ 1) for b in range(BANDS)]
    packed = pack(mine, halo, minus)
    swapped = lax.ppermute(packed, "band", swap)
    return final_part(packed, swapped, mine2, own0, own1)


def solution(mesh):
    placed = (P("band", "dom", None, None), P("band"), P("band"), P("dom", None, None))
    return jax.shard_map(
        on_device,
        mesh=mesh,
        in_specs=placed,
        out_specs=(P("dom", None, None), P("dom", None, None)),
        check_vma=False,
    )
```
